32 devices in a mesh: section: 2 (over core), fsdp: 4 (over z), ctx: 4 (over y, x).
Axes of the slice: x: 2, y: 2, z: 4, core: 2. Of those that a mesh axis runs over, the one named last changes fastest.
Arguments:
- boundary: bfloat16 [2, 2, 4, 1024, 640], P('section', None, 'fsdp', 'ctx'), may hold values from -6 to 6
- positions: int32 [2, 4, 1024], P(None, 'fsdp'), may hold values from 0 to 1023, each once within a row
- w_query: bfloat16 [2, 640, 1024], P('section', ('fsdp', 'ctx')), may hold values from -0.25 to 0.25
- w_key_value: bfloat16 [2, 640, 512], P('section', ('fsdp', 'ctx')), may hold values from -0.25 to 0.25
- w_out: bfloat16 [2, 1024, 640], P('section', ('fsdp', 'ctx')), may hold values from -0.1875 to 0.1875
- w_gate_up: bfloat16 [2, 640, 4096], P('section', ('fsdp', 'ctx')), may hold values from -0.25 to 0.25
- w_down: bfloat16 [2, 2048, 640], P('section', ('fsdp', 'ctx')), may hold values from -0.125 to 0.125
- norm_gains: bfloat16 [2, 4, 640], P('section', None, ('fsdp', 'ctx')), may hold values from 0.25 to 1.75
- head_gains: bfloat16 [2, 2, 256], P('section', None, ('fsdp', 'ctx')), may hold values from 0.25 to 1.75
Outputs:
- boundary_out: float32 [2, 2, 4, 1024, 640], P('section', None, 'fsdp', 'ctx')
- grad_query: float32 [2, 640, 1024], P('section', ('fsdp', 'ctx'))
- grad_key_value: float32 [2, 640, 512], P('section', ('fsdp', 'ctx'))
- grad_out: float32 [2, 1024, 640], P('section', ('fsdp', 'ctx'))
- grad_gate_up: float32 [2, 640, 4096], P('section', ('fsdp', 'ctx'))
- grad_down: float32 [2, 2048, 640], P('section', ('fsdp', 'ctx'))
- grad_norm_gains: float32 [2, 4, 640], P('section', None, ('fsdp', 'ctx'))
- grad_head_gains: float32 [2, 2, 256], P('section', None, ('fsdp', 'ctx'))
The draws below stay inside these ranges and needn't reach their ends.
Inputs may be any that keep to these rules, and one draw needn't show every extreme that they name: `positions`: each row of 1024 holds every place 0 to 1023 once.
All inputs are finite; a program needn't handle non-finite values.
Results may differ from the reference program's by a relative error of at most 0.025.
Values may be sent and summed in bfloat16 or wider, within the bound.
No kernel may reach another device: no remote copies, remote signals or barrier semaphores. Data moves between devices by JAX's collectives and lax.ppermute only.
A program may use at most 320 MiB of HBM per device.

```python
import math
import jax
import jax.numpy as jnp
from jax import lax

D = 640
FF = 2048
HEADS = 4
HD = 256
WIN = 512
MB = 2
LEN = 1024
SEQS = 4


def levels(rng, dims, pieces, low, largest):
    def one(axis_at, shards_of):
        heights = jax.random.uniform(jax.random.fold_in(jax.random.fold_in(rng, 6), axis_at), (shards_of,), jnp.float32, low / len(pieces), largest / len(pieces))
        return jnp.repeat(jnp.exp(heights), dims[axis_at] // shards_of).reshape((-1,) + (1,) * (len(dims) - axis_at - 1))

    loudness = one(*pieces[0])
    for cut in pieces[1:]:
        loudness = loudness * one(*cut)
    return loudness


def centred(own_key, shape, width, bound, shards=(), kind=jnp.bfloat16):
    loudness = levels(own_key, shape, shards, -0.22, 0.18) if shards else 1.0
    entries = jax.random.normal(own_key, shape, jnp.float32) * width * loudness
    return jnp.minimum(jnp.maximum(entries, -bound), bound).astype(kind)


def setup_inputs(seed: int = 0) -> dict:
    streams_of = jax.random.split(jax.random.key(seed), 10)
    boundary = centred(streams_of[0], (2, MB, SEQS, LEN, D), 1.0, 6.0, ((0, 2), (2, 4), (3, 4)))
    positions = jax.vmap(lambda own: jax.random.permutation(own, LEN))(jax.random.split(streams_of[1], MB * SEQS)).reshape((MB, SEQS, LEN)).astype(jnp.int32)
    w_query = centred(streams_of[2], (2, D, HEADS * HD), D ** -0.5, 0.25, ((0, 2), (1, 16)))
    w_key_value = centred(streams_of[3], (2, D, 2 * HD), D ** -0.5, 0.25, ((0, 2), (1, 16)))
    w_out = centred(streams_of[4], (2, HEADS * HD, D), (HEADS * HD) ** -0.5, 0.1875, ((0, 2), (1, 16)))
    w_gate_up = centred(streams_of[5], (2, D, 2 * FF), D ** -0.5, 0.25, ((0, 2), (1, 16)))
    w_down = centred(streams_of[6], (2, FF, D), FF ** -0.5, 0.125, ((0, 2), (1, 16)))
    norm_gains = jnp.clip(1.0 + 0.15 * jax.random.normal(streams_of[7], (2, 4, D), jnp.float32), 0.25, 1.75).astype(jnp.bfloat16)
    head_gains = jnp.clip(1.0 + 0.15 * jax.random.normal(streams_of[8], (2, 2, HD), jnp.float32), 0.25, 1.75).astype(jnp.bfloat16)
    return {"boundary": boundary, "positions": positions, "w_query": w_query, "w_key_value": w_key_value, "w_out": w_out, "w_gate_up": w_gate_up, "w_down": w_down, "norm_gains": norm_gains, "head_gains": head_gains}


@jax.custom_vjp
def low(v):
    return lax.optimization_barrier(v.astype(jnp.bfloat16)).astype(jnp.float32)

@jax.custom_vjp
def low_back(v):
    return v

def low_keep(v):
    return (low(v), None)

def low_pass(kept, grad):
    return (grad,)

def back_keep(v):
    return (v, None)

def back_low(kept, grad):
    return (low(grad),)
low.defvjp(low_keep, low_pass)
low_back.defvjp(back_keep, back_low)
EPS = 1e-06
HIGH = lax.Precision.HIGHEST
LOG_LOCAL = math.log(10000.0)
LOG_GLOBAL = math.log(1000000.0)

def rms_norm(values_in, gain):
    return values_in * lax.rsqrt(lax.optimization_barrier(jnp.mean(values_in * values_in, axis=-1, keepdims=True)) + EPS) * gain

def rotate(values_in, cosine, sine_table):
    half_width = values_in.shape[-1] // 2
    lower_half = values_in[..., :half_width]
    upper_half = values_in[..., half_width:]
    return jnp.concatenate([lower_half * cosine - upper_half * sine_table, upper_half * cosine + lower_half * sine_table], axis=-1)

def rope_tables(places, log_base):
    half_width = HD // 2
    inverse = jnp.exp(-log_base * (jnp.arange(half_width, dtype=jnp.float32) * (2.0 / HD)))
    angles = places.astype(jnp.float32)[:, None] * inverse[None, :]
    return (jnp.cos(angles), jnp.sin(angles))

def head_prepare(query_product, key_product, query_gain, key_gain, cosine, sine_table):
    token_count = query_product.shape[0]
    queries = rms_norm(query_product.reshape(token_count, HEADS, HD), query_gain)
    keys_normed = rms_norm(key_product, key_gain)
    return (rotate(queries, cosine[:, None, :], sine_table[:, None, :]), rotate(keys_normed, cosine, sine_table))

def gated(gate_up):
    return jax.nn.gelu(gate_up[:, :FF], approximate=True) * gate_up[:, FF:]

def attend(queries, keys_rot, values, places, window):
    block_rows = min(512, LEN)
    query_blocks = queries.reshape(LEN // block_rows, block_rows, HEADS, HD)
    place_blocks = places.reshape(LEN // block_rows, block_rows)
    score_scale = 1.0 / math.sqrt(HD)

    def one_block(scan_item):
        query_block, query_places = scan_item
        scores = jnp.einsum('qhd,kd->qhk', query_block, keys_rot, precision=HIGH) * score_scale
        scores = low_back(scores)
        allowed = (places[None, :] <= query_places[:, None]) & (query_places[:, None] - places[None, :] < window)
        scores = jnp.where(allowed[:, None, :], scores, -1e+30)
        maximum = lax.optimization_barrier(jnp.max(scores, axis=-1, keepdims=True))
        weights = jnp.exp(scores - maximum)
        probabilities = low(weights / lax.optimization_barrier(jnp.sum(weights, axis=-1, keepdims=True)))
        return jnp.einsum('qhk,kd->qhd', probabilities, values, precision=HIGH)
    mixed = lax.map(jax.checkpoint(one_block), (query_blocks, place_blocks))
    return mixed.reshape(LEN, HEADS * HD)

def layer(params, section_slot, hidden_in, places, window, log_base):
    w_query, w_key_value, w_out, w_gate_up, w_down, norm_gains, head_gains = [weight[section_slot] for weight in params]
    normed = low(rms_norm(hidden_in, norm_gains[0]))
    query_product = low_back(jnp.dot(normed, w_query, precision=HIGH))
    pair_product = low_back(jnp.dot(normed, w_key_value, precision=HIGH))
    cosine, sine_table = rope_tables(places, log_base)
    queries, keys_rot = head_prepare(query_product, pair_product[:, :HD], head_gains[0], head_gains[1], cosine, sine_table)
    mixed = attend(low(queries), low(keys_rot), low(pair_product[:, HD:]), places, window)
    mixed = low(low_back(mixed))
    branch = low_back(jnp.dot(mixed, w_out, precision=HIGH))
    middle = hidden_in + rms_norm(branch, norm_gains[1])
    normed_two = low(rms_norm(middle, norm_gains[2]))
    gate_up = low_back(jnp.dot(normed_two, w_gate_up, precision=HIGH))
    hidden = low(gated(gate_up))
    down_out = low_back(jnp.dot(hidden, w_down, precision=HIGH))
    return middle + rms_norm(down_out, norm_gains[3])

def reference(boundary, positions, w_query, w_key_value, w_out, w_gate_up, w_down, norm_gains, head_gains):
    params = tuple((weight.astype(jnp.float32) for weight in (w_query, w_key_value, w_out, w_gate_up, w_down, norm_gains, head_gains)))
    inputs = boundary[0].astype(jnp.float32).reshape(MB * SEQS, LEN, D)
    cotangent = boundary[1].astype(jnp.float32).reshape(MB * SEQS, LEN, D)
    places_all = positions.reshape(MB * SEQS, LEN)

    def forward(inputs_in, params_in):

        def one_sequence(carried, scan_item):
            sequence, places = scan_item
            first_out = layer(params_in, 0, sequence, places, WIN, LOG_LOCAL)
            passed = low(low_back(first_out))
            return (carried, layer(params_in, 1, passed, places, LEN, LOG_GLOBAL))
        _, outputs = lax.scan(one_sequence, jnp.zeros((), jnp.float32), (inputs_in, places_all))
        return outputs
    outputs, pullback = jax.vjp(forward, inputs, params)
    grad_inputs, grad_params = pullback(cotangent)
    boundary_out = jnp.stack([grad_inputs.reshape(MB, SEQS, LEN, D), outputs.reshape(MB, SEQS, LEN, D)])
    return (boundary_out, grad_params[0], grad_params[1], grad_params[2], grad_params[3], grad_params[4], grad_params[5], grad_params[6])
```

```python
import math

import jax
import jax.numpy as jnp
from jax import lax
from jax.sharding import PartitionSpec as P

D = 640
FF = 2048
HEADS = 4
HD = 256
WIN = 512
MB = 2
QH = 2 * HD
QW = QH + HD
QP = QW + 128

EPS = 1e-06
BASES = (math.log(10000.0), math.log(1000000.0))
SCALE = 1.0 / math.sqrt(HD)
BF = jnp.bfloat16
F32 = jnp.float32


def bits_of(axis):
    return (lax.axis_size(axis) - 1).bit_length()


def exchange(shard, axis, flip):
    pairs = [(i, i ^ flip) for i in range(lax.axis_size(axis))]
    return lax.ppermute(shard, axis, pairs)


def my_bit(axis, bit):
    return (lax.axis_index(axis) >> bit) & 1


def grid_steps(order):
    steps = []
    fb, cb = bits_of("fsdp"), bits_of("ctx")
    fsteps = [("fsdp", b, fb - 1 - b) for b in range(fb)]
    csteps = [("ctx", b, fb + cb - 1 - b) for b in range(cb)]
    if order == "yx":
        csteps = csteps[::-1]
    return fsteps + csteps


def gather_blocks(block, order):
    nb = bits_of("fsdp") + bits_of("ctx")
    buf = block.reshape((1,) * nb + block.shape)
    for axis, bit, dim in grid_steps(order):
        recv = exchange(buf, axis, 1 << bit)
        low = my_bit(axis, bit) == 0
        buf = jnp.concatenate([jnp.where(low, buf, recv), jnp.where(low, recv, buf)], axis=dim)
    return buf.reshape((-1,) + block.shape)


def scatter_blocks(blocks, order, last=F32):
    nb = bits_of("fsdp") + bits_of("ctx")
    buf = blocks.reshape((2,) * nb + blocks.shape[1:])
    steps = grid_steps(order)[::-1]
    for at, (axis, bit, dim) in enumerate(steps):
        mine = my_bit(axis, bit)
        send = lax.dynamic_index_in_dim(buf, 1 - mine, dim, keepdims=True)
        keep = lax.dynamic_index_in_dim(buf, mine, dim, keepdims=True)
        recv = exchange(send, axis, 1 << bit)
        kind = last if at == len(steps) - 1 else BF
        buf = (keep.astype(F32) + recv.astype(F32)).astype(kind)
    return buf.reshape(blocks.shape[1:])


def rms_norm(values_in, gain):
    return (
        values_in * lax.rsqrt(jnp.mean(values_in * values_in, axis=-1, keepdims=True) + EPS) * gain
    )


def rotate(values_in, cosine, sine_table):
    half_width = values_in.shape[-1] // 2
    lower_half = values_in[..., :half_width]
    upper_half = values_in[..., half_width:]
    return jnp.concatenate(
        [
            lower_half * cosine - upper_half * sine_table,
            upper_half * cosine + lower_half * sine_table,
        ],
        axis=-1,
    )


def rope_tables(places, log_base):
    half_width = HD // 2
    inverse = jnp.exp(-log_base * (jnp.arange(half_width, dtype=F32) * (2.0 / HD)))
    angles = places.astype(F32)[:, None] * inverse[None, :]
    return (jnp.cos(angles), jnp.sin(angles))


def head_prepare(query_product, key_product, query_gain, key_gain, cosine, sine_table):
    token_count = query_product.shape[0]
    queries = rms_norm(query_product.reshape(token_count, HEADS, HD), query_gain)
    keys_normed = rms_norm(key_product, key_gain)
    return (
        rotate(queries, cosine[:, None, :], sine_table[:, None, :]),
        rotate(keys_normed, cosine, sine_table),
    )


def gated(gate, up):
    return jax.nn.gelu(gate, approximate=True) * up


def dot(a, b):
    return jnp.dot(a, b, preferred_element_type=F32)


def dot_t(a, b):
    return jnp.einsum("tc,dc->td", a, b, preferred_element_type=F32)


def t_dot(a, b):
    return jnp.einsum("ta,tb->ab", a, b, preferred_element_type=F32)


def attention_weights(flat_queries, all_keys, places, all_places, window):
    query_places = jnp.repeat(places, HEADS)
    allowed = (all_places[None, :] <= query_places[:, None]) & (
        query_places[:, None] - all_places[None, :] < window
    )
    scores = dot_t(flat_queries, all_keys) * SCALE
    scores = jnp.where(allowed, scores, -1e30)
    maximum = jnp.max(scores, axis=-1, keepdims=True)
    weights = jnp.exp(scores - maximum)
    return weights / jnp.sum(weights, axis=-1, keepdims=True)


def pick(first, own, other):
    return jnp.where(first, own, other), jnp.where(first, other, own)


def key_exchange(keys_values):
    count = lax.axis_size("ctx")
    return [keys_values] + [exchange(keys_values, "ctx", j) for j in range(1, count)]


def key_return(blocks):
    count = lax.axis_size("ctx")
    total = blocks[0]
    for j in range(1, count):
        total = total + exchange(blocks[j].astype(BF), "ctx", j).astype(F32)
    return total


def layer_forward(full, x, places, all_places, window, cosine, sine_table, first):
    q_own, q_oth, g_own, g_oth, w_out, w_down, gains, heads = full
    tokens = x.shape[0]
    normed = rms_norm(x, gains[0]).astype(BF)
    lo, hi = pick(first, dot(normed, q_own), dot(normed, q_oth))
    query_product = jnp.concatenate([lo[:, :QH], hi[:, :QH]], axis=1)
    key_product = lo[:, QH:]
    queries, keys_rot = head_prepare(
        query_product, key_product, heads[0], heads[1], cosine, sine_table
    )
    flat_queries = queries.astype(BF).reshape(tokens * HEADS, HD)
    keys_values = jnp.concatenate([keys_rot, hi[:, QH:]], axis=1).astype(BF)
    all_kv = jnp.concatenate(key_exchange(keys_values), axis=0)
    all_keys, all_values = all_kv[:, :HD], all_kv[:, HD:]
    prob_low = attention_weights(flat_queries, all_keys, places, all_places, window).astype(BF)
    mixed = dot(prob_low, all_values).reshape(tokens, HEADS * HD).astype(BF)
    branch = dot(mixed, w_out)
    middle = x + rms_norm(branch, gains[1])
    normed_two = rms_norm(middle, gains[2]).astype(BF)
    gate, up = pick(first, dot(normed_two, g_own), dot(normed_two, g_oth))
    hidden = gated(gate, up).astype(BF)
    down_out = dot(hidden, w_down)
    result = middle + rms_norm(down_out, gains[3])
    kept = dict(
        normed=normed, query_product=query_product, key_product=key_product,
        flat_queries=flat_queries, all_keys=all_keys, all_values=all_values, mixed=mixed,
        branch=branch, middle=middle, normed_two=normed_two, gate=gate, up=up, hidden=hidden,
        down_out=down_out, x=x,
    )
    return result, kept


def halves(grad, count):
    return grad.reshape(count, 2, -1, grad.shape[-1])


def layer_backward(full, kept, grad_result, places, all_places, window, cosine, sine_table, first):
    q_own, q_oth, g_own, g_oth, w_out, w_down, gains, heads = full
    x = kept["x"]
    tokens = x.shape[0]
    _, back_last = jax.vjp(rms_norm, kept["down_out"], gains[3])
    grad_down, gain_three = back_last(grad_result)
    grad_down_low = grad_down.astype(BF)
    grad_hidden = dot_t(grad_down_low, w_down)
    _, back_gated = jax.vjp(gated, kept["gate"], kept["up"])
    grad_gate, grad_up = back_gated(grad_hidden)
    gu_own, gu_oth = pick(first, grad_gate.astype(BF), grad_up.astype(BF))
    grad_normed_two = dot_t(gu_own, g_own) + dot_t(gu_oth, g_oth)
    _, back_norm_two = jax.vjp(rms_norm, kept["middle"], gains[2])
    grad_middle_part, gain_two = back_norm_two(grad_normed_two)
    grad_middle = grad_result + grad_middle_part
    _, back_norm_one = jax.vjp(rms_norm, kept["branch"], gains[1])
    grad_branch, gain_one = back_norm_one(grad_middle)
    grad_branch_low = grad_branch.astype(BF)
    grad_mixed = dot_t(grad_branch_low, w_out).astype(BF).reshape(tokens * HEADS, HD)
    wg_g = (
        t_dot(kept["normed_two"], gu_own).astype(BF),
        t_dot(kept["normed_two"], gu_oth).astype(BF),
    )
    wg_out = t_dot(kept["mixed"], grad_branch_low).astype(BF)
    wg_down = t_dot(kept["hidden"], grad_down_low).astype(BF)
    flat_queries, all_keys, all_values = kept["flat_queries"], kept["all_keys"], kept["all_values"]
    probabilities = attention_weights(flat_queries, all_keys, places, all_places, window)
    prob_low = probabilities.astype(BF)
    grad_probs = dot_t(grad_mixed, all_values)
    inner_sum = jnp.sum(probabilities * grad_probs, axis=-1, keepdims=True)
    grad_scores = (probabilities * (grad_probs - inner_sum)).astype(BF)
    grad_keys_all = t_dot(grad_scores, flat_queries) * SCALE
    grad_values_all = t_dot(prob_low, grad_mixed)
    blocks = jnp.concatenate([grad_keys_all, grad_values_all], axis=1)
    grad_kv = key_return(jnp.split(blocks, lax.axis_size("ctx"), axis=0))
    grad_queries = dot(grad_scores, all_keys) * SCALE

    def prepare(query_in, key_in, query_gain, key_gain):
        return head_prepare(query_in, key_in, query_gain, key_gain, cosine, sine_table)

    _, back_heads = jax.vjp(
        prepare, kept["query_product"], kept["key_product"], heads[0], heads[1]
    )
    grad_qp, grad_kp, query_gain, key_gain = back_heads(
        (grad_queries.reshape(tokens, HEADS, HD), grad_kv[:, :HD])
    )
    lo = jnp.concatenate([grad_qp[:, :QH], grad_kp], axis=1).astype(BF)
    hi = jnp.concatenate([grad_qp[:, QH:], grad_kv[:, HD:]], axis=1).astype(BF)
    q_grad_own, q_grad_oth = pick(first, lo, hi)
    grad_normed = dot_t(q_grad_own, q_own) + dot_t(q_grad_oth, q_oth)
    _, back_norm_zero = jax.vjp(rms_norm, x, gains[0])
    grad_part, gain_zero = back_norm_zero(grad_normed)
    grad_x = grad_middle + grad_part
    wg_q = (
        t_dot(kept["normed"], q_grad_own).astype(BF),
        t_dot(kept["normed"], q_grad_oth).astype(BF),
    )
    gain_grads = (
        jnp.stack([gain_zero, gain_one, gain_two, gain_three]),
        jnp.stack([query_gain, key_gain]),
    )
    return grad_x, wg_q, wg_g, wg_out, wg_down, gain_grads


def local(
    boundary, positions, w_query, w_key_value, w_out, w_gate_up, w_down, norm_gains, head_gains
):
    section = lax.axis_index("section")
    first = section == 0
    ctx_index = lax.axis_index("ctx")
    tokens = boundary.shape[3]
    seq_length = positions.shape[-1]
    nr = w_query.shape[1]
    hr = head_gains.shape[2]
    ro, rd = w_out.shape[1], w_down.shape[1]
    blocks = lax.axis_size("fsdp") * lax.axis_size("ctx")

    moved = exchange(lax.dynamic_index_in_dim(boundary[0, :, 0], 1 - section, 0, False), "section", 1)
    kept_in = lax.dynamic_index_in_dim(boundary[0, :, 0], section, 0, False)
    x0, cotangent = pick(first, kept_in, moved)
    x0, cotangent = x0.astype(F32), cotangent.astype(F32)
    seq_places = lax.dynamic_index_in_dim(positions[:, 0], section, 0, False)
    near = [
        lax.dynamic_slice_in_dim(seq_places, (ctx_index ^ j) * tokens, tokens)
        for j in range(lax.axis_size("ctx"))
    ]
    places, all_places = near[0], jnp.concatenate(near)

    gain_cols = jnp.concatenate(
        [
            norm_gains[0].T,
            jnp.pad(head_gains[0].T, ((0, nr - hr), (0, 0))),
            jnp.zeros((nr, 128 - 6), BF),
        ],
        axis=1,
    )
    cols = [
        jnp.concatenate(
            [
                w_query[0, :, h * QH : (h + 1) * QH],
                w_key_value[0, :, h * HD : (h + 1) * HD],
                gain_cols,
                w_gate_up[0, :, h * FF : (h + 1) * FF],
            ],
            axis=1,
        )
        for h in range(2)
    ]
    rows = [
        jnp.concatenate(
            [
                w_out[0, h * ro // 2 : (h + 1) * ro // 2],
                w_down[0, h * rd // 2 : (h + 1) * rd // 2],
            ],
            axis=0,
        )
        for h in range(2)
    ]
    col_keep, col_send = pick(first, cols[0], cols[1])
    row_keep, row_send = pick(first, rows[0], rows[1])
    col_recv = exchange(col_send, "section", 1)
    row_recv = exchange(row_send, "section", 1)
    layer_cols = pick(first, col_keep, col_recv)
    layer_rows = pick(first, row_keep, row_recv)

    def swap(own):
        return own, exchange(own, "section", 1)

    def assemble(q_pair, g_pair, b_pair):
        q_own, q_oth = [v.reshape(blocks * nr, -1) for v in q_pair]
        g_own, g_oth = [v.reshape(blocks * nr, -1) for v in g_pair]
        b_own, b_oth = b_pair
        b_lo, b_hi = pick(first, b_own, b_oth)
        full_out = jnp.concatenate([b_lo[:, : ro // 2], b_hi[:, : ro // 2]], axis=1)
        full_down = jnp.concatenate([b_lo[:, ro // 2 :], b_hi[:, ro // 2 :]], axis=1)
        gain_part = q_own[:, QW:].astype(F32)
        gains = gain_part[:, :4].T
        heads = gain_part[:, 4:6].reshape(blocks, nr, 2)[:, :hr].reshape(blocks * hr, 2).T
        return (
            q_own[:, :QW], q_oth[:, :QW], g_own, g_oth,
            full_out.reshape(-1, D), full_down.reshape(-1, D), gains, heads,
        )

    full0 = assemble(
        swap(gather_blocks(layer_cols[0][:, :QP], "yx")),
        swap(gather_blocks(layer_cols[0][:, QP:], "xy")),
        swap(gather_blocks(layer_rows[0], "yx")),
    )
    col_pair = swap(gather_blocks(layer_cols[1], "xy"))
    full1 = assemble(
        [v[..., :QP] for v in col_pair],
        [v[..., QP:] for v in col_pair],
        swap(gather_blocks(layer_rows[1], "yx")),
    )

    tables = [rope_tables(places, base) for base in BASES]
    windows = (WIN, seq_length)

    y0, kept0 = layer_forward(full0, x0, places, all_places, windows[0], *tables[0], first)
    y1, kept1 = layer_forward(
        full1, y0.astype(BF).astype(F32), places, all_places, windows[1], *tables[1], first
    )

    def reduce_g(wg_g):
        return wg_g[0].astype(F32) + exchange(wg_g[1], "section", 1).astype(F32)

    def reduce_b(wg_out, wg_down):
        out_half, down_half = halves(wg_out, blocks), halves(wg_down, blocks)

        def part(index):
            return jnp.concatenate(
                [
                    lax.dynamic_index_in_dim(out_half, index, 1, False),
                    lax.dynamic_index_in_dim(down_half, index, 1, False),
                ],
                axis=1,
            )

        recv = exchange(part(1 - section), "section", 1)
        summed = (part(section).astype(F32) + recv.astype(F32)).astype(BF)
        return scatter_blocks(summed, "yx")

    def gain_columns(gain_grads):
        norm_part = gain_grads[0].T
        head_part = gain_grads[1].T.reshape(blocks, hr, 2)
        head_part = jnp.pad(head_part, ((0, 0), (0, nr - hr), (0, 0))).reshape(blocks * nr, 2)
        return jnp.concatenate(
            [norm_part, head_part, jnp.zeros((blocks * nr, 128 - 6), F32)], axis=1
        ).astype(BF)

    def reduce_q(wg_q, gain_grads):
        cols = gain_columns(gain_grads)
        own = jnp.concatenate([wg_q[0], cols], axis=1)
        oth = jnp.concatenate([wg_q[1], cols], axis=1)
        return own.astype(F32) + exchange(oth, "section", 1).astype(F32)

    def in_blocks(v):
        return v.astype(BF).reshape(blocks, nr, -1)

    grad1, wg_q, wg_g, wg_out, wg_down, gain_grads = layer_backward(
        full1, kept1, cotangent, places, all_places, windows[1], *tables[1], first
    )
    red_b1 = reduce_b(wg_out, wg_down)
    col_sum = jnp.concatenate([reduce_q(wg_q, gain_grads), reduce_g(wg_g)], axis=1)
    red_c1 = scatter_blocks(in_blocks(col_sum), "xy")
    grad0, wg_q, wg_g, wg_out, wg_down, gain_grads = layer_backward(
        full0, kept0, grad1.astype(BF).astype(F32), places, all_places, windows[0], *tables[0], first
    )
    red_b0 = reduce_b(wg_out, wg_down)
    red_g0 = scatter_blocks(in_blocks(reduce_g(wg_g)), "xy")
    red_q0 = scatter_blocks(in_blocks(reduce_q(wg_q, gain_grads)), "yx")
    red_c0 = jnp.concatenate([red_q0, red_g0], axis=1)

    out_moved = exchange(jnp.where(first, y1, grad0), "section", 1)
    c_keep, c_send = pick(first, red_c0, red_c1)
    b_keep, b_send = pick(first, red_b0, red_b1)
    c_lo, c_hi = pick(first, c_keep, exchange(c_send, "section", 1))
    b_lo, b_hi = pick(first, b_keep, exchange(b_send, "section", 1))
    boundary_out = jnp.where(
        first, jnp.stack([grad0, out_moved]), jnp.stack([out_moved, y1])
    )[None, :, None]
    return (
        boundary_out,
        jnp.concatenate([c_lo[:, :QH], c_hi[:, :QH]], axis=1)[None],
        jnp.concatenate([c_lo[:, QH:QW], c_hi[:, QH:QW]], axis=1)[None],
        jnp.concatenate([b_lo[: ro // 2], b_hi[: ro // 2]], axis=0)[None],
        jnp.concatenate([c_lo[:, QP:], c_hi[:, QP:]], axis=1)[None],
        jnp.concatenate([b_lo[ro // 2 :], b_hi[ro // 2 :]], axis=0)[None],
        c_lo[:, QW : QW + 4].T[None],
        c_lo[:hr, QW + 4 : QW + 6].T[None],
    )


def solution(mesh):
    in_specs = (
        P("section", None, "fsdp", "ctx", None),
        P(None, "fsdp", None),
        P("section", ("fsdp", "ctx"), None),
        P("section", ("fsdp", "ctx"), None),
        P("section", ("fsdp", "ctx"), None),
        P("section", ("fsdp", "ctx"), None),
        P("section", ("fsdp", "ctx"), None),
        P("section", None, ("fsdp", "ctx")),
        P("section", None, ("fsdp", "ctx")),
    )
    out_specs = (
        P("section", None, "fsdp", "ctx", None),
        P("section", ("fsdp", "ctx"), None),
        P("section", ("fsdp", "ctx"), None),
        P("section", ("fsdp", "ctx"), None),
        P("section", ("fsdp", "ctx"), None),
        P("section", ("fsdp", "ctx"), None),
        P("section", None, ("fsdp", "ctx")),
        P("section", None, ("fsdp", "ctx")),
    )
    return jax.shard_map(local, mesh=mesh, in_specs=in_specs, out_specs=out_specs, check_vma=False)
```

```python
import math

import jax
import jax.numpy as jnp
from jax import lax
from jax.sharding import PartitionSpec as P

D = 640
FF = 2048
HEADS = 4
HD = 256
WIN = 512
MB = 2
QH = 2 * HD
QW = QH + HD
QP = QW + 128

EPS = 1e-06
BASES = (math.log(10000.0), math.log(1000000.0))
SCALE = 1.0 / math.sqrt(HD)
BF = jnp.bfloat16
F32 = jnp.float32


def bits_of(axis):
    return (lax.axis_size(axis) - 1).bit_length()


def exchange(shard, axis, flip):
    pairs = [(i, i ^ flip) for i in range(lax.axis_size(axis))]
    return lax.ppermute(shard, axis, pairs)


def my_bit(axis, bit):
    return (lax.axis_index(axis) >> bit) & 1


def tie(*values):
    return lax.optimization_barrier(values)


def ctx_steps(order):
    count = bits_of("ctx")
    steps = [(bit, count - bit) for bit in range(count)]
    return steps if order == "xy" else steps[::-1]


def z_gather(block):
    count = lax.axis_size("fsdp")
    pieces = [block] + [exchange(block, "fsdp", j) for j in range(1, count)]
    me = lax.axis_index("fsdp")
    return jnp.stack([lax.select_n(me ^ at, *pieces) for at in range(count)])


def ctx_open(buf):
    return buf.reshape((buf.shape[0],) + (1,) * bits_of("ctx") + buf.shape[1:])


def ctx_gather(buf, steps):
    for bit, dim in steps:
        recv = exchange(buf, "ctx", 1 << bit)
        low = my_bit("ctx", bit) == 0
        buf = jnp.concatenate([jnp.where(low, buf, recv), jnp.where(low, recv, buf)], axis=dim)
    return buf


def ctx_close(buf, tail):
    return buf.reshape((-1,) + tail)


def ctx_scatter(buf, steps):
    for bit, dim in steps:
        mine = my_bit("ctx", bit)
        send = lax.dynamic_index_in_dim(buf, 1 - mine, dim, keepdims=True)
        keep = lax.dynamic_index_in_dim(buf, mine, dim, keepdims=True)
        recv = exchange(send, "ctx", 1 << bit)
        buf = (keep.astype(F32) + recv.astype(F32)).astype(BF)
    return buf


def z_scatter(buf):
    me = lax.axis_index("fsdp")
    total = lax.dynamic_index_in_dim(buf, me, 0, False).astype(F32)
    for j in range(1, lax.axis_size("fsdp")):
        part = lax.dynamic_index_in_dim(buf, me ^ j, 0, False)
        total = total + exchange(part, "fsdp", j).astype(F32)
    return total


class Gather:
    ORDERS = ("yx", "xy", "yx", "xy")

    def __init__(self, cols, rows):
        self.q, self.g, self.b = cols[:, :QP], cols[:, QP:], rows

    def after(self, *others):
        self.q, self.g, self.b = tie(self.q, self.g, self.b, *others)[:3]

    def along_z(self):
        q, g, b = z_gather(self.q), z_gather(self.g), z_gather(self.b)
        half = g.shape[0] // 2
        self.parts = [ctx_open(v) for v in (q, g[:half], g[half:], b)]

    def parts_after(self, *others):
        self.parts = list(tie(*self.parts, *others)[:4])

    def plane(self, stage):
        done = []
        for v, order in zip(self.parts, self.ORDERS):
            steps = ctx_steps(order)
            done.append(ctx_gather(v, steps[:1] if stage == 0 else steps[1:]))
        self.parts = done

    def pairs(self):
        q, g1, g2, b = self.parts
        q = ctx_close(q, self.q.shape)
        b = ctx_close(b, self.b.shape)
        g = jnp.concatenate([ctx_close(g1, self.g.shape), ctx_close(g2, self.g.shape)], axis=0)
        return [(v, exchange(v, "section", 1)) for v in (q, g, b)]


class Scatter:
    def __init__(self, blocks, split):
        fs, cb = lax.axis_size("fsdp"), bits_of("ctx")
        self.tail = blocks.shape[1:]
        buf = blocks.reshape((fs,) + (2,) * cb + self.tail)
        self.parts = [(buf[: fs // 2], "xy"), (buf[fs // 2 :], "yx")] if split else [(buf, "xy")]

    def after(self, *others):
        values = tie(*[p[0] for p in self.parts], *others)
        self.parts = [(v, p[1]) for v, p in zip(values, self.parts)]

    def values(self):
        return [p[0] for p in self.parts]

    def plane(self, stage):
        done = []
        for v, order in self.parts:
            steps = ctx_steps(order)
            done.append((ctx_scatter(v, steps[:1] if stage == 0 else steps[1:]), order))
        self.parts = done

    def along_z(self):
        buf = jnp.concatenate([v.reshape((-1,) + self.tail) for v in self.values()], axis=0)
        return z_scatter(buf)


def rms_norm(values_in, gain):
    return (
        values_in * lax.rsqrt(jnp.mean(values_in * values_in, axis=-1, keepdims=True) + EPS) * gain
    )


def rotate(values_in, cosine, sine_table):
    half_width = values_in.shape[-1] // 2
    lower_half = values_in[..., :half_width]
    upper_half = values_in[..., half_width:]
    return jnp.concatenate(
        [
            lower_half * cosine - upper_half * sine_table,
            upper_half * cosine + lower_half * sine_table,
        ],
        axis=-1,
    )


def rope_tables(places, log_base):
    half_width = HD // 2
    inverse = jnp.exp(-log_base * (jnp.arange(half_width, dtype=F32) * (2.0 / HD)))
    angles = places.astype(F32)[:, None] * inverse[None, :]
    return (jnp.cos(angles), jnp.sin(angles))


def head_prepare(query_product, key_product, query_gain, key_gain, cosine, sine_table):
    token_count = query_product.shape[0]
    queries = rms_norm(query_product.reshape(token_count, HEADS, HD), query_gain)
    keys_normed = rms_norm(key_product, key_gain)
    return (
        rotate(queries, cosine[:, None, :], sine_table[:, None, :]),
        rotate(keys_normed, cosine, sine_table),
    )


def gated(gate, up):
    return jax.nn.gelu(gate, approximate=True) * up


def dot(a, b):
    return jnp.dot(a, b, preferred_element_type=F32)


def dot_t(a, b):
    return jnp.einsum("tc,dc->td", a, b, preferred_element_type=F32)


def t_dot(a, b):
    return jnp.einsum("ta,tb->ab", a, b, preferred_element_type=F32)


def attention_weights(flat_queries, all_keys, places, all_places, window):
    query_places = jnp.repeat(places, HEADS)
    allowed = (all_places[None, :] <= query_places[:, None]) & (
        query_places[:, None] - all_places[None, :] < window
    )
    scores = dot_t(flat_queries, all_keys) * SCALE
    scores = jnp.where(allowed, scores, -1e30)
    maximum = jnp.max(scores, axis=-1, keepdims=True)
    weights = jnp.exp(scores - maximum)
    return weights / jnp.sum(weights, axis=-1, keepdims=True)


def pick(first, own, other):
    return jnp.where(first, own, other), jnp.where(first, other, own)


def key_exchange(keys_values):
    count = lax.axis_size("ctx")
    return [keys_values] + [exchange(keys_values, "ctx", j) for j in range(1, count)]


def key_return(blocks):
    count = lax.axis_size("ctx")
    total = blocks[0]
    for j in range(1, count):
        total = total + exchange(blocks[j].astype(BF), "ctx", j).astype(F32)
    return total


def forward_keys(full, x, cosine, sine_table, first):
    q_own, q_oth, gains, heads = full
    tokens = x.shape[0]
    normed = rms_norm(x, gains[0]).astype(BF)
    lo, hi = pick(first, dot(normed, q_own), dot(normed, q_oth))
    query_product = jnp.concatenate([lo[:, :QH], hi[:, :QH]], axis=1)
    key_product = lo[:, QH:]
    queries, keys_rot = head_prepare(
        query_product, key_product, heads[0], heads[1], cosine, sine_table
    )
    flat_queries = queries.astype(BF).reshape(tokens * HEADS, HD)
    keys_values = jnp.concatenate([keys_rot, hi[:, QH:]], axis=1).astype(BF)
    all_kv = jnp.concatenate(key_exchange(keys_values), axis=0)
    return dict(
        x=x, normed=normed, query_product=query_product, key_product=key_product,
        flat_queries=flat_queries, all_keys=all_kv[:, :HD], all_values=all_kv[:, HD:],
    )


def forward_attend(kept, places, all_places, window):
    tokens = kept["x"].shape[0]
    prob_low = attention_weights(
        kept["flat_queries"], kept["all_keys"], places, all_places, window
    ).astype(BF)
    return dot(prob_low, kept["all_values"]).reshape(tokens, HEADS * HD).astype(BF)


def forward_rest(full, kept, mixed, first):
    g_own, g_oth, w_out, w_down, gains = full
    branch = dot(mixed, w_out)
    middle = kept["x"] + rms_norm(branch, gains[1])
    normed_two = rms_norm(middle, gains[2]).astype(BF)
    gate, up = pick(first, dot(normed_two, g_own), dot(normed_two, g_oth))
    hidden = gated(gate, up).astype(BF)
    down_out = dot(hidden, w_down)
    kept.update(
        mixed=mixed, branch=branch, middle=middle, normed_two=normed_two, gate=gate, up=up,
        hidden=hidden, down_out=down_out,
    )
    return middle + rms_norm(down_out, gains[3])


def halves(grad, count):
    return grad.reshape(count, 2, -1, grad.shape[-1])


def backward_feed(full, kept, grad_result, first):
    g_own, g_oth, w_out, w_down, gains = full
    _, back_last = jax.vjp(rms_norm, kept["down_out"], gains[3])
    grad_down, gain_three = back_last(grad_result)
    grad_down_low = grad_down.astype(BF)
    grad_hidden = dot_t(grad_down_low, w_down)
    _, back_gated = jax.vjp(gated, kept["gate"], kept["up"])
    grad_gate, grad_up = back_gated(grad_hidden)
    gu_own, gu_oth = pick(first, grad_gate.astype(BF), grad_up.astype(BF))
    grad_normed_two = dot_t(gu_own, g_own) + dot_t(gu_oth, g_oth)
    _, back_norm_two = jax.vjp(rms_norm, kept["middle"], gains[2])
    grad_middle_part, gain_two = back_norm_two(grad_normed_two)
    grad_middle = grad_result + grad_middle_part
    _, back_norm_one = jax.vjp(rms_norm, kept["branch"], gains[1])
    grad_branch, gain_one = back_norm_one(grad_middle)
    grad_branch_low = grad_branch.astype(BF)
    wg_g = (t_dot(kept["normed_two"], gu_own), t_dot(kept["normed_two"], gu_oth).astype(BF))
    wg_out = t_dot(kept["mixed"], grad_branch_low).astype(BF)
    wg_down = t_dot(kept["hidden"], grad_down_low).astype(BF)
    return grad_middle, grad_branch_low, wg_g, wg_out, wg_down, [gain_one, gain_two, gain_three]


def backward_attend(w_out, kept, grad_branch_low, places, all_places, window):
    tokens = kept["x"].shape[0]
    grad_mixed = dot_t(grad_branch_low, w_out).astype(BF).reshape(tokens * HEADS, HD)
    flat_queries, all_keys, all_values = kept["flat_queries"], kept["all_keys"], kept["all_values"]
    probabilities = attention_weights(flat_queries, all_keys, places, all_places, window)
    prob_low = probabilities.astype(BF)
    grad_probs = dot_t(grad_mixed, all_values)
    inner_sum = jnp.sum(probabilities * grad_probs, axis=-1, keepdims=True)
    grad_scores = (probabilities * (grad_probs - inner_sum)).astype(BF)
    grad_keys_all = t_dot(grad_scores, flat_queries) * SCALE
    grad_values_all = t_dot(prob_low, grad_mixed)
    blocks = jnp.concatenate([grad_keys_all, grad_values_all], axis=1)
    grad_kv = key_return(jnp.split(blocks, lax.axis_size("ctx"), axis=0))
    grad_queries = dot(grad_scores, all_keys) * SCALE
    return grad_queries.reshape(tokens, HEADS, HD), grad_kv


def backward_keys(full, kept, grad_middle, grad_queries, grad_kv, cosine, sine_table, first):
    q_own, q_oth, gains, heads = full

    def prepare(query_in, key_in, query_gain, key_gain):
        return head_prepare(query_in, key_in, query_gain, key_gain, cosine, sine_table)

    _, back_heads = jax.vjp(
        prepare, kept["query_product"], kept["key_product"], heads[0], heads[1]
    )
    grad_qp, grad_kp, query_gain, key_gain = back_heads((grad_queries, grad_kv[:, :HD]))
    lo = jnp.concatenate([grad_qp[:, :QH], grad_kp], axis=1).astype(BF)
    hi = jnp.concatenate([grad_qp[:, QH:], grad_kv[:, HD:]], axis=1).astype(BF)
    q_grad_own, q_grad_oth = pick(first, lo, hi)
    grad_normed = dot_t(q_grad_own, q_own) + dot_t(q_grad_oth, q_oth)
    _, back_norm_zero = jax.vjp(rms_norm, kept["x"], gains[0])
    grad_part, gain_zero = back_norm_zero(grad_normed)
    wg_q = (
        t_dot(kept["normed"], q_grad_own).astype(BF),
        t_dot(kept["normed"], q_grad_oth).astype(BF),
    )
    return grad_middle + grad_part, wg_q, gain_zero, [query_gain, key_gain]


def local(
    boundary, positions, w_query, w_key_value, w_out, w_gate_up, w_down, norm_gains, head_gains
):
    section = lax.axis_index("section")
    first = section == 0
    ctx_index = lax.axis_index("ctx")
    tokens = boundary.shape[3]
    seq_length = positions.shape[-1]
    nr = w_query.shape[1]
    hr = head_gains.shape[2]
    ro, rd = w_out.shape[1], w_down.shape[1]
    blocks = lax.axis_size("fsdp") * lax.axis_size("ctx")

    moved = exchange(lax.dynamic_index_in_dim(boundary[0, :, 0], 1 - section, 0, False), "section", 1)
    kept_in = lax.dynamic_index_in_dim(boundary[0, :, 0], section, 0, False)
    x0, cotangent = pick(first, kept_in, moved)
    x0, cotangent = x0.astype(F32), cotangent.astype(F32)
    seq_places = lax.dynamic_index_in_dim(positions[:, 0], section, 0, False)
    near = [
        lax.dynamic_slice_in_dim(seq_places, (ctx_index ^ j) * tokens, tokens)
        for j in range(lax.axis_size("ctx"))
    ]
    places, all_places = near[0], jnp.concatenate(near)

    gain_cols = jnp.concatenate(
        [
            norm_gains[0].T,
            jnp.pad(head_gains[0].T, ((0, nr - hr), (0, 0))),
            jnp.zeros((nr, 128 - 6), BF),
        ],
        axis=1,
    )
    cols = [
        jnp.concatenate(
            [
                w_query[0, :, h * QH : (h + 1) * QH],
                w_key_value[0, :, h * HD : (h + 1) * HD],
                gain_cols,
                w_gate_up[0, :, h * FF : (h + 1) * FF],
            ],
            axis=1,
        )
        for h in range(2)
    ]
    rows = [
        jnp.concatenate(
            [
                w_out[0, h * ro // 2 : (h + 1) * ro // 2],
                w_down[0, h * rd // 2 : (h + 1) * rd // 2],
            ],
            axis=0,
        )
        for h in range(2)
    ]
    col_keep, col_send = pick(first, cols[0], cols[1])
    row_keep, row_send = pick(first, rows[0], rows[1])
    col_recv = exchange(col_send, "section", 1)
    row_recv = exchange(row_send, "section", 1)
    layer_cols = pick(first, col_keep, col_recv)
    layer_rows = pick(first, row_keep, row_recv)

    def query_side(pair):
        q_own, q_oth = [v.reshape(blocks * nr, -1) for v in pair]
        gain_part = q_own[:, QW:].astype(F32)
        gains = gain_part[:, :4].T
        heads = gain_part[:, 4:6].reshape(blocks, nr, 2)[:, :hr].reshape(blocks * hr, 2).T
        return q_own[:, :QW], q_oth[:, :QW], gains, heads

    def feed_side(g_pair, b_pair, gains):
        g_own, g_oth = [v.reshape(blocks * nr, -1) for v in g_pair]
        b_lo, b_hi = pick(first, *b_pair)
        full_out = jnp.concatenate([b_lo[:, : ro // 2], b_hi[:, : ro // 2]], axis=1)
        full_down = jnp.concatenate([b_lo[:, ro // 2 :], b_hi[:, ro // 2 :]], axis=1)
        return g_own, g_oth, full_out.reshape(-1, D), full_down.reshape(-1, D), gains

    def reduce_cols(own, other):
        summed = own.astype(F32) + exchange(other, "section", 1).astype(F32)
        return summed.astype(BF).reshape(blocks, nr, -1)

    def reduce_rows(wg_out, wg_down):
        out_half, down_half = halves(wg_out, blocks), halves(wg_down, blocks)

        def part(index):
            return jnp.concatenate(
                [
                    lax.dynamic_index_in_dim(out_half, index, 1, False),
                    lax.dynamic_index_in_dim(down_half, index, 1, False),
                ],
                axis=1,
            )

        recv = exchange(part(1 - section), "section", 1)
        return (part(section).astype(F32) + recv.astype(F32)).astype(BF)

    def reduce_query(wg_q, norm_grads, head_grads):
        norm_part = jnp.stack(norm_grads).T
        head_part = jnp.stack(head_grads).T.reshape(blocks, hr, 2)
        head_part = jnp.pad(head_part, ((0, 0), (0, nr - hr), (0, 0))).reshape(blocks * nr, 2)
        fill = jnp.zeros((blocks * nr, 128 - 6), F32)
        cols = jnp.concatenate([norm_part, head_part, fill], axis=1).astype(BF)
        own = jnp.concatenate([wg_q[0], cols], axis=1)
        oth = jnp.concatenate([wg_q[1], cols], axis=1)
        return reduce_cols(own, oth)

    tables = [rope_tables(places, base) for base in BASES]
    windows = (WIN, seq_length)

    gather0 = Gather(layer_cols[0], layer_rows[0])
    gather1 = Gather(layer_cols[1], layer_rows[1])
    gather0.along_z()
    gather1.after(*gather0.parts)
    gather0.plane(0)
    gather0.plane(1)
    pairs0 = gather0.pairs()
    query0 = query_side(pairs0[0])
    kept0 = forward_keys(query0, x0, *tables[0], first)
    gather1.along_z()
    kept0["all_keys"], *gather1.parts = tie(kept0["all_keys"], *gather1.parts, *gather0.parts)[:5]
    mixed = forward_attend(kept0, places, all_places, windows[0])
    gather1.plane(0)
    mixed, *gather1.parts = tie(mixed, *gather1.parts)
    feed0 = feed_side(*pairs0[1:], query0[2])
    y0 = forward_rest(feed0, kept0, mixed, first).astype(BF)
    gather1.plane(1)
    y0, *gather1.parts = tie(y0, *gather1.parts)
    pairs1 = gather1.pairs()
    query1 = query_side(pairs1[0])
    kept1 = forward_keys(query1, y0.astype(F32), *tables[1], first)
    mixed = forward_attend(kept1, places, all_places, windows[1])
    feed1 = feed_side(*pairs1[1:], query1[2])
    y1 = forward_rest(feed1, kept1, mixed, first)

    middle1, branch1, wg_g, wg_out, wg_down, norm_grads = backward_feed(
        feed1, kept1, cotangent, first
    )
    wg_own, wg_oth, wg_out, wg_down = tie(wg_g[0], wg_g[1], wg_out, wg_down)
    scat_g1 = Scatter(reduce_cols(wg_own, wg_oth), True)
    scat_b1 = Scatter(reduce_rows(wg_out, wg_down), False)
    grad_q, grad_kv = backward_attend(feed1[2], kept1, branch1, places, all_places, windows[1])
    grad_q, grad_kv, *held = tie(grad_q, grad_kv, *scat_g1.values(), *scat_b1.values())
    scat_g1.after(*held)
    scat_b1.after(*held)
    scat_g1.plane(0)
    scat_b1.plane(0)
    grad1, wg_q, gain_zero, head_grads = backward_keys(
        query1, kept1, middle1, grad_q, grad_kv, *tables[1], first
    )
    grad1 = grad1.astype(BF)
    wg_q0, wg_q1, grad1, *held = tie(wg_q[0], wg_q[1], grad1, *scat_g1.values(), *scat_b1.values())
    scat_g1.after(*held)
    scat_b1.after(*held)
    scat_g1.plane(1)
    scat_b1.plane(1)
    scat_q1 = Scatter(reduce_query((wg_q0, wg_q1), [gain_zero] + norm_grads, head_grads), False)

    middle0, branch0, wg_g, wg_out, wg_down, norm_grads = backward_feed(
        feed0, kept0, grad1.astype(F32), first
    )
    branch0, wg_own, wg_oth, wg_out, wg_down, *held = tie(
        branch0, wg_g[0], wg_g[1], wg_out, wg_down,
        *scat_g1.values(), *scat_b1.values(), *scat_q1.values()
    )
    scat_g1.after(*held)
    scat_b1.after(*held)
    scat_q1.after(*held)
    red_g1, red_b1 = scat_g1.along_z(), scat_b1.along_z()
    scat_g0 = Scatter(reduce_cols(wg_own, wg_oth), True)
    scat_b0 = Scatter(reduce_rows(wg_out, wg_down), False)
    scat_q1.plane(0)
    grad_q, grad_kv = backward_attend(feed0[2], kept0, branch0, places, all_places, windows[0])
    grad_q, grad_kv, red_g1, red_b1, *held = tie(
        grad_q, grad_kv, red_g1, red_b1,
        *scat_g0.values(), *scat_b0.values(), *scat_q1.values()
    )
    scat_g0.after(*held)
    scat_b0.after(*held)
    scat_q1.after(*held)
    scat_q1.plane(1)
    scat_g0.plane(0)
    scat_b0.plane(0)
    grad0, wg_q, gain_zero, head_grads = backward_keys(
        query0, kept0, middle0, grad_q, grad_kv, *tables[0], first
    )
    red_q1 = scat_q1.along_z()
    scat_q0 = Scatter(reduce_query(wg_q, [gain_zero] + norm_grads, head_grads), False)
    scat_g0.plane(1)
    scat_b0.plane(1)
    scat_q0.plane(0)
    scat_q0.plane(1)
    red_g0, red_b0 = scat_g0.along_z(), scat_b0.along_z()
    red_q0 = scat_q0.along_z()
    red_c0 = jnp.concatenate([red_q0, red_g0], axis=1)
    red_c1 = jnp.concatenate([red_q1, red_g1], axis=1)

    out_moved = exchange(jnp.where(first, y1, grad0), "section", 1)
    c_keep, c_send = pick(first, red_c0, red_c1)
    b_keep, b_send = pick(first, red_b0, red_b1)
    c_lo, c_hi = pick(first, c_keep, exchange(c_send, "section", 1))
    b_lo, b_hi = pick(first, b_keep, exchange(b_send, "section", 1))
    boundary_out = jnp.where(
        first, jnp.stack([grad0, out_moved]), jnp.stack([out_moved, y1])
    )[None, :, None]
    return (
        boundary_out,
        jnp.concatenate([c_lo[:, :QH], c_hi[:, :QH]], axis=1)[None],
        jnp.concatenate([c_lo[:, QH:QW], c_hi[:, QH:QW]], axis=1)[None],
        jnp.concatenate([b_lo[: ro // 2], b_hi[: ro // 2]], axis=0)[None],
        jnp.concatenate([c_lo[:, QP:], c_hi[:, QP:]], axis=1)[None],
        jnp.concatenate([b_lo[ro // 2 :], b_hi[ro // 2 :]], axis=0)[None],
        c_lo[:, QW : QW + 4].T[None],
        c_lo[:hr, QW + 4 : QW + 6].T[None],
    )


def solution(mesh):
    in_specs = (
        P("section", None, "fsdp", "ctx", None),
        P(None, "fsdp", None),
        P("section", ("fsdp", "ctx"), None),
        P("section", ("fsdp", "ctx"), None),
        P("section", ("fsdp", "ctx"), None),
        P("section", ("fsdp", "ctx"), None),
        P("section", ("fsdp", "ctx"), None),
        P("section", None, ("fsdp", "ctx")),
        P("section", None, ("fsdp", "ctx")),
    )
    out_specs = (
        P("section", None, "fsdp", "ctx", None),
        P("section", ("fsdp", "ctx"), None),
        P("section", ("fsdp", "ctx"), None),
        P("section", ("fsdp", "ctx"), None),
        P("section", ("fsdp", "ctx"), None),
        P("section", ("fsdp", "ctx"), None),
        P("section", None, ("fsdp", "ctx")),
        P("section", None, ("fsdp", "ctx")),
    )
    return jax.shard_map(local, mesh=mesh, in_specs=in_specs, out_specs=out_specs, check_vma=False)
```

```python
import math

import jax
import jax.numpy as jnp
from jax import lax
from jax.sharding import PartitionSpec as P

D = 640
FF = 2048
HEADS = 4
HD = 256
WIN = 512
MB = 2
QH = 2 * HD
QW = QH + HD
QP = QW + 128

EPS = 1e-06
BASES = (math.log(10000.0), math.log(1000000.0))
SCALE = 1.0 / math.sqrt(HD)
BF = jnp.bfloat16
GRID = ("fsdp", "ctx")
F32 = jnp.float32


def bits_of(axis):
    return (lax.axis_size(axis) - 1).bit_length()


def exchange(shard, axis, flip):
    pairs = [(i, i ^ flip) for i in range(lax.axis_size(axis))]
    return lax.ppermute(shard, axis, pairs)


def my_bit(axis, bit):
    return (lax.axis_index(axis) >> bit) & 1


def tie(*values):
    return lax.optimization_barrier(values)


def ctx_steps(order):
    count = bits_of("ctx")
    steps = [(bit, count - bit) for bit in range(count)]
    return steps if order == "xy" else steps[::-1]


def z_gather(block):
    count = lax.axis_size("fsdp")
    pairs = [(i, (i + 1) % count) for i in range(count)]
    pieces = [block]
    for _ in range(count - 1):
        pieces.append(lax.ppermute(pieces[-1], "fsdp", pairs))
    me = lax.axis_index("fsdp")
    return jnp.stack([lax.select_n((me - at) % count, *pieces) for at in range(count)])


def ctx_open(buf):
    return buf.reshape((buf.shape[0],) + (1,) * bits_of("ctx") + buf.shape[1:])


def ctx_gather(buf, steps):
    for bit, dim in steps:
        recv = exchange(buf, "ctx", 1 << bit)
        low = my_bit("ctx", bit) == 0
        buf = jnp.concatenate([jnp.where(low, buf, recv), jnp.where(low, recv, buf)], axis=dim)
    return buf


def ctx_close(buf, tail):
    return buf.reshape((-1,) + tail)


def ctx_scatter(buf, steps):
    for bit, dim in steps:
        mine = my_bit("ctx", bit)
        send = lax.dynamic_index_in_dim(buf, 1 - mine, dim, keepdims=True)
        keep = lax.dynamic_index_in_dim(buf, mine, dim, keepdims=True)
        recv = exchange(send, "ctx", 1 << bit)
        buf = (keep.astype(F32) + recv.astype(F32)).astype(BF)
    return buf


def z_scatter(buf):
    me = lax.axis_index("fsdp")
    total = lax.dynamic_index_in_dim(buf, me, 0, False).astype(F32)
    for j in range(1, lax.axis_size("fsdp")):
        part = lax.dynamic_index_in_dim(buf, me ^ j, 0, False)
        total = total + exchange(part, "fsdp", j).astype(F32)
    return total


class Gather:
    ORDERS = ("yx", "xy", "yx", "xy")

    def __init__(self, cols, rows):
        self.q, self.g, self.b = cols[:, :QP], cols[:, QP:], rows

    def after(self, *others):
        self.q, self.g, self.b = tie(self.q, self.g, self.b, *others)[:3]

    def along_z(self):
        q, g, b = z_gather(self.q), z_gather(self.g), z_gather(self.b)
        half = g.shape[0] // 2
        self.parts = [ctx_open(v) for v in (q, g[:half], g[half:], b)]

    def parts_after(self, *others):
        self.parts = list(tie(*self.parts, *others)[:4])

    def plane(self, stage):
        done = []
        for v, order in zip(self.parts, self.ORDERS):
            steps = ctx_steps(order)
            done.append(ctx_gather(v, steps[:1] if stage == 0 else steps[1:]))
        self.parts = done

    def pairs(self):
        q, g1, g2, b = self.parts
        q = ctx_close(q, self.q.shape)
        b = ctx_close(b, self.b.shape)
        g = jnp.concatenate([ctx_close(g1, self.g.shape), ctx_close(g2, self.g.shape)], axis=0)
        return [(v, exchange(v, "section", 1)) for v in (q, g, b)]


class Scatter:
    def __init__(self, blocks, split):
        fs, cb = lax.axis_size("fsdp"), bits_of("ctx")
        self.tail = blocks.shape[1:]
        buf = blocks.reshape((fs,) + (2,) * cb + self.tail)
        self.parts = [(buf[: fs // 2], "xy"), (buf[fs // 2 :], "yx")] if split else [(buf, "xy")]

    def after(self, *others):
        values = tie(*[p[0] for p in self.parts], *others)
        self.parts = [(v, p[1]) for v, p in zip(values, self.parts)]

    def values(self):
        return [p[0] for p in self.parts]

    def plane(self, stage):
        done = []
        for v, order in self.parts:
            steps = ctx_steps(order)
            done.append((ctx_scatter(v, steps[:1] if stage == 0 else steps[1:]), order))
        self.parts = done

    def along_z(self):
        buf = jnp.concatenate([v.reshape((-1,) + self.tail) for v in self.values()], axis=0)
        return z_scatter(buf)


def rms_norm(values_in, gain):
    return (
        values_in * lax.rsqrt(jnp.mean(values_in * values_in, axis=-1, keepdims=True) + EPS) * gain
    )


def rotate(values_in, cosine, sine_table):
    half_width = values_in.shape[-1] // 2
    lower_half = values_in[..., :half_width]
    upper_half = values_in[..., half_width:]
    return jnp.concatenate(
        [
            lower_half * cosine - upper_half * sine_table,
            upper_half * cosine + lower_half * sine_table,
        ],
        axis=-1,
    )


def rope_tables(places, log_base):
    half_width = HD // 2
    inverse = jnp.exp(-log_base * (jnp.arange(half_width, dtype=F32) * (2.0 / HD)))
    angles = places.astype(F32)[:, None] * inverse[None, :]
    return (jnp.cos(angles), jnp.sin(angles))


def head_prepare(query_product, key_product, query_gain, key_gain, cosine, sine_table):
    token_count = query_product.shape[0]
    queries = rms_norm(query_product.reshape(token_count, HEADS, HD), query_gain)
    keys_normed = rms_norm(key_product, key_gain)
    return (
        rotate(queries, cosine[:, None, :], sine_table[:, None, :]),
        rotate(keys_normed, cosine, sine_table),
    )


def gated(gate, up):
    return jax.nn.gelu(gate, approximate=True) * up


def dot(a, b):
    return jnp.dot(a, b, preferred_element_type=F32)


def dot_t(a, b):
    return jnp.einsum("tc,dc->td", a, b, preferred_element_type=F32)


def t_dot(a, b):
    return jnp.einsum("ta,tb->ab", a, b, preferred_element_type=F32)


def attention_weights(flat_queries, all_keys, places, all_places, window):
    query_places = jnp.repeat(places, HEADS)
    allowed = (all_places[None, :] <= query_places[:, None]) & (
        query_places[:, None] - all_places[None, :] < window
    )
    scores = dot_t(flat_queries, all_keys) * SCALE
    scores = jnp.where(allowed, scores, -1e30)
    maximum = jnp.max(scores, axis=-1, keepdims=True)
    weights = jnp.exp(scores - maximum)
    return weights / jnp.sum(weights, axis=-1, keepdims=True)


def pick(first, own, other):
    return jnp.where(first, own, other), jnp.where(first, other, own)


def key_exchange(keys_values):
    count = lax.axis_size("ctx")
    return [keys_values] + [exchange(keys_values, "ctx", j) for j in range(1, count)]


def key_return(blocks):
    count = lax.axis_size("ctx")
    blocks = jnp.split(blocks, count, axis=0)
    total = blocks[0]
    for j in range(1, count):
        total = total + exchange(blocks[j].astype(BF), "ctx", j).astype(F32)
    return total


def forward_keys(full, x, cosine, sine_table, first):
    q_own, q_oth, gains, heads = full
    tokens = x.shape[0]
    normed = rms_norm(x, gains[0]).astype(BF)
    lo, hi = pick(first, dot(normed, q_own), dot(normed, q_oth))
    query_product = jnp.concatenate([lo[:, :QH], hi[:, :QH]], axis=1)
    key_product = lo[:, QH:]
    queries, keys_rot = head_prepare(
        query_product, key_product, heads[0], heads[1], cosine, sine_table
    )
    flat_queries = queries.astype(BF).reshape(tokens * HEADS, HD)
    keys_values = jnp.concatenate([keys_rot, hi[:, QH:]], axis=1).astype(BF)
    all_kv = jnp.concatenate(key_exchange(keys_values), axis=0)
    return dict(
        x=x, normed=normed, query_product=query_product, key_product=key_product,
        flat_queries=flat_queries, all_keys=all_kv[:, :HD], all_values=all_kv[:, HD:],
    )


def forward_attend(kept, places, all_places, window):
    tokens = kept["x"].shape[0]
    prob_low = attention_weights(
        kept["flat_queries"], kept["all_keys"], places, all_places, window
    ).astype(BF)
    return dot(prob_low, kept["all_values"]).reshape(tokens, HEADS * HD).astype(BF)


def forward_rest(full, kept, mixed, first):
    g_own, g_oth, w_out, w_down, gains = full
    branch = dot(mixed, w_out)
    middle = kept["x"] + rms_norm(branch, gains[1])
    normed_two = rms_norm(middle, gains[2]).astype(BF)
    gate, up = pick(first, dot(normed_two, g_own), dot(normed_two, g_oth))
    hidden = gated(gate, up).astype(BF)
    down_out = dot(hidden, w_down)
    kept.update(
        mixed=mixed, branch=branch, middle=middle, normed_two=normed_two, gate=gate, up=up,
        hidden=hidden, down_out=down_out,
    )
    return middle + rms_norm(down_out, gains[3])


def halves(grad, count):
    return grad.reshape(count, 2, -1, grad.shape[-1])


def backward_feed(full, kept, grad_result, first):
    g_own, g_oth, w_out, w_down, gains = full
    _, back_last = jax.vjp(rms_norm, kept["down_out"], gains[3])
    grad_down, gain_three = back_last(grad_result)
    grad_down_low = grad_down.astype(BF)
    grad_hidden = dot_t(grad_down_low, w_down)
    _, back_gated = jax.vjp(gated, kept["gate"], kept["up"])
    grad_gate, grad_up = back_gated(grad_hidden)
    gu_own, gu_oth = pick(first, grad_gate.astype(BF), grad_up.astype(BF))
    grad_normed_two = dot_t(gu_own, g_own) + dot_t(gu_oth, g_oth)
    _, back_norm_two = jax.vjp(rms_norm, kept["middle"], gains[2])
    grad_middle_part, gain_two = back_norm_two(grad_normed_two)
    grad_middle = grad_result + grad_middle_part
    _, back_norm_one = jax.vjp(rms_norm, kept["branch"], gains[1])
    grad_branch, gain_one = back_norm_one(grad_middle)
    grad_branch_low = grad_branch.astype(BF)
    wg_g = (t_dot(kept["normed_two"], gu_own), t_dot(kept["normed_two"], gu_oth).astype(BF))
    wg_out = t_dot(kept["mixed"], grad_branch_low).astype(BF)
    wg_down = t_dot(kept["hidden"], grad_down_low).astype(BF)
    return grad_middle, grad_branch_low, wg_g, wg_out, wg_down, [gain_one, gain_two, gain_three]


def backward_attend(w_out, kept, grad_branch_low, places, all_places, window):
    tokens = kept["x"].shape[0]
    grad_mixed = dot_t(grad_branch_low, w_out).astype(BF).reshape(tokens * HEADS, HD)
    flat_queries, all_keys, all_values = kept["flat_queries"], kept["all_keys"], kept["all_values"]
    probabilities = attention_weights(flat_queries, all_keys, places, all_places, window)
    prob_low = probabilities.astype(BF)
    grad_probs = dot_t(grad_mixed, all_values)
    inner_sum = jnp.sum(probabilities * grad_probs, axis=-1, keepdims=True)
    grad_scores = (probabilities * (grad_probs - inner_sum)).astype(BF)
    grad_keys_all = t_dot(grad_scores, flat_queries) * SCALE
    grad_values_all = t_dot(prob_low, grad_mixed)
    blocks = jnp.concatenate([grad_keys_all, grad_values_all], axis=1)
    return grad_scores, blocks


def backward_queries(kept, grad_scores):
    grad_queries = dot(grad_scores, kept["all_keys"]) * SCALE
    return grad_queries.reshape(-1, HEADS, HD)


def backward_keys(full, kept, grad_middle, grad_queries, grad_kv, cosine, sine_table, first):
    q_own, q_oth, gains, heads = full

    def prepare(query_in, key_in, query_gain, key_gain):
        return head_prepare(query_in, key_in, query_gain, key_gain, cosine, sine_table)

    _, back_heads = jax.vjp(
        prepare, kept["query_product"], kept["key_product"], heads[0], heads[1]
    )
    grad_qp, grad_kp, query_gain, key_gain = back_heads((grad_queries, grad_kv[:, :HD]))
    lo = jnp.concatenate([grad_qp[:, :QH], grad_kp], axis=1).astype(BF)
    hi = jnp.concatenate([grad_qp[:, QH:], grad_kv[:, HD:]], axis=1).astype(BF)
    q_grad_own, q_grad_oth = pick(first, lo, hi)
    grad_normed = dot_t(q_grad_own, q_own) + dot_t(q_grad_oth, q_oth)
    _, back_norm_zero = jax.vjp(rms_norm, kept["x"], gains[0])
    grad_part, gain_zero = back_norm_zero(grad_normed)
    wg_q = (
        t_dot(kept["normed"], q_grad_own).astype(BF),
        t_dot(kept["normed"], q_grad_oth).astype(BF),
    )
    return grad_middle + grad_part, wg_q, gain_zero, [query_gain, key_gain]


def local(
    boundary, positions, w_query, w_key_value, w_out, w_gate_up, w_down, norm_gains, head_gains
):
    section = lax.axis_index("section")
    first = section == 0
    ctx_index = lax.axis_index("ctx")
    tokens = boundary.shape[3]
    seq_length = positions.shape[-1]
    nr = w_query.shape[1]
    hr = head_gains.shape[2]
    ro, rd = w_out.shape[1], w_down.shape[1]
    blocks = lax.axis_size("fsdp") * lax.axis_size("ctx")

    moved = exchange(lax.dynamic_index_in_dim(boundary[0, :, 0], 1 - section, 0, False), "section", 1)
    kept_in = lax.dynamic_index_in_dim(boundary[0, :, 0], section, 0, False)
    x0, cotangent = pick(first, kept_in, moved)
    x0, cotangent = x0.astype(F32), cotangent.astype(F32)
    seq_places = lax.dynamic_index_in_dim(positions[:, 0], section, 0, False)
    near = [
        lax.dynamic_slice_in_dim(seq_places, (ctx_index ^ j) * tokens, tokens)
        for j in range(lax.axis_size("ctx"))
    ]
    places, all_places = near[0], jnp.concatenate(near)

    gain_cols = jnp.concatenate(
        [
            norm_gains[0].T,
            jnp.pad(head_gains[0].T, ((0, nr - hr), (0, 0))),
            jnp.zeros((nr, 128 - 6), BF),
        ],
        axis=1,
    )
    cols = [
        jnp.concatenate(
            [
                w_query[0, :, h * QH : (h + 1) * QH],
                w_key_value[0, :, h * HD : (h + 1) * HD],
                gain_cols,
                w_gate_up[0, :, h * FF : (h + 1) * FF],
            ],
            axis=1,
        )
        for h in range(2)
    ]
    rows = [
        jnp.concatenate(
            [
                w_out[0, h * ro // 2 : (h + 1) * ro // 2],
                w_down[0, h * rd // 2 : (h + 1) * rd // 2],
            ],
            axis=0,
        )
        for h in range(2)
    ]
    col_keep, col_send = pick(first, cols[0], cols[1])
    row_keep, row_send = pick(first, rows[0], rows[1])
    col_recv = exchange(col_send, "section", 1)
    row_recv = exchange(row_send, "section", 1)
    layer_cols = pick(first, col_keep, col_recv)
    layer_rows = pick(first, row_keep, row_recv)

    def query_side(pair):
        q_own, q_oth = [v.reshape(blocks * nr, -1) for v in pair]
        gain_part = q_own[:, QW:].astype(F32)
        gains = gain_part[:, :4].T
        heads = gain_part[:, 4:6].reshape(blocks, nr, 2)[:, :hr].reshape(blocks * hr, 2).T
        return q_own[:, :QW], q_oth[:, :QW], gains, heads

    def feed_side(g_pair, b_pair, gains):
        g_own, g_oth = [v.reshape(blocks * nr, -1) for v in g_pair]
        b_lo, b_hi = pick(first, *b_pair)
        full_out = jnp.concatenate([b_lo[:, : ro // 2], b_hi[:, : ro // 2]], axis=1)
        full_down = jnp.concatenate([b_lo[:, ro // 2 :], b_hi[:, ro // 2 :]], axis=1)
        return g_own, g_oth, full_out.reshape(-1, D), full_down.reshape(-1, D), gains

    def reduce_cols(own, other):
        summed = own.astype(F32) + exchange(other, "section", 1).astype(F32)
        return summed.astype(BF).reshape(blocks, nr, -1)

    def reduce_rows(wg_out, wg_down):
        out_half, down_half = halves(wg_out, blocks), halves(wg_down, blocks)

        def part(index):
            return jnp.concatenate(
                [
                    lax.dynamic_index_in_dim(out_half, index, 1, False),
                    lax.dynamic_index_in_dim(down_half, index, 1, False),
                ],
                axis=1,
            )

        recv = exchange(part(1 - section), "section", 1)
        return (part(section).astype(F32) + recv.astype(F32)).astype(BF)

    def reduce_query(wg_q, norm_grads, head_grads):
        norm_part = jnp.stack(norm_grads).T
        head_part = jnp.stack(head_grads).T.reshape(blocks, hr, 2)
        head_part = jnp.pad(head_part, ((0, 0), (0, nr - hr), (0, 0))).reshape(blocks * nr, 2)
        fill = jnp.zeros((blocks * nr, 128 - 6), F32)
        cols = jnp.concatenate([norm_part, head_part, fill], axis=1).astype(BF)
        own = jnp.concatenate([wg_q[0], cols], axis=1)
        oth = jnp.concatenate([wg_q[1], cols], axis=1)
        return reduce_cols(own, oth)

    tables = [rope_tables(places, base) for base in BASES]
    windows = (WIN, seq_length)

    gather0 = Gather(layer_cols[0], layer_rows[0])
    gather0.along_z()
    cols1, rows1, *gather0.parts = tie(layer_cols[1], layer_rows[1], *gather0.parts)
    cols1 = lax.all_gather(cols1, GRID, axis=0)
    rows1 = lax.all_gather(rows1, GRID, axis=0)
    gather0.plane(0)
    gather0.plane(1)
    pairs0 = gather0.pairs()
    query0 = query_side(pairs0[0])
    kept0 = forward_keys(query0, x0, *tables[0], first)
    mixed = forward_attend(kept0, places, all_places, windows[0])
    feed0 = feed_side(*pairs0[1:], query0[2])
    y0 = forward_rest(feed0, kept0, mixed, first).astype(BF)
    cols1 = (cols1, exchange(cols1, "section", 1))
    rows1 = (rows1, exchange(rows1, "section", 1))
    query1 = query_side([v[..., :QP] for v in cols1])
    kept1 = forward_keys(query1, y0.astype(F32), *tables[1], first)
    mixed = forward_attend(kept1, places, all_places, windows[1])
    feed1 = feed_side([v[..., QP:] for v in cols1], rows1, query1[2])
    y1 = forward_rest(feed1, kept1, mixed, first)

    middle1, branch1, wg_g, wg_out, wg_down, norm_grads = backward_feed(
        feed1, kept1, cotangent, first
    )
    sum_g1 = reduce_cols(*wg_g)
    sum_b1 = reduce_rows(wg_out, wg_down)
    red_b1 = lax.psum_scatter(sum_b1, GRID, scatter_dimension=0).astype(F32)
    scores1, kv_blocks = backward_attend(feed1[2], kept1, branch1, places, all_places, windows[1])
    scores1, kv_blocks, sum_g1 = tie(scores1, kv_blocks, sum_g1)
    grad_kv = key_return(kv_blocks)
    grad_q = backward_queries(kept1, scores1)
    grad1, wg_q, gain_zero, head_grads = backward_keys(
        query1, kept1, middle1, grad_q, grad_kv, *tables[1], first
    )
    sum_q1 = reduce_query(wg_q, [gain_zero] + norm_grads, head_grads)
    sum_c1 = jnp.concatenate([sum_q1, sum_g1], axis=-1)
    red_c1 = lax.psum_scatter(sum_c1, GRID, scatter_dimension=0).astype(F32)
    grad1 = grad1.astype(BF)

    middle0, branch0, wg_g, wg_out, wg_down, norm_grads = backward_feed(
        feed0, kept0, grad1.astype(F32), first
    )
    scat_g0 = Scatter(reduce_cols(*wg_g), True)
    scat_b0 = Scatter(reduce_rows(wg_out, wg_down), False)
    scores0, kv_blocks = backward_attend(feed0[2], kept0, branch0, places, all_places, windows[0])
    scores0, kv_blocks, *held = tie(scores0, kv_blocks, *scat_g0.values(), *scat_b0.values())
    scat_g0.after(*held)
    scat_b0.after(*held)
    grad_kv = key_return(kv_blocks)
    scat_g0.plane(0)
    scat_b0.plane(0)
    grad_q = backward_queries(kept0, scores0)
    grad0, wg_q, gain_zero, head_grads = backward_keys(
        query0, kept0, middle0, grad_q, grad_kv, *tables[0], first
    )
    wg_q0, wg_q1, *held = tie(wg_q[0], wg_q[1], *scat_g0.values(), *scat_b0.values())
    scat_g0.after(*held)
    scat_b0.after(*held)
    scat_q0 = Scatter(reduce_query((wg_q0, wg_q1), [gain_zero] + norm_grads, head_grads), False)
    scat_g0.plane(1)
    scat_b0.plane(1)
    scat_q0.plane(0)
    scat_q0.plane(1)
    red_g0, red_b0 = scat_g0.along_z(), scat_b0.along_z()
    red_q0 = scat_q0.along_z()
    red_c0 = jnp.concatenate([red_q0, red_g0], axis=1)

    out_moved = exchange(jnp.where(first, y1, grad0), "section", 1)
    c_keep, c_send = pick(first, red_c0, red_c1)
    b_keep, b_send = pick(first, red_b0, red_b1)
    c_lo, c_hi = pick(first, c_keep, exchange(c_send, "section", 1))
    b_lo, b_hi = pick(first, b_keep, exchange(b_send, "section", 1))
    boundary_out = jnp.where(
        first, jnp.stack([grad0, out_moved]), jnp.stack([out_moved, y1])
    )[None, :, None]
    return (
        boundary_out,
        jnp.concatenate([c_lo[:, :QH], c_hi[:, :QH]], axis=1)[None],
        jnp.concatenate([c_lo[:, QH:QW], c_hi[:, QH:QW]], axis=1)[None],
        jnp.concatenate([b_lo[: ro // 2], b_hi[: ro // 2]], axis=0)[None],
        jnp.concatenate([c_lo[:, QP:], c_hi[:, QP:]], axis=1)[None],
        jnp.concatenate([b_lo[ro // 2 :], b_hi[ro // 2 :]], axis=0)[None],
        c_lo[:, QW : QW + 4].T[None],
        c_lo[:hr, QW + 4 : QW + 6].T[None],
    )


def solution(mesh):
    in_specs = (
        P("section", None, "fsdp", "ctx", None),
        P(None, "fsdp", None),
        P("section", ("fsdp", "ctx"), None),
        P("section", ("fsdp", "ctx"), None),
        P("section", ("fsdp", "ctx"), None),
        P("section", ("fsdp", "ctx"), None),
        P("section", ("fsdp", "ctx"), None),
        P("section", None, ("fsdp", "ctx")),
        P("section", None, ("fsdp", "ctx")),
    )
    out_specs = (
        P("section", None, "fsdp", "ctx", None),
        P("section", ("fsdp", "ctx"), None),
        P("section", ("fsdp", "ctx"), None),
        P("section", ("fsdp", "ctx"), None),
        P("section", ("fsdp", "ctx"), None),
        P("section", ("fsdp", "ctx"), None),
        P("section", None, ("fsdp", "ctx")),
        P("section", None, ("fsdp", "ctx")),
    )
    return jax.shard_map(local, mesh=mesh, in_specs=in_specs, out_specs=out_specs, check_vma=False)
```

```python
import functools
import math

import jax
import jax.numpy as jnp
from jax import lax
from jax.experimental import pallas as pl
from jax.experimental.pallas import tpu as pltpu
from jax.sharding import PartitionSpec as P

D = 640
FF = 2048
HEADS = 4
HD = 256
WIN = 512
MB = 2
QH = 2 * HD
QW = QH + HD
QP = QW + 128

EPS = 1e-06
BASES = (math.log(10000.0), math.log(1000000.0))
SCALE = 1.0 / math.sqrt(HD)
BF = jnp.bfloat16
GRID = ("fsdp", "ctx")
F32 = jnp.float32


def bits_of(axis):
    return (lax.axis_size(axis) - 1).bit_length()


def exchange(shard, axis, flip):
    pairs = [(i, i ^ flip) for i in range(lax.axis_size(axis))]
    return lax.ppermute(shard, axis, pairs)


def my_bit(axis, bit):
    return (lax.axis_index(axis) >> bit) & 1


def tie(*values):
    return lax.optimization_barrier(values)


def ctx_steps(order):
    count = bits_of("ctx")
    steps = [(bit, count - bit) for bit in range(count)]
    return steps if order == "xy" else steps[::-1]


def z_gather(block):
    count = lax.axis_size("fsdp")
    pairs = [(i, (i + 1) % count) for i in range(count)]
    pieces = [block]
    for _ in range(count - 1):
        pieces.append(lax.ppermute(pieces[-1], "fsdp", pairs))
    me = lax.axis_index("fsdp")
    return jnp.stack([lax.select_n((me - at) % count, *pieces) for at in range(count)])


def ctx_open(buf):
    return buf.reshape((buf.shape[0],) + (1,) * bits_of("ctx") + buf.shape[1:])


def ctx_gather(buf, steps):
    for bit, dim in steps:
        recv = exchange(buf, "ctx", 1 << bit)
        low = my_bit("ctx", bit) == 0
        buf = jnp.concatenate([jnp.where(low, buf, recv), jnp.where(low, recv, buf)], axis=dim)
    return buf


def ctx_close(buf, tail):
    return buf.reshape((-1,) + tail)


def ctx_scatter(buf, steps):
    for bit, dim in steps:
        mine = my_bit("ctx", bit)
        send = lax.dynamic_index_in_dim(buf, 1 - mine, dim, keepdims=True)
        keep = lax.dynamic_index_in_dim(buf, mine, dim, keepdims=True)
        recv = exchange(send, "ctx", 1 << bit)
        buf = (keep.astype(F32) + recv.astype(F32)).astype(BF)
    return buf


def z_scatter(buf):
    me = lax.axis_index("fsdp")
    total = lax.dynamic_index_in_dim(buf, me, 0, False).astype(F32)
    for j in range(1, lax.axis_size("fsdp")):
        part = lax.dynamic_index_in_dim(buf, me ^ j, 0, False)
        total = total + exchange(part, "fsdp", j).astype(F32)
    return total


class Gather:
    ORDERS = ("yx", "xy", "yx", "xy")

    def __init__(self, cols, rows):
        self.q, self.g, self.b = cols[:, :QP], cols[:, QP:], rows

    def after(self, *others):
        self.q, self.g, self.b = tie(self.q, self.g, self.b, *others)[:3]

    def along_z(self):
        q, g, b = z_gather(self.q), z_gather(self.g), z_gather(self.b)
        half = g.shape[0] // 2
        self.parts = [ctx_open(v) for v in (q, g[:half], g[half:], b)]

    def parts_after(self, *others):
        self.parts = list(tie(*self.parts, *others)[:4])

    def plane(self, stage):
        done = []
        for v, order in zip(self.parts, self.ORDERS):
            steps = ctx_steps(order)
            done.append(ctx_gather(v, steps[:1] if stage == 0 else steps[1:]))
        self.parts = done

    def pairs(self):
        q, g1, g2, b = self.parts
        q = ctx_close(q, self.q.shape)
        b = ctx_close(b, self.b.shape)
        g = jnp.concatenate([ctx_close(g1, self.g.shape), ctx_close(g2, self.g.shape)], axis=0)
        return [(v, exchange(v, "section", 1)) for v in (q, g, b)]


class Scatter:
    def __init__(self, blocks, split):
        fs, cb = lax.axis_size("fsdp"), bits_of("ctx")
        self.tail = blocks.shape[1:]
        buf = blocks.reshape((fs,) + (2,) * cb + self.tail)
        self.parts = [(buf[: fs // 2], "xy"), (buf[fs // 2 :], "yx")] if split else [(buf, "xy")]

    def after(self, *others):
        values = tie(*[p[0] for p in self.parts], *others)
        self.parts = [(v, p[1]) for v, p in zip(values, self.parts)]

    def values(self):
        return [p[0] for p in self.parts]

    def plane(self, stage):
        done = []
        for v, order in self.parts:
            steps = ctx_steps(order)
            done.append((ctx_scatter(v, steps[:1] if stage == 0 else steps[1:]), order))
        self.parts = done

    def along_z(self):
        buf = jnp.concatenate([v.reshape((-1,) + self.tail) for v in self.values()], axis=0)
        return z_scatter(buf)


def rope_tables(places, log_base):
    half_width = HD // 2
    inverse = jnp.exp(-log_base * (jnp.arange(half_width, dtype=F32) * (2.0 / HD)))
    angles = places.astype(F32)[:, None] * inverse[None, :]
    return (jnp.cos(angles), jnp.sin(angles))


def dot(a, b):
    return jnp.dot(a, b, preferred_element_type=F32)


def dot_t(a, b):
    return jnp.einsum("tc,dc->td", a, b, preferred_element_type=F32)


def t_dot(a, b):
    return jnp.einsum("ta,tb->ab", a, b, preferred_element_type=F32)


def pick(first, own, other):
    return jnp.where(first, own, other), jnp.where(first, other, own)


def key_exchange(keys_values):
    count = lax.axis_size("ctx")
    return [keys_values] + [exchange(keys_values, "ctx", j) for j in range(1, count)]


def key_return(blocks):
    count = lax.axis_size("ctx")
    blocks = jnp.split(blocks, count, axis=0)
    total = blocks[0]
    for j in range(1, count):
        total = total + exchange(blocks[j].astype(BF), "ctx", j).astype(F32)
    return total


def whole_call(body, outs, args, flops, window=None):
    vmem = pl.BlockSpec(memory_space=pltpu.VMEM)
    moved = sum(math.prod(v.shape) * v.dtype.itemsize for v in args)
    moved += sum(math.prod(s) * jnp.dtype(t).itemsize for s, t in outs)
    return pl.pallas_call(
        body,
        out_shape=[jax.ShapeDtypeStruct(s, t) for s, t in outs],
        in_specs=[pl.BlockSpec(memory_space=pltpu.SMEM)] + [vmem] * (len(args) - 1),
        out_specs=[vmem] * len(outs),
        compiler_params=pltpu.CompilerParams(vmem_limit_bytes=52 * 2**20),
        cost_estimate=pl.CostEstimate(
            flops=int(flops), bytes_accessed=int(moved), transcendentals=0
        ),
    )(*args)


def inverse_rms(u):
    return lax.rsqrt(jnp.mean(u * u, axis=-1, keepdims=True) + EPS)


def rms_back(u, gain, dz):
    r = inverse_rms(u)
    scaled = dz * gain
    mean = jnp.mean(u * scaled, axis=-1, keepdims=True)
    du = r * (scaled - u * (r * r * mean))
    return du, jnp.sum(dz * u * r, axis=0, keepdims=True)


def last_dot(a, b):
    return lax.dot_general(a, b, (((1,), (1,)), ((), ())), preferred_element_type=F32)


def first_dot(a, b):
    return lax.dot_general(a, b, (((0,), (0,)), ((), ())), preferred_element_type=F32)


def chosen(flag, own, other):
    return jnp.where(flag, own, other), jnp.where(flag, other, own)


def keys_body(flag, x, q_own, q_oth, gains, heads, cosine, sine, normed, qp, kp, q, kv):
    first = flag[0] == 0
    u = x[...]
    h = (u * inverse_rms(u) * gains[0:1, :]).astype(BF)
    normed[...] = h
    lo, hi = chosen(first, dot(h, q_own[:, :QW]), dot(h, q_oth[:, :QW]))
    cos, sin = cosine[...], sine[...]
    half = HD // 2

    def turned(v, gain, out, at):
        n = v * inverse_rms(v) * gain
        a, b = n[:, :half], n[:, half:]
        out[:, at : at + half] = (a * cos - b * sin).astype(BF)
        out[:, at + half : at + HD] = (b * cos + a * sin).astype(BF)

    for head in range(HEADS):
        part = (lo if head < 2 else hi)[:, (head % 2) * HD : (head % 2 + 1) * HD]
        qp[:, head * HD : (head + 1) * HD] = part
        turned(part, heads[0:1, :], q, head * HD)
    k_part = lo[:, QH:]
    kp[...] = k_part
    turned(k_part, heads[1:2, :], kv, 0)
    kv[:, HD:] = hi[:, QH:].astype(BF)


def forward_keys(full, x, cosine, sine_table, flag):
    q_own, q_oth, gains, heads = full
    t = x.shape[0]
    normed, qp, kp, q, kv = whole_call(
        keys_body,
        [((t, D), BF), ((t, HEADS * HD), F32), ((t, HD), F32), ((t, HEADS * HD), BF), ((t, 2 * HD), BF)],
        (flag, x, q_own, q_oth, gains, heads, cosine, sine_table),
        2 * t * D * 2 * QW,
    )
    all_kv = jnp.concatenate(key_exchange(kv), axis=0)
    return dict(x=x, normed=normed, qp=qp, kp=kp, q=q, kv=all_kv)


CHUNK = 512
GELU_A = math.sqrt(2.0 / math.pi)
GELU_B = 0.044715


def rest_body(
    window, flag, x, q, kv, pos_q, pos_k, w_out, g_own, g_oth, w_down, gains,
    mixed, branch, middle, normed, gate_out, up_out, hidden, down, result,
):
    first = flag[0] == 0
    reach = pos_q[...] - pos_k[...]
    allowed = (reach >= 0) & (reach < window)
    k, v = kv[:, :HD], kv[:, HD:]
    for head in range(HEADS):
        cols = slice(head * HD, (head + 1) * HD)
        s = jnp.where(allowed, last_dot(q[:, cols], k) * SCALE, -1e30)
        e = jnp.exp(s - jnp.max(s, axis=-1, keepdims=True))
        total = jnp.sum(e, axis=-1, keepdims=True)
        mixed[:, cols] = (dot(e.astype(BF), v) * (1.0 / total)).astype(BF)
    b = dot(mixed[...], w_out[...])
    branch[...] = b
    m = x[...] + b * inverse_rms(b) * gains[1:2, :]
    middle[...] = m
    h = (m * inverse_rms(m) * gains[2:3, :]).astype(BF)
    normed[...] = h
    total = jnp.zeros(m.shape, F32)
    for at in range(0, FF, CHUNK):
        cols = slice(at, at + CHUNK)
        gate, up = chosen(first, dot(h, g_own[:, cols]), dot(h, g_oth[:, cols]))
        gate_out[:, cols] = gate
        up_out[:, cols] = up
        th = jnp.tanh(GELU_A * (gate + GELU_B * gate * gate * gate))
        hid = (0.5 * gate * (1.0 + th) * up).astype(BF)
        hidden[:, cols] = hid
        total = total + dot(hid, w_down[cols, :])
    down[...] = total
    result[...] = m + total * inverse_rms(total) * gains[3:4, :]


def forward_rest(full, kept, pos, window, flag):
    g_own, g_oth, w_out, w_down, gains = full
    t = kept["x"].shape[0]
    keys = kept["kv"].shape[0]
    names = ("mixed", "branch", "middle", "normed_two", "gate", "up", "hidden", "down", "result")
    outs = whole_call(
        functools.partial(rest_body, window),
        [
            ((t, HEADS * HD), BF), ((t, D), F32), ((t, D), F32), ((t, D), BF), ((t, FF), F32),
            ((t, FF), F32), ((t, FF), BF), ((t, D), F32), ((t, D), F32),
        ],
        (
            flag, kept["x"], kept["q"], kept["kv"], pos[0][:, None], pos[1][None, :], w_out,
            g_own, g_oth, w_down, gains,
        ),
        2 * t * HEADS * HD * (2 * keys + D) + 6 * t * D * FF,
    )
    kept.update(zip(names, outs))
    return kept["result"]


def feed_body(
    flag, dy, down, gate, up, middle, branch, gains, w_down, g_own, g_oth,
    grad_middle, grad_down, gu_own, gu_oth, grad_branch, gain_grads,
):
    first = flag[0] == 0
    dz = dy[...].astype(F32)
    df, gain_three = rms_back(down[...], gains[3:4, :], dz)
    df = df.astype(BF)
    grad_down[...] = df
    total = jnp.zeros(dz.shape, F32)
    for at in range(0, FF, CHUNK):
        cols = slice(at, at + CHUNK)
        dm = last_dot(df, w_down[cols, :])
        u = gate[:, cols]
        th = jnp.tanh(GELU_A * (u + GELU_B * u * u * u))
        plus = 0.5 * (1.0 + th)
        slope = plus + 0.5 * u * (1.0 - th * th) * (GELU_A * (1.0 + 3.0 * GELU_B * u * u))
        d_gate = (dm * up[:, cols] * slope).astype(BF)
        d_up = (dm * (u * plus)).astype(BF)
        own, oth = chosen(first, d_gate, d_up)
        gu_own[:, cols] = own
        gu_oth[:, cols] = oth
        total = total + last_dot(own, g_own[:, cols]) + last_dot(oth, g_oth[:, cols])
    part, gain_two = rms_back(middle[...], gains[2:3, :], total)
    dx = dz + part
    grad_middle[...] = dx
    da, gain_one = rms_back(branch[...], gains[1:2, :], dx)
    grad_branch[...] = da.astype(BF)
    gain_grads[...] = jnp.concatenate([gain_one, gain_two, gain_three], axis=0)


def backward_feed(full, kept, grad_result, flag):
    g_own, g_oth, w_out, w_down, gains = full
    t = kept["x"].shape[0]
    middle, down_low, gu_own, gu_oth, branch_low, gain_grads = whole_call(
        feed_body,
        [((t, D), F32), ((t, D), BF), ((t, FF), BF), ((t, FF), BF), ((t, D), BF), ((3, D), F32)],
        (
            flag, grad_result, kept["down"], kept["gate"], kept["up"], kept["middle"],
            kept["branch"], gains, w_down, g_own, g_oth,
        ),
        6 * t * D * FF,
    )
    wg_g = (t_dot(kept["normed_two"], gu_own), t_dot(kept["normed_two"], gu_oth).astype(BF))
    wg_out = t_dot(kept["mixed"], branch_low).astype(BF)
    wg_down = t_dot(kept["hidden"], down_low).astype(BF)
    return middle, branch_low, wg_g, wg_out, wg_down, gain_grads


def attend_body(window, flag, da, w_out, q, kv, pos_q, pos_k, grad_q, grad_kv):
    reach = pos_q[...] - pos_k[...]
    allowed = (reach >= 0) & (reach < window)
    k, v = kv[:, :HD], kv[:, HD:]
    for head in range(HEADS):
        cols = slice(head * HD, (head + 1) * HD)
        do = last_dot(da[...], w_out[cols, :]).astype(BF)
        s = jnp.where(allowed, last_dot(k, q[:, cols]) * SCALE, -1e30)
        e = jnp.exp(s - jnp.max(s, axis=0, keepdims=True))
        p = e * (1.0 / jnp.sum(e, axis=0, keepdims=True))
        dp = last_dot(v, do)
        inner = jnp.sum(p * dp, axis=0, keepdims=True)
        ds = (p * (dp - inner)).astype(BF)
        grad_q[:, cols] = first_dot(ds, k) * SCALE
        dk = dot(ds, q[:, cols]) * SCALE
        dv = dot(p.astype(BF), do)
        if head == 0:
            total_k, total_v = dk, dv
        else:
            total_k, total_v = total_k + dk, total_v + dv
    grad_kv[:, :HD] = total_k.astype(BF)
    grad_kv[:, HD:] = total_v.astype(BF)


def backward_attend(w_out, kept, branch_low, pos, window, flag):
    t, keys = kept["x"].shape[0], kept["kv"].shape[0]
    return whole_call(
        functools.partial(attend_body, window),
        [((t, HEADS * HD), F32), ((keys, 2 * HD), BF)],
        (flag, branch_low, w_out, kept["q"], kept["kv"], pos[0][None, :], pos[1][:, None]),
        2 * t * HEADS * HD * (5 * keys + D),
    )


def back_body(
    flag, grad_q, grad_kv, qp, kp, heads, cosine, sine, x, dx, q_own, q_oth, gains,
    grad_x, gq_own, gq_oth, gain_zero, head_grads,
):
    first = flag[0] == 0
    cos, sin = cosine[...], sine[...]
    half = HD // 2

    def turned_back(d, u, gain):
        a, b = d[:, :half], d[:, half:]
        n = jnp.concatenate([a * cos + b * sin, b * cos - a * sin], axis=1)
        return rms_back(u, gain, n)

    parts = []
    query_gain = jnp.zeros((1, HD), F32)
    for head in range(HEADS):
        cols = slice(head * HD, (head + 1) * HD)
        du, dg = turned_back(grad_q[:, cols], qp[:, cols], heads[0:1, :])
        parts.append(du.astype(BF))
        query_gain = query_gain + dg
    dk, key_gain = turned_back(grad_kv[:, :HD], kp[...], heads[1:2, :])
    lo = jnp.concatenate(parts[:2] + [dk.astype(BF)], axis=1)
    hi = jnp.concatenate(parts[2:] + [grad_kv[:, HD:].astype(BF)], axis=1)
    own, oth = chosen(first, lo, hi)
    gq_own[...] = own
    gq_oth[...] = oth
    dz = last_dot(own, q_own[:, :QW]) + last_dot(oth, q_oth[:, :QW])
    part, gain = rms_back(x[...], gains[0:1, :], dz)
    grad_x[...] = dx[...] + part
    gain_zero[...] = gain
    head_grads[...] = jnp.concatenate([query_gain, key_gain], axis=0)


def backward_keys(full, kept, middle, grad_q, grad_kv, cosine, sine_table, flag):
    q_own, q_oth, gains, heads = full
    t = kept["x"].shape[0]
    grad_x, gq_own, gq_oth, gain_zero, head_grads = whole_call(
        back_body,
        [((t, D), F32), ((t, QW), BF), ((t, QW), BF), ((1, D), F32), ((2, HD), F32)],
        (
            flag, grad_q, grad_kv, kept["qp"], kept["kp"], heads, cosine, sine_table, kept["x"],
            middle, q_own, q_oth, gains,
        ),
        4 * t * D * QW,
    )
    wg_q = (t_dot(kept["normed"], gq_own).astype(BF), t_dot(kept["normed"], gq_oth).astype(BF))
    return grad_x, wg_q, gain_zero, head_grads


def halves(grad, count):
    return grad.reshape(count, 2, -1, grad.shape[-1])


def local(
    boundary, positions, w_query, w_key_value, w_out, w_gate_up, w_down, norm_gains, head_gains
):
    section = lax.axis_index("section")
    first = section == 0
    ctx_index = lax.axis_index("ctx")
    tokens = boundary.shape[3]
    seq_length = positions.shape[-1]
    nr = w_query.shape[1]
    hr = head_gains.shape[2]
    ro, rd = w_out.shape[1], w_down.shape[1]
    blocks = lax.axis_size("fsdp") * lax.axis_size("ctx")

    moved = exchange(lax.dynamic_index_in_dim(boundary[0, :, 0], 1 - section, 0, False), "section", 1)
    kept_in = lax.dynamic_index_in_dim(boundary[0, :, 0], section, 0, False)
    x0, cotangent = pick(first, kept_in, moved)
    x0 = x0.astype(F32)
    seq_places = lax.dynamic_index_in_dim(positions[:, 0], section, 0, False)
    near = [
        lax.dynamic_slice_in_dim(seq_places, (ctx_index ^ j) * tokens, tokens)
        for j in range(lax.axis_size("ctx"))
    ]
    pos = (near[0], jnp.concatenate(near))
    flag = section.astype(jnp.int32).reshape(1)

    gain_cols = jnp.concatenate(
        [
            norm_gains[0].T,
            jnp.pad(head_gains[0].T, ((0, nr - hr), (0, 0))),
            jnp.zeros((nr, 128 - 6), BF),
        ],
        axis=1,
    )
    cols = [
        jnp.concatenate(
            [
                w_query[0, :, h * QH : (h + 1) * QH],
                w_key_value[0, :, h * HD : (h + 1) * HD],
                gain_cols,
                w_gate_up[0, :, h * FF : (h + 1) * FF],
            ],
            axis=1,
        )
        for h in range(2)
    ]
    rows = [
        jnp.concatenate(
            [
                w_out[0, h * ro // 2 : (h + 1) * ro // 2],
                w_down[0, h * rd // 2 : (h + 1) * rd // 2],
            ],
            axis=0,
        )
        for h in range(2)
    ]
    col_keep, col_send = pick(first, cols[0], cols[1])
    row_keep, row_send = pick(first, rows[0], rows[1])
    col_recv = exchange(col_send, "section", 1)
    row_recv = exchange(row_send, "section", 1)
    layer_cols = pick(first, col_keep, col_recv)
    layer_rows = pick(first, row_keep, row_recv)

    def query_side(pair):
        q_own, q_oth = [v.reshape(blocks * nr, -1) for v in pair]
        gain_part = q_own[:, QW:].astype(F32)
        gains = gain_part[:, :4].T
        heads = gain_part[:, 4:6].reshape(blocks, nr, 2)[:, :hr].reshape(blocks * hr, 2).T
        return q_own, q_oth, gains, heads

    def feed_side(g_pair, b_pair, gains):
        g_own, g_oth = [v.reshape(blocks * nr, -1) for v in g_pair]
        b_lo, b_hi = pick(first, *b_pair)
        full_out = jnp.concatenate([b_lo[:, : ro // 2], b_hi[:, : ro // 2]], axis=1)
        full_down = jnp.concatenate([b_lo[:, ro // 2 :], b_hi[:, ro // 2 :]], axis=1)
        return g_own, g_oth, full_out.reshape(-1, D), full_down.reshape(-1, D), gains

    def reduce_cols(own, other):
        summed = own.astype(F32) + exchange(other, "section", 1).astype(F32)
        return summed.astype(BF).reshape(blocks, nr, -1)

    def reduce_rows(wg_out, wg_down):
        out_half, down_half = halves(wg_out, blocks), halves(wg_down, blocks)

        def part(index):
            return jnp.concatenate(
                [
                    lax.dynamic_index_in_dim(out_half, index, 1, False),
                    lax.dynamic_index_in_dim(down_half, index, 1, False),
                ],
                axis=1,
            )

        recv = exchange(part(1 - section), "section", 1)
        return (part(section).astype(F32) + recv.astype(F32)).astype(BF)

    def reduce_query(wg_q, norm_grads, head_grads):
        norm_part = jnp.concatenate(norm_grads, axis=0).T
        head_part = head_grads.T.reshape(blocks, hr, 2)
        head_part = jnp.pad(head_part, ((0, 0), (0, nr - hr), (0, 0))).reshape(blocks * nr, 2)
        fill = jnp.zeros((blocks * nr, 128 - 6), F32)
        cols = jnp.concatenate([norm_part, head_part, fill], axis=1).astype(BF)
        own = jnp.concatenate([wg_q[0], cols], axis=1)
        oth = jnp.concatenate([wg_q[1], cols], axis=1)
        return reduce_cols(own, oth)

    tables = [rope_tables(pos[0], base) for base in BASES]
    windows = (WIN, seq_length)

    gather0 = Gather(layer_cols[0], layer_rows[0])
    gather0.along_z()
    cols1, rows1 = tie(layer_cols[1], layer_rows[1], *gather0.parts)[:2]
    cols1 = lax.all_gather(cols1, GRID, axis=0)
    rows1 = lax.all_gather(rows1, GRID, axis=0)
    gather0.plane(0)
    gather0.plane(1)
    pairs0 = gather0.pairs()
    query0 = query_side(pairs0[0])
    kept0 = forward_keys(query0, x0, *tables[0], flag)
    feed0 = feed_side(*pairs0[1:], query0[2])
    y0 = forward_rest(feed0, kept0, pos, windows[0], flag).astype(BF)
    cols1 = (cols1, exchange(cols1, "section", 1))
    rows1 = (rows1, exchange(rows1, "section", 1))
    query1 = query_side([v[..., :QP] for v in cols1])
    kept1 = forward_keys(query1, y0.astype(F32), *tables[1], flag)
    feed1 = feed_side([v[..., QP:] for v in cols1], rows1, query1[2])
    y1 = forward_rest(feed1, kept1, pos, windows[1], flag)

    middle1, branch1, wg_g, wg_out, wg_down, norm_grads = backward_feed(
        feed1, kept1, cotangent, flag
    )
    sum_g1 = reduce_cols(*wg_g)
    sum_b1 = reduce_rows(wg_out, wg_down)
    red_b1 = lax.psum_scatter(sum_b1, GRID, scatter_dimension=0).astype(F32)
    grad_q1, kv_blocks = backward_attend(feed1[2], kept1, branch1, pos, windows[1], flag)
    grad_q1, kv_blocks, sum_g1 = tie(grad_q1, kv_blocks, sum_g1)
    grad_kv = key_return(kv_blocks)
    grad1, wg_q, gain_zero, head_grads = backward_keys(
        query1, kept1, middle1, grad_q1, grad_kv, *tables[1], flag
    )
    sum_q1 = reduce_query(wg_q, [gain_zero, norm_grads], head_grads)
    sum_c1 = jnp.concatenate([sum_q1, sum_g1], axis=-1)
    red_c1 = lax.psum_scatter(sum_c1, GRID, scatter_dimension=0).astype(F32)
    grad1 = grad1.astype(BF)

    middle0, branch0, wg_g, wg_out, wg_down, norm_grads = backward_feed(
        feed0, kept0, grad1, flag
    )
    scat_g0 = Scatter(reduce_cols(*wg_g), True)
    scat_b0 = Scatter(reduce_rows(wg_out, wg_down), False)
    grad_q0, kv_blocks = backward_attend(feed0[2], kept0, branch0, pos, windows[0], flag)
    grad_q0, kv_blocks, *held = tie(grad_q0, kv_blocks, *scat_g0.values(), *scat_b0.values())
    scat_g0.after(*held)
    scat_b0.after(*held)
    grad_kv = key_return(kv_blocks)
    scat_g0.plane(0)
    scat_b0.plane(0)
    grad0, wg_q, gain_zero, head_grads = backward_keys(
        query0, kept0, middle0, grad_q0, grad_kv, *tables[0], flag
    )
    wg_q0, wg_q1, *held = tie(wg_q[0], wg_q[1], *scat_g0.values(), *scat_b0.values())
    scat_g0.after(*held)
    scat_b0.after(*held)
    scat_q0 = Scatter(reduce_query((wg_q0, wg_q1), [gain_zero, norm_grads], head_grads), False)
    scat_g0.plane(1)
    scat_b0.plane(1)
    scat_q0.plane(0)
    scat_q0.plane(1)
    red_g0, red_b0 = scat_g0.along_z(), scat_b0.along_z()
    red_q0 = scat_q0.along_z()
    red_c0 = jnp.concatenate([red_q0, red_g0], axis=1)

    out_moved = exchange(jnp.where(first, y1, grad0), "section", 1)
    c_keep, c_send = pick(first, red_c0, red_c1)
    b_keep, b_send = pick(first, red_b0, red_b1)
    c_lo, c_hi = pick(first, c_keep, exchange(c_send, "section", 1))
    b_lo, b_hi = pick(first, b_keep, exchange(b_send, "section", 1))
    boundary_out = jnp.where(
        first, jnp.stack([grad0, out_moved]), jnp.stack([out_moved, y1])
    )[None, :, None]
    return (
        boundary_out,
        jnp.concatenate([c_lo[:, :QH], c_hi[:, :QH]], axis=1)[None],
        jnp.concatenate([c_lo[:, QH:QW], c_hi[:, QH:QW]], axis=1)[None],
        jnp.concatenate([b_lo[: ro // 2], b_hi[: ro // 2]], axis=0)[None],
        jnp.concatenate([c_lo[:, QP:], c_hi[:, QP:]], axis=1)[None],
        jnp.concatenate([b_lo[ro // 2 :], b_hi[ro // 2 :]], axis=0)[None],
        c_lo[:, QW : QW + 4].T[None],
        c_lo[:hr, QW + 4 : QW + 6].T[None],
    )


def solution(mesh):
    in_specs = (
        P("section", None, "fsdp", "ctx", None),
        P(None, "fsdp", None),
        P("section", ("fsdp", "ctx"), None),
        P("section", ("fsdp", "ctx"), None),
        P("section", ("fsdp", "ctx"), None),
        P("section", ("fsdp", "ctx"), None),
        P("section", ("fsdp", "ctx"), None),
        P("section", None, ("fsdp", "ctx")),
        P("section", None, ("fsdp", "ctx")),
    )
    out_specs = (
        P("section", None, "fsdp", "ctx", None),
        P("section", ("fsdp", "ctx"), None),
        P("section", ("fsdp", "ctx"), None),
        P("section", ("fsdp", "ctx"), None),
        P("section", ("fsdp", "ctx"), None),
        P("section", ("fsdp", "ctx"), None),
        P("section", None, ("fsdp", "ctx")),
        P("section", None, ("fsdp", "ctx")),
    )
    return jax.shard_map(local, mesh=mesh, in_specs=in_specs, out_specs=out_specs, check_vma=False)
```

```python
import functools
import math

import jax
import jax.numpy as jnp
from jax import lax
from jax.experimental import pallas as pl
from jax.experimental.pallas import tpu as pltpu
from jax.sharding import PartitionSpec as P

D = 640
FF = 2048
HEADS = 4
HD = 256
WIN = 512
MB = 2
QH = 2 * HD
QW = QH + HD
QP = QW + 128

EPS = 1e-06
BASES = (math.log(10000.0), math.log(1000000.0))
SCALE = 1.0 / math.sqrt(HD)
BF = jnp.bfloat16
F32 = jnp.float32


def bits_of(axis):
    return (lax.axis_size(axis) - 1).bit_length()


def exchange(shard, axis, flip):
    pairs = [(i, i ^ flip) for i in range(lax.axis_size(axis))]
    return lax.ppermute(shard, axis, pairs)


def my_bit(axis, bit):
    return (lax.axis_index(axis) >> bit) & 1


def tie(*values):
    return lax.optimization_barrier(values)


def ctx_steps(order):
    count = bits_of("ctx")
    steps = [(bit, count - bit) for bit in range(count)]
    return steps if order == "xy" else steps[::-1]


def z_gather(block):
    count = lax.axis_size("fsdp")
    pairs = [(i, (i + 1) % count) for i in range(count)]
    pieces = [block]
    for _ in range(count - 1):
        pieces.append(lax.ppermute(pieces[-1], "fsdp", pairs))
    me = lax.axis_index("fsdp")
    return jnp.stack([lax.select_n((me - at) % count, *pieces) for at in range(count)])


def ctx_open(buf):
    return buf.reshape((buf.shape[0],) + (1,) * bits_of("ctx") + buf.shape[1:])


def ctx_gather(buf, steps):
    for bit, dim in steps:
        recv = exchange(buf, "ctx", 1 << bit)
        low = my_bit("ctx", bit) == 0
        buf = jnp.concatenate([jnp.where(low, buf, recv), jnp.where(low, recv, buf)], axis=dim)
    return buf


def ctx_close(buf, tail):
    return buf.reshape((-1,) + tail)


def ctx_scatter(buf, steps):
    for bit, dim in steps:
        mine = my_bit("ctx", bit)
        send = lax.dynamic_index_in_dim(buf, 1 - mine, dim, keepdims=True)
        keep = lax.dynamic_index_in_dim(buf, mine, dim, keepdims=True)
        recv = exchange(send, "ctx", 1 << bit)
        buf = (keep.astype(F32) + recv.astype(F32)).astype(BF)
    return buf


def z_scatter(buf):
    me = lax.axis_index("fsdp")
    total = lax.dynamic_index_in_dim(buf, me, 0, False).astype(F32)
    for j in range(1, lax.axis_size("fsdp")):
        part = lax.dynamic_index_in_dim(buf, me ^ j, 0, False)
        total = total + exchange(part, "fsdp", j).astype(F32)
    return total


def z_ring_scatter(buf):
    count = lax.axis_size("fsdp")
    pairs = [(i, (i + 1) % count) for i in range(count)]
    me = lax.axis_index("fsdp")

    def block(back):
        return lax.dynamic_index_in_dim(buf, (me - back) % count, 0, False)

    total = block(1)
    for step in range(count - 1):
        recv = lax.ppermute(total, "fsdp", pairs)
        total = (recv.astype(F32) + block(step + 2).astype(F32)).astype(BF)
    return total


class Gather:
    ORDERS = ("yx", "xy", "yx")

    def __init__(self, cols, rows):
        self.q, self.g, self.b = cols[:, :QP], cols[:, QP:], rows

    def begin(self):
        q, g = z_gather(self.q), z_gather(self.g)
        half = g.shape[0] // 2
        self.parts = [ctx_open(v) for v in (q, g[:half], g[half:])]
        self.rows = ctx_gather(ctx_open(self.b[None]), ctx_steps("xy"))

    def plane(self, stage):
        done = []
        for v, order in zip(self.parts, self.ORDERS):
            steps = ctx_steps(order)
            done.append(ctx_gather(v, steps[:1] if stage == 0 else steps[1:]))
        self.parts = done

    def rows_z(self):
        self.rows = z_gather(self.rows[0])

    def pairs(self):
        q, g1, g2 = self.parts
        q = ctx_close(q, self.q.shape)
        b = ctx_close(self.rows, self.b.shape)
        g = jnp.concatenate([ctx_close(g1, self.g.shape), ctx_close(g2, self.g.shape)], axis=0)
        return [(v, exchange(v, "section", 1)) for v in (q, g, b)]


class Scatter:
    def __init__(self, blocks, split):
        fs, cb = lax.axis_size("fsdp"), bits_of("ctx")
        self.tail = blocks.shape[1:]
        buf = blocks.reshape((fs,) + (2,) * cb + self.tail)
        self.parts = [(buf[: fs // 2], "xy"), (buf[fs // 2 :], "yx")] if split else [(buf, "xy")]

    def values(self):
        return [p[0] for p in self.parts]

    def put(self, values):
        self.parts = [(v, p[1]) for v, p in zip(values, self.parts)]

    def plane(self, stage):
        done = []
        for v, order in self.parts:
            steps = ctx_steps(order)
            done.append(ctx_scatter(v, steps[:1] if stage == 0 else steps[1:]))
        self.put(done)

    def along_z(self):
        buf = jnp.concatenate([v.reshape((-1,) + self.tail) for v in self.values()], axis=0)
        return z_scatter(buf)


def rows_z(blocks):
    fs, cb = lax.axis_size("fsdp"), bits_of("ctx")
    return z_ring_scatter(blocks.reshape((fs,) + (2,) * cb + blocks.shape[1:]))


def rows_plane(buf):
    return ctx_scatter(buf[None], ctx_steps("yx")).reshape(buf.shape[-2:]).astype(F32)


def rope_tables(places, log_base):
    half_width = HD // 2
    inverse = jnp.exp(-log_base * (jnp.arange(half_width, dtype=F32) * (2.0 / HD)))
    angles = places.astype(F32)[:, None] * inverse[None, :]
    return (jnp.cos(angles), jnp.sin(angles))


def dot(a, b):
    return jnp.dot(a, b, preferred_element_type=F32)


def dot_t(a, b):
    return jnp.einsum("tc,dc->td", a, b, preferred_element_type=F32)


def t_dot(a, b):
    return jnp.einsum("ta,tb->ab", a, b, preferred_element_type=F32)


def pick(first, own, other):
    return jnp.where(first, own, other), jnp.where(first, other, own)


def key_exchange(keys_values):
    count = lax.axis_size("ctx")
    return [keys_values] + [exchange(keys_values, "ctx", j) for j in range(1, count)]


def key_return(blocks):
    count = lax.axis_size("ctx")
    blocks = jnp.split(blocks, count, axis=0)
    total = blocks[0]
    for j in range(1, count):
        total = total + exchange(blocks[j].astype(BF), "ctx", j).astype(F32)
    return total


def whole_call(body, outs, args, flops, window=None):
    vmem = pl.BlockSpec(memory_space=pltpu.VMEM)
    moved = sum(math.prod(v.shape) * v.dtype.itemsize for v in args)
    moved += sum(math.prod(s) * jnp.dtype(t).itemsize for s, t in outs)
    return pl.pallas_call(
        body,
        out_shape=[jax.ShapeDtypeStruct(s, t) for s, t in outs],
        in_specs=[pl.BlockSpec(memory_space=pltpu.SMEM)] + [vmem] * (len(args) - 1),
        out_specs=[vmem] * len(outs),
        compiler_params=pltpu.CompilerParams(vmem_limit_bytes=52 * 2**20),
        cost_estimate=pl.CostEstimate(
            flops=int(flops), bytes_accessed=int(moved), transcendentals=0
        ),
    )(*args)


def inverse_rms(u):
    return lax.rsqrt(jnp.mean(u * u, axis=-1, keepdims=True) + EPS)


def rms_back(u, gain, dz):
    r = inverse_rms(u)
    scaled = dz * gain
    mean = jnp.mean(u * scaled, axis=-1, keepdims=True)
    du = r * (scaled - u * (r * r * mean))
    return du, jnp.sum(dz * u * r, axis=0, keepdims=True)


def last_dot(a, b):
    return lax.dot_general(a, b, (((1,), (1,)), ((), ())), preferred_element_type=F32)


def first_dot(a, b):
    return lax.dot_general(a, b, (((0,), (0,)), ((), ())), preferred_element_type=F32)


def chosen(flag, own, other):
    return jnp.where(flag, own, other), jnp.where(flag, other, own)


def keys_body(flag, x, q_own, q_oth, gains, heads, cosine, sine, normed, qp, kp, q, kv):
    first = flag[0] == 0
    u = x[...]
    h = (u * inverse_rms(u) * gains[0:1, :]).astype(BF)
    normed[...] = h
    lo, hi = chosen(first, dot(h, q_own[:, :QW]), dot(h, q_oth[:, :QW]))
    cos, sin = cosine[...], sine[...]
    half = HD // 2

    def turned(v, gain, out, at):
        n = v * inverse_rms(v) * gain
        a, b = n[:, :half], n[:, half:]
        out[:, at : at + half] = (a * cos - b * sin).astype(BF)
        out[:, at + half : at + HD] = (b * cos + a * sin).astype(BF)

    for head in range(HEADS):
        part = (lo if head < 2 else hi)[:, (head % 2) * HD : (head % 2 + 1) * HD]
        qp[:, head * HD : (head + 1) * HD] = part
        turned(part, heads[0:1, :], q, head * HD)
    k_part = lo[:, QH:]
    kp[...] = k_part
    turned(k_part, heads[1:2, :], kv, 0)
    kv[:, HD:] = hi[:, QH:].astype(BF)


def forward_keys(full, x, cosine, sine_table, flag):
    q_own, q_oth, gains, heads = full
    t = x.shape[0]
    normed, qp, kp, q, kv = whole_call(
        keys_body,
        [((t, D), BF), ((t, HEADS * HD), F32), ((t, HD), F32), ((t, HEADS * HD), BF), ((t, 2 * HD), BF)],
        (flag, x, q_own, q_oth, gains, heads, cosine, sine_table),
        2 * t * D * 2 * QW,
    )
    all_kv = jnp.concatenate(key_exchange(kv), axis=0)
    return dict(x=x, normed=normed, qp=qp, kp=kp, q=q, kv=all_kv)


CHUNK = 512
GELU_A = math.sqrt(2.0 / math.pi)
GELU_B = 0.044715


def mix_body(window, flag, q, kv, pos_q, pos_k, mixed):
    reach = pos_q[...] - pos_k[...]
    allowed = (reach >= 0) & (reach < window)
    k, v = kv[:, :HD], kv[:, HD:]
    for head in range(HEADS):
        cols = slice(head * HD, (head + 1) * HD)
        s = jnp.where(allowed, last_dot(q[:, cols], k) * SCALE, -1e30)
        e = jnp.exp(s - jnp.max(s, axis=-1, keepdims=True))
        total = jnp.sum(e, axis=-1, keepdims=True)
        mixed[:, cols] = (dot(e.astype(BF), v) * (1.0 / total)).astype(BF)


def forward_attend(kept, pos, window, flag):
    t, keys = kept["x"].shape[0], kept["kv"].shape[0]
    return whole_call(
        functools.partial(mix_body, window),
        [((t, HEADS * HD), BF)],
        (flag, kept["q"], kept["kv"], pos[0][:, None], pos[1][None, :]),
        4 * t * HEADS * HD * keys,
    )[0]


def rest_body(
    flag, x, mixed, w_out, g_own, g_oth, w_down, gains,
    branch, middle, normed, gate_out, up_out, hidden, down, result,
):
    first = flag[0] == 0
    b = dot(mixed[...], w_out[...])
    branch[...] = b
    m = x[...] + b * inverse_rms(b) * gains[1:2, :]
    middle[...] = m
    h = (m * inverse_rms(m) * gains[2:3, :]).astype(BF)
    normed[...] = h
    total = jnp.zeros(m.shape, F32)
    for at in range(0, FF, CHUNK):
        cols = slice(at, at + CHUNK)
        gate, up = chosen(first, dot(h, g_own[:, cols]), dot(h, g_oth[:, cols]))
        gate_out[:, cols] = gate
        up_out[:, cols] = up
        th = jnp.tanh(GELU_A * (gate + GELU_B * gate * gate * gate))
        hid = (0.5 * gate * (1.0 + th) * up).astype(BF)
        hidden[:, cols] = hid
        total = total + dot(hid, w_down[cols, :])
    down[...] = total
    result[...] = m + total * inverse_rms(total) * gains[3:4, :]


def forward_rest(full, kept, mixed, flag):
    g_own, g_oth, w_out, w_down, gains = full
    t = kept["x"].shape[0]
    kept["mixed"] = mixed
    names = ("branch", "middle", "normed_two", "gate", "up", "hidden", "down", "result")
    outs = whole_call(
        rest_body,
        [
            ((t, D), F32), ((t, D), F32), ((t, D), BF), ((t, FF), F32),
            ((t, FF), F32), ((t, FF), BF), ((t, D), F32), ((t, D), F32),
        ],
        (flag, kept["x"], mixed, w_out, g_own, g_oth, w_down, gains),
        2 * t * HEADS * HD * D + 6 * t * D * FF,
    )
    kept.update(zip(names, outs))
    return kept["result"]


def feed_body(
    flag, dy, down, gate, up, middle, branch, gains, w_down, g_own, g_oth,
    grad_middle, grad_down, gu_own, gu_oth, grad_branch, gain_grads,
):
    first = flag[0] == 0
    dz = dy[...].astype(F32)
    df, gain_three = rms_back(down[...], gains[3:4, :], dz)
    df = df.astype(BF)
    grad_down[...] = df
    total = jnp.zeros(dz.shape, F32)
    for at in range(0, FF, CHUNK):
        cols = slice(at, at + CHUNK)
        dm = last_dot(df, w_down[cols, :])
        u = gate[:, cols]
        th = jnp.tanh(GELU_A * (u + GELU_B * u * u * u))
        plus = 0.5 * (1.0 + th)
        slope = plus + 0.5 * u * (1.0 - th * th) * (GELU_A * (1.0 + 3.0 * GELU_B * u * u))
        d_gate = (dm * up[:, cols] * slope).astype(BF)
        d_up = (dm * (u * plus)).astype(BF)
        own, oth = chosen(first, d_gate, d_up)
        gu_own[:, cols] = own
        gu_oth[:, cols] = oth
        total = total + last_dot(own, g_own[:, cols]) + last_dot(oth, g_oth[:, cols])
    part, gain_two = rms_back(middle[...], gains[2:3, :], total)
    dx = dz + part
    grad_middle[...] = dx
    da, gain_one = rms_back(branch[...], gains[1:2, :], dx)
    grad_branch[...] = da.astype(BF)
    gain_grads[...] = jnp.concatenate([gain_one, gain_two, gain_three], axis=0)


def backward_feed(full, kept, grad_result, flag):
    g_own, g_oth, w_out, w_down, gains = full
    t = kept["x"].shape[0]
    middle, down_low, gu_own, gu_oth, branch_low, gain_grads = whole_call(
        feed_body,
        [((t, D), F32), ((t, D), BF), ((t, FF), BF), ((t, FF), BF), ((t, D), BF), ((3, D), F32)],
        (
            flag, grad_result, kept["down"], kept["gate"], kept["up"], kept["middle"],
            kept["branch"], gains, w_down, g_own, g_oth,
        ),
        6 * t * D * FF,
    )
    wg_g = (t_dot(kept["normed_two"], gu_own), t_dot(kept["normed_two"], gu_oth).astype(BF))
    wg_out = t_dot(kept["mixed"], branch_low).astype(BF)
    wg_down = t_dot(kept["hidden"], down_low).astype(BF)
    return middle, branch_low, wg_g, wg_out, wg_down, gain_grads


def attend_body(window, flag, da, w_out, q, kv, pos_q, pos_k, grad_q, grad_kv):
    reach = pos_q[...] - pos_k[...]
    allowed = (reach >= 0) & (reach < window)
    k, v = kv[:, :HD], kv[:, HD:]
    for head in range(HEADS):
        cols = slice(head * HD, (head + 1) * HD)
        do = last_dot(da[...], w_out[cols, :]).astype(BF)
        s = jnp.where(allowed, last_dot(k, q[:, cols]) * SCALE, -1e30)
        e = jnp.exp(s - jnp.max(s, axis=0, keepdims=True))
        p = e * (1.0 / jnp.sum(e, axis=0, keepdims=True))
        dp = last_dot(v, do)
        inner = jnp.sum(p * dp, axis=0, keepdims=True)
        ds = (p * (dp - inner)).astype(BF)
        grad_q[:, cols] = first_dot(ds, k) * SCALE
        dk = dot(ds, q[:, cols]) * SCALE
        dv = dot(p.astype(BF), do)
        if head == 0:
            total_k, total_v = dk, dv
        else:
            total_k, total_v = total_k + dk, total_v + dv
    grad_kv[:, :HD] = total_k.astype(BF)
    grad_kv[:, HD:] = total_v.astype(BF)


def backward_attend(w_out, kept, branch_low, pos, window, flag):
    t, keys = kept["x"].shape[0], kept["kv"].shape[0]
    return whole_call(
        functools.partial(attend_body, window),
        [((t, HEADS * HD), F32), ((keys, 2 * HD), BF)],
        (flag, branch_low, w_out, kept["q"], kept["kv"], pos[0][None, :], pos[1][:, None]),
        2 * t * HEADS * HD * (5 * keys + D),
    )


def back_body(
    flag, grad_q, grad_kv, qp, kp, heads, cosine, sine, x, dx, q_own, q_oth, gains,
    grad_x, gq_own, gq_oth, gain_zero, head_grads,
):
    first = flag[0] == 0
    cos, sin = cosine[...], sine[...]
    half = HD // 2

    def turned_back(d, u, gain):
        a, b = d[:, :half], d[:, half:]
        n = jnp.concatenate([a * cos + b * sin, b * cos - a * sin], axis=1)
        return rms_back(u, gain, n)

    parts = []
    query_gain = jnp.zeros((1, HD), F32)
    for head in range(HEADS):
        cols = slice(head * HD, (head + 1) * HD)
        du, dg = turned_back(grad_q[:, cols], qp[:, cols], heads[0:1, :])
        parts.append(du.astype(BF))
        query_gain = query_gain + dg
    dk, key_gain = turned_back(grad_kv[:, :HD], kp[...], heads[1:2, :])
    lo = jnp.concatenate(parts[:2] + [dk.astype(BF)], axis=1)
    hi = jnp.concatenate(parts[2:] + [grad_kv[:, HD:].astype(BF)], axis=1)
    own, oth = chosen(first, lo, hi)
    gq_own[...] = own
    gq_oth[...] = oth
    dz = last_dot(own, q_own[:, :QW]) + last_dot(oth, q_oth[:, :QW])
    part, gain = rms_back(x[...], gains[0:1, :], dz)
    grad_x[...] = dx[...] + part
    gain_zero[...] = gain
    head_grads[...] = jnp.concatenate([query_gain, key_gain], axis=0)


def backward_keys(full, kept, middle, grad_q, grad_kv, cosine, sine_table, flag):
    q_own, q_oth, gains, heads = full
    t = kept["x"].shape[0]
    grad_x, gq_own, gq_oth, gain_zero, head_grads = whole_call(
        back_body,
        [((t, D), F32), ((t, QW), BF), ((t, QW), BF), ((1, D), F32), ((2, HD), F32)],
        (
            flag, grad_q, grad_kv, kept["qp"], kept["kp"], heads, cosine, sine_table, kept["x"],
            middle, q_own, q_oth, gains,
        ),
        4 * t * D * QW,
    )
    wg_q = (t_dot(kept["normed"], gq_own).astype(BF), t_dot(kept["normed"], gq_oth).astype(BF))
    return grad_x, wg_q, gain_zero, head_grads


def halves(grad, count):
    return grad.reshape(count, 2, -1, grad.shape[-1])


def local(
    boundary, positions, w_query, w_key_value, w_out, w_gate_up, w_down, norm_gains, head_gains
):
    section = lax.axis_index("section")
    first = section == 0
    ctx_index = lax.axis_index("ctx")
    tokens = boundary.shape[3]
    seq_length = positions.shape[-1]
    nr = w_query.shape[1]
    hr = head_gains.shape[2]
    ro, rd = w_out.shape[1], w_down.shape[1]
    blocks = lax.axis_size("fsdp") * lax.axis_size("ctx")

    moved = exchange(lax.dynamic_index_in_dim(boundary[0, :, 0], 1 - section, 0, False), "section", 1)
    kept_in = lax.dynamic_index_in_dim(boundary[0, :, 0], section, 0, False)
    x0, cotangent = pick(first, kept_in, moved)
    x0 = x0.astype(F32)
    seq_places = lax.dynamic_index_in_dim(positions[:, 0], section, 0, False)
    near = [
        lax.dynamic_slice_in_dim(seq_places, (ctx_index ^ j) * tokens, tokens)
        for j in range(lax.axis_size("ctx"))
    ]
    pos = (near[0], jnp.concatenate(near))
    flag = section.astype(jnp.int32).reshape(1)

    gain_cols = jnp.concatenate(
        [
            norm_gains[0].T,
            jnp.pad(head_gains[0].T, ((0, nr - hr), (0, 0))),
            jnp.zeros((nr, 128 - 6), BF),
        ],
        axis=1,
    )
    cols = [
        jnp.concatenate(
            [
                w_query[0, :, h * QH : (h + 1) * QH],
                w_key_value[0, :, h * HD : (h + 1) * HD],
                gain_cols,
                w_gate_up[0, :, h * FF : (h + 1) * FF],
            ],
            axis=1,
        )
        for h in range(2)
    ]
    rows = [
        jnp.concatenate(
            [
                w_out[0, h * ro // 2 : (h + 1) * ro // 2],
                w_down[0, h * rd // 2 : (h + 1) * rd // 2],
            ],
            axis=0,
        )
        for h in range(2)
    ]
    col_keep, col_send = pick(first, cols[0], cols[1])
    row_keep, row_send = pick(first, rows[0], rows[1])
    col_recv = exchange(col_send, "section", 1)
    row_recv = exchange(row_send, "section", 1)
    layer_cols = pick(first, col_keep, col_recv)
    layer_rows = pick(first, row_keep, row_recv)

    def query_side(pair):
        q_own, q_oth = [v.reshape(blocks * nr, -1) for v in pair]
        gain_part = q_own[:, QW:].astype(F32)
        gains = gain_part[:, :4].T
        heads = gain_part[:, 4:6].reshape(blocks, nr, 2)[:, :hr].reshape(blocks * hr, 2).T
        return q_own, q_oth, gains, heads

    def feed_side(g_pair, b_pair, gains):
        g_own, g_oth = [v.reshape(blocks * nr, -1) for v in g_pair]
        b_lo, b_hi = pick(first, *b_pair)
        full_out = jnp.concatenate([b_lo[:, : ro // 2], b_hi[:, : ro // 2]], axis=1)
        full_down = jnp.concatenate([b_lo[:, ro // 2 :], b_hi[:, ro // 2 :]], axis=1)
        return g_own, g_oth, full_out.reshape(-1, D), full_down.reshape(-1, D), gains

    def reduce_cols(own, other):
        summed = own.astype(F32) + exchange(other, "section", 1).astype(F32)
        return summed.astype(BF).reshape(blocks, nr, -1)

    def reduce_rows(wg_out, wg_down):
        out_half, down_half = halves(wg_out, blocks), halves(wg_down, blocks)

        def part(index):
            return jnp.concatenate(
                [
                    lax.dynamic_index_in_dim(out_half, index, 1, False),
                    lax.dynamic_index_in_dim(down_half, index, 1, False),
                ],
                axis=1,
            )

        recv = exchange(part(1 - section), "section", 1)
        return (part(section).astype(F32) + recv.astype(F32)).astype(BF)

    def reduce_query(wg_q, norm_grads, head_grads):
        norm_part = jnp.concatenate(norm_grads, axis=0).T
        head_part = head_grads.T.reshape(blocks, hr, 2)
        head_part = jnp.pad(head_part, ((0, 0), (0, nr - hr), (0, 0))).reshape(blocks * nr, 2)
        fill = jnp.zeros((blocks * nr, 128 - 6), F32)
        cols = jnp.concatenate([norm_part, head_part, fill], axis=1).astype(BF)
        own = jnp.concatenate([wg_q[0], cols], axis=1)
        oth = jnp.concatenate([wg_q[1], cols], axis=1)
        return reduce_cols(own, oth)

    tables = [rope_tables(pos[0], base) for base in BASES]
    windows = (WIN, seq_length)

    gather0 = Gather(layer_cols[0], layer_rows[0])
    gather0.begin()
    gather0.rows_z()
    gather0.plane(0)
    gather0.plane(1)
    cols1, rows1 = tie(layer_cols[1], layer_rows[1], *gather0.parts, gather0.rows)[:2]
    gather1 = Gather(cols1, rows1)
    pairs0 = gather0.pairs()
    query0 = query_side(pairs0[0])
    kept0 = forward_keys(query0, x0, *tables[0], flag)
    gather1.begin()
    swapped = [v for pair in pairs0[1:] for v in pair]
    kept0["kv"], *held = tie(kept0["kv"], *swapped, *gather1.parts)
    pairs0[1:] = [held[:2], held[2:4]]
    gather1.parts = held[4:]
    gather1.rows_z()
    gather1.plane(0)
    mixed = forward_attend(kept0, pos, windows[0], flag)
    mixed, *gather1.parts = tie(mixed, *gather1.parts)
    gather1.plane(1)
    feed0 = feed_side(*pairs0[1:], query0[2])
    y0 = forward_rest(feed0, kept0, mixed, flag).astype(BF)
    pairs1 = gather1.pairs()
    query1 = query_side(pairs1[0])
    kept1 = forward_keys(query1, y0.astype(F32), *tables[1], flag)
    feed1 = feed_side(*pairs1[1:], query1[2])
    mixed = forward_attend(kept1, pos, windows[1], flag)
    y1 = forward_rest(feed1, kept1, mixed, flag)

    middle1, branch1, wg_g, wg_out, wg_down, norm_grads = backward_feed(
        feed1, kept1, cotangent, flag
    )
    sum_g1 = reduce_cols(*wg_g)
    sum_b1 = reduce_rows(wg_out, wg_down)
    grad_q1, kv_blocks = backward_attend(feed1[2], kept1, branch1, pos, windows[1], flag)
    grad_q1, kv_blocks, sum_g1, sum_b1 = tie(grad_q1, kv_blocks, sum_g1, sum_b1)
    grad_kv = key_return(kv_blocks)
    rows1 = rows_z(sum_b1)
    grad_kv, sum_g1 = tie(grad_kv, sum_g1)
    scat_g1 = Scatter(sum_g1, True)
    scat_g1.plane(0)
    grad1, wg_q, gain_zero, head_grads = backward_keys(
        query1, kept1, middle1, grad_q1, grad_kv, *tables[1], flag
    )
    grad1 = grad1.astype(BF)
    sum_q1 = reduce_query(wg_q, [gain_zero, norm_grads], head_grads)
    grad1, rows1, sum_q1, *held = tie(grad1, rows1, sum_q1, *scat_g1.values())
    scat_g1.put(held)
    scat_g1.plane(1)
    scat_q1 = Scatter(sum_q1, False)
    scat_q1.plane(0)

    middle0, branch0, wg_g, wg_out, wg_down, norm_grads = backward_feed(
        feed0, kept0, grad1, flag
    )
    branch0, rows1, *held = tie(branch0, rows1, *scat_q1.values(), *scat_g1.values())
    scat_q1.put(held[:1])
    scat_g1.put(held[1:])
    red_g1 = scat_g1.along_z()
    red_b1 = rows_plane(rows1)
    scat_q1.plane(1)
    sum_g0 = reduce_cols(*wg_g)
    sum_b0 = reduce_rows(wg_out, wg_down)
    grad_q0, kv_blocks = backward_attend(feed0[2], kept0, branch0, pos, windows[0], flag)
    grad_q0, kv_blocks, sum_g0, sum_b0, red_g1, red_b1, *held = tie(
        grad_q0, kv_blocks, sum_g0, sum_b0, red_g1, red_b1, *scat_q1.values()
    )
    scat_q1.put(held)
    grad_kv = key_return(kv_blocks)
    red_q1 = scat_q1.along_z()
    rows0 = rows_z(sum_b0)
    grad_kv, red_q1, sum_g0 = tie(grad_kv, red_q1, sum_g0)
    scat_g0 = Scatter(sum_g0, True)
    scat_g0.plane(0)
    grad0, wg_q, gain_zero, head_grads = backward_keys(
        query0, kept0, middle0, grad_q0, grad_kv, *tables[0], flag
    )
    sum_q0 = reduce_query(wg_q, [gain_zero, norm_grads], head_grads)
    sum_q0, rows0, *held = tie(sum_q0, rows0, *scat_g0.values())
    scat_g0.put(held)
    scat_q0 = Scatter(sum_q0, False)
    scat_q0.plane(0)
    scat_g0.plane(1)
    scat_q0.plane(1)
    red_q0 = scat_q0.along_z()
    red_g0 = scat_g0.along_z()
    red_b0 = rows_plane(rows0)
    red_c0 = jnp.concatenate([red_q0, red_g0], axis=1)
    red_c1 = jnp.concatenate([red_q1, red_g1], axis=1)

    out_moved = exchange(jnp.where(first, y1, grad0), "section", 1)
    c_keep, c_send = pick(first, red_c0, red_c1)
    b_keep, b_send = pick(first, red_b0, red_b1)
    c_lo, c_hi = pick(first, c_keep, exchange(c_send, "section", 1))
    b_lo, b_hi = pick(first, b_keep, exchange(b_send, "section", 1))
    boundary_out = jnp.where(
        first, jnp.stack([grad0, out_moved]), jnp.stack([out_moved, y1])
    )[None, :, None]
    return (
        boundary_out,
        jnp.concatenate([c_lo[:, :QH], c_hi[:, :QH]], axis=1)[None],
        jnp.concatenate([c_lo[:, QH:QW], c_hi[:, QH:QW]], axis=1)[None],
        jnp.concatenate([b_lo[: ro // 2], b_hi[: ro // 2]], axis=0)[None],
        jnp.concatenate([c_lo[:, QP:], c_hi[:, QP:]], axis=1)[None],
        jnp.concatenate([b_lo[ro // 2 :], b_hi[ro // 2 :]], axis=0)[None],
        c_lo[:, QW : QW + 4].T[None],
        c_lo[:hr, QW + 4 : QW + 6].T[None],
    )


def solution(mesh):
    in_specs = (
        P("section", None, "fsdp", "ctx", None),
        P(None, "fsdp", None),
        P("section", ("fsdp", "ctx"), None),
        P("section", ("fsdp", "ctx"), None),
        P("section", ("fsdp", "ctx"), None),
        P("section", ("fsdp", "ctx"), None),
        P("section", ("fsdp", "ctx"), None),
        P("section", None, ("fsdp", "ctx")),
        P("section", None, ("fsdp", "ctx")),
    )
    out_specs = (
        P("section", None, "fsdp", "ctx", None),
        P("section", ("fsdp", "ctx"), None),
        P("section", ("fsdp", "ctx"), None),
        P("section", ("fsdp", "ctx"), None),
        P("section", ("fsdp", "ctx"), None),
        P("section", ("fsdp", "ctx"), None),
        P("section", None, ("fsdp", "ctx")),
        P("section", None, ("fsdp", "ctx")),
    )
    return jax.shard_map(local, mesh=mesh, in_specs=in_specs, out_specs=out_specs, check_vma=False)
```

```python
import functools
import math

import jax
import jax.numpy as jnp
from jax import lax
from jax.experimental import pallas as pl
from jax.experimental.pallas import tpu as pltpu
from jax.sharding import PartitionSpec as P

D = 640
FF = 2048
HEADS = 4
HD = 256
WIN = 512
MB = 2
QH = 2 * HD
QW = QH + HD
QP = QW + 128

EPS = 1e-06
BASES = (math.log(10000.0), math.log(1000000.0))
SCALE = 1.0 / math.sqrt(HD)
BF = jnp.bfloat16
F32 = jnp.float32


def bits_of(axis):
    return (lax.axis_size(axis) - 1).bit_length()


def exchange(shard, axis, flip):
    pairs = [(i, i ^ flip) for i in range(lax.axis_size(axis))]
    return lax.ppermute(shard, axis, pairs)


def my_bit(axis, bit):
    return (lax.axis_index(axis) >> bit) & 1


def tie(*values):
    return lax.optimization_barrier(values)


def ctx_steps(order):
    count = bits_of("ctx")
    steps = [(bit, count - bit) for bit in range(count)]
    return steps if order == "xy" else steps[::-1]


def z_gather(block):
    count = lax.axis_size("fsdp")
    pieces = [block] + [exchange(block, "fsdp", j) for j in range(1, count)]
    me = lax.axis_index("fsdp")
    return jnp.stack([lax.select_n(me ^ at, *pieces) for at in range(count)])


def ctx_open(buf):
    return buf.reshape((buf.shape[0],) + (1,) * bits_of("ctx") + buf.shape[1:])


def ctx_gather(buf, steps):
    for bit, dim in steps:
        recv = exchange(buf, "ctx", 1 << bit)
        low = my_bit("ctx", bit) == 0
        buf = jnp.concatenate([jnp.where(low, buf, recv), jnp.where(low, recv, buf)], axis=dim)
    return buf


def ctx_close(buf, tail):
    return buf.reshape((-1,) + tail)


def ctx_scatter(buf, steps):
    for bit, dim in steps:
        mine = my_bit("ctx", bit)
        send = lax.dynamic_index_in_dim(buf, 1 - mine, dim, keepdims=True)
        keep = lax.dynamic_index_in_dim(buf, mine, dim, keepdims=True)
        recv = exchange(send, "ctx", 1 << bit)
        buf = (keep.astype(F32) + recv.astype(F32)).astype(BF)
    return buf


def z_scatter(buf):
    me = lax.axis_index("fsdp")
    total = lax.dynamic_index_in_dim(buf, me, 0, False).astype(F32)
    for j in range(1, lax.axis_size("fsdp")):
        part = lax.dynamic_index_in_dim(buf, me ^ j, 0, False)
        total = total + exchange(part, "fsdp", j).astype(F32)
    return total


class Gather:
    ORDERS = ("yx", "xy", "yx")

    def __init__(self, cols, rows):
        self.q, self.g, self.b = cols[:, :QP], cols[:, QP:], rows

    def begin(self):
        q, g = z_gather(self.q), z_gather(self.g)
        half = g.shape[0] // 2
        self.parts = [ctx_open(v) for v in (q, g[:half], g[half:])]
        self.rows = ctx_gather(ctx_open(self.b[None]), ctx_steps("xy"))

    def plane(self, stage):
        done = []
        for v, order in zip(self.parts, self.ORDERS):
            steps = ctx_steps(order)
            done.append(ctx_gather(v, steps[:1] if stage == 0 else steps[1:]))
        self.parts = done

    def rows_z(self):
        self.rows = z_gather(self.rows[0])

    def pairs(self):
        q, g1, g2 = self.parts
        q = ctx_close(q, self.q.shape)
        b = ctx_close(self.rows, self.b.shape)
        g = jnp.concatenate([ctx_close(g1, self.g.shape), ctx_close(g2, self.g.shape)], axis=0)
        return [(v, exchange(v, "section", 1)) for v in (q, g, b)]


class Scatter:
    def __init__(self, blocks, order):
        fs, cb = lax.axis_size("fsdp"), bits_of("ctx")
        self.tail = blocks.shape[1:]
        buf = blocks.reshape((fs,) + (2,) * cb + self.tail)
        split = order == "both"
        self.parts = [(buf[: fs // 2], "xy"), (buf[fs // 2 :], "yx")] if split else [(buf, order)]

    def values(self):
        return [p[0] for p in self.parts]

    def put(self, values):
        self.parts = [(v, p[1]) for v, p in zip(values, self.parts)]

    def plane(self, stage):
        done = []
        for v, order in self.parts:
            steps = ctx_steps(order)
            done.append(ctx_scatter(v, steps[:1] if stage == 0 else steps[1:]))
        self.put(done)

    def along_z(self):
        buf = jnp.concatenate([v.reshape((-1,) + self.tail) for v in self.values()], axis=0)
        return z_scatter(buf)


def rope_tables(places, log_base):
    half_width = HD // 2
    inverse = jnp.exp(-log_base * (jnp.arange(half_width, dtype=F32) * (2.0 / HD)))
    angles = places.astype(F32)[:, None] * inverse[None, :]
    return (jnp.cos(angles), jnp.sin(angles))


def dot(a, b):
    return jnp.dot(a, b, preferred_element_type=F32)


def dot_t(a, b):
    return jnp.einsum("tc,dc->td", a, b, preferred_element_type=F32)


def t_dot(a, b):
    return jnp.einsum("ta,tb->ab", a, b, preferred_element_type=F32)


def pick(first, own, other):
    return jnp.where(first, own, other), jnp.where(first, other, own)


def key_exchange(keys_values):
    count = lax.axis_size("ctx")
    return [keys_values] + [exchange(keys_values, "ctx", j) for j in range(1, count)]


def key_return(blocks):
    count = lax.axis_size("ctx")
    blocks = jnp.split(blocks, count, axis=0)
    total = blocks[0]
    for j in range(1, count):
        total = total + exchange(blocks[j].astype(BF), "ctx", j).astype(F32)
    return total


def whole_call(body, outs, args, flops, window=None):
    vmem = pl.BlockSpec(memory_space=pltpu.VMEM)
    moved = sum(math.prod(v.shape) * v.dtype.itemsize for v in args)
    moved += sum(math.prod(s) * jnp.dtype(t).itemsize for s, t in outs)
    return pl.pallas_call(
        body,
        out_shape=[jax.ShapeDtypeStruct(s, t) for s, t in outs],
        in_specs=[pl.BlockSpec(memory_space=pltpu.SMEM)] + [vmem] * (len(args) - 1),
        out_specs=[vmem] * len(outs),
        compiler_params=pltpu.CompilerParams(vmem_limit_bytes=52 * 2**20),
        cost_estimate=pl.CostEstimate(
            flops=int(flops), bytes_accessed=int(moved), transcendentals=0
        ),
    )(*args)


def inverse_rms(u):
    return lax.rsqrt(jnp.mean(u * u, axis=-1, keepdims=True) + EPS)


def rms_back(u, gain, dz):
    r = inverse_rms(u)
    scaled = dz * gain
    mean = jnp.mean(u * scaled, axis=-1, keepdims=True)
    du = r * (scaled - u * (r * r * mean))
    return du, jnp.sum(dz * u * r, axis=0, keepdims=True)


def last_dot(a, b):
    return lax.dot_general(a, b, (((1,), (1,)), ((), ())), preferred_element_type=F32)


def first_dot(a, b):
    return lax.dot_general(a, b, (((0,), (0,)), ((), ())), preferred_element_type=F32)


def chosen(flag, own, other):
    return jnp.where(flag, own, other), jnp.where(flag, other, own)


def keys_body(flag, x, q_own, q_oth, gains, heads, cosine, sine, normed, qp, kp, q, kv):
    first = flag[0] == 0
    u = x[...]
    h = (u * inverse_rms(u) * gains[0:1, :]).astype(BF)
    normed[...] = h
    lo, hi = chosen(first, dot(h, q_own[:, :QW]), dot(h, q_oth[:, :QW]))
    cos, sin = cosine[...], sine[...]
    half = HD // 2

    def turned(v, gain, out, at):
        n = v * inverse_rms(v) * gain
        a, b = n[:, :half], n[:, half:]
        out[:, at : at + half] = (a * cos - b * sin).astype(BF)
        out[:, at + half : at + HD] = (b * cos + a * sin).astype(BF)

    for head in range(HEADS):
        part = (lo if head < 2 else hi)[:, (head % 2) * HD : (head % 2 + 1) * HD]
        qp[:, head * HD : (head + 1) * HD] = part
        turned(part, heads[0:1, :], q, head * HD)
    k_part = lo[:, QH:]
    kp[...] = k_part
    turned(k_part, heads[1:2, :], kv, 0)
    kv[:, HD:] = hi[:, QH:].astype(BF)


def forward_keys(full, x, cosine, sine_table, flag):
    q_own, q_oth, gains, heads = full
    t = x.shape[0]
    normed, qp, kp, q, kv = whole_call(
        keys_body,
        [((t, D), BF), ((t, HEADS * HD), F32), ((t, HD), F32), ((t, HEADS * HD), BF), ((t, 2 * HD), BF)],
        (flag, x, q_own, q_oth, gains, heads, cosine, sine_table),
        2 * t * D * 2 * QW,
    )
    all_kv = jnp.concatenate(key_exchange(kv), axis=0)
    return dict(x=x, normed=normed, qp=qp, kp=kp, q=q, kv=all_kv)


CHUNK = 512
GELU_A = math.sqrt(2.0 / math.pi)
GELU_B = 0.044715


def mix_body(window, flag, q, kv, pos_q, pos_k, mixed):
    reach = pos_q[...] - pos_k[...]
    allowed = (reach >= 0) & (reach < window)
    k, v = kv[:, :HD], kv[:, HD:]
    for head in range(HEADS):
        cols = slice(head * HD, (head + 1) * HD)
        s = jnp.where(allowed, last_dot(q[:, cols], k) * SCALE, -1e30)
        e = jnp.exp(s - jnp.max(s, axis=-1, keepdims=True))
        total = jnp.sum(e, axis=-1, keepdims=True)
        mixed[:, cols] = (dot(e.astype(BF), v) * (1.0 / total)).astype(BF)


def forward_attend(kept, pos, window, flag):
    t, keys = kept["x"].shape[0], kept["kv"].shape[0]
    return whole_call(
        functools.partial(mix_body, window),
        [((t, HEADS * HD), BF)],
        (flag, kept["q"], kept["kv"], pos[0][:, None], pos[1][None, :]),
        4 * t * HEADS * HD * keys,
    )[0]


def rest_body(
    flag, x, mixed, w_out, g_own, g_oth, w_down, gains,
    branch, middle, normed, gate_out, up_out, hidden, down, result,
):
    first = flag[0] == 0
    b = dot(mixed[...], w_out[...])
    branch[...] = b
    m = x[...] + b * inverse_rms(b) * gains[1:2, :]
    middle[...] = m
    h = (m * inverse_rms(m) * gains[2:3, :]).astype(BF)
    normed[...] = h
    total = jnp.zeros(m.shape, F32)
    for at in range(0, FF, CHUNK):
        cols = slice(at, at + CHUNK)
        gate, up = chosen(first, dot(h, g_own[:, cols]), dot(h, g_oth[:, cols]))
        gate_out[:, cols] = gate
        up_out[:, cols] = up
        th = jnp.tanh(GELU_A * (gate + GELU_B * gate * gate * gate))
        hid = (0.5 * gate * (1.0 + th) * up).astype(BF)
        hidden[:, cols] = hid
        total = total + dot(hid, w_down[cols, :])
    down[...] = total
    result[...] = m + total * inverse_rms(total) * gains[3:4, :]


def forward_rest(full, kept, mixed, flag):
    g_own, g_oth, w_out, w_down, gains = full
    t = kept["x"].shape[0]
    kept["mixed"] = mixed
    names = ("branch", "middle", "normed_two", "gate", "up", "hidden", "down", "result")
    outs = whole_call(
        rest_body,
        [
            ((t, D), F32), ((t, D), F32), ((t, D), BF), ((t, FF), F32),
            ((t, FF), F32), ((t, FF), BF), ((t, D), F32), ((t, D), F32),
        ],
        (flag, kept["x"], mixed, w_out, g_own, g_oth, w_down, gains),
        2 * t * HEADS * HD * D + 6 * t * D * FF,
    )
    kept.update(zip(names, outs))
    return kept["result"]


def feed_body(
    flag, dy, down, gate, up, middle, branch, gains, w_down, g_own, g_oth,
    grad_middle, grad_down, gu_own, gu_oth, grad_branch, gain_grads,
):
    first = flag[0] == 0
    dz = dy[...].astype(F32)
    df, gain_three = rms_back(down[...], gains[3:4, :], dz)
    df = df.astype(BF)
    grad_down[...] = df
    total = jnp.zeros(dz.shape, F32)
    for at in range(0, FF, CHUNK):
        cols = slice(at, at + CHUNK)
        dm = last_dot(df, w_down[cols, :])
        u = gate[:, cols]
        th = jnp.tanh(GELU_A * (u + GELU_B * u * u * u))
        plus = 0.5 * (1.0 + th)
        slope = plus + 0.5 * u * (1.0 - th * th) * (GELU_A * (1.0 + 3.0 * GELU_B * u * u))
        d_gate = (dm * up[:, cols] * slope).astype(BF)
        d_up = (dm * (u * plus)).astype(BF)
        own, oth = chosen(first, d_gate, d_up)
        gu_own[:, cols] = own
        gu_oth[:, cols] = oth
        total = total + last_dot(own, g_own[:, cols]) + last_dot(oth, g_oth[:, cols])
    part, gain_two = rms_back(middle[...], gains[2:3, :], total)
    dx = dz + part
    grad_middle[...] = dx
    da, gain_one = rms_back(branch[...], gains[1:2, :], dx)
    grad_branch[...] = da.astype(BF)
    gain_grads[...] = jnp.concatenate([gain_one, gain_two, gain_three], axis=0)


def backward_feed(full, kept, grad_result, flag):
    g_own, g_oth, w_out, w_down, gains = full
    t = kept["x"].shape[0]
    middle, down_low, gu_own, gu_oth, branch_low, gain_grads = whole_call(
        feed_body,
        [((t, D), F32), ((t, D), BF), ((t, FF), BF), ((t, FF), BF), ((t, D), BF), ((3, D), F32)],
        (
            flag, grad_result, kept["down"], kept["gate"], kept["up"], kept["middle"],
            kept["branch"], gains, w_down, g_own, g_oth,
        ),
        6 * t * D * FF,
    )
    wg_g = (t_dot(kept["normed_two"], gu_own), t_dot(kept["normed_two"], gu_oth).astype(BF))
    wg_out = t_dot(kept["mixed"], branch_low).astype(BF)
    wg_down = t_dot(kept["hidden"], down_low).astype(BF)
    return middle, branch_low, wg_g, wg_out, wg_down, gain_grads


def attend_body(window, flag, da, w_out, q, kv, pos_q, pos_k, grad_q, grad_kv):
    reach = pos_q[...] - pos_k[...]
    allowed = (reach >= 0) & (reach < window)
    k, v = kv[:, :HD], kv[:, HD:]
    for head in range(HEADS):
        cols = slice(head * HD, (head + 1) * HD)
        do = last_dot(da[...], w_out[cols, :]).astype(BF)
        s = jnp.where(allowed, last_dot(k, q[:, cols]) * SCALE, -1e30)
        e = jnp.exp(s - jnp.max(s, axis=0, keepdims=True))
        p = e * (1.0 / jnp.sum(e, axis=0, keepdims=True))
        dp = last_dot(v, do)
        inner = jnp.sum(p * dp, axis=0, keepdims=True)
        ds = (p * (dp - inner)).astype(BF)
        grad_q[:, cols] = first_dot(ds, k) * SCALE
        dk = dot(ds, q[:, cols]) * SCALE
        dv = dot(p.astype(BF), do)
        if head == 0:
            total_k, total_v = dk, dv
        else:
            total_k, total_v = total_k + dk, total_v + dv
    grad_kv[:, :HD] = total_k.astype(BF)
    grad_kv[:, HD:] = total_v.astype(BF)


def backward_attend(w_out, kept, branch_low, pos, window, flag):
    t, keys = kept["x"].shape[0], kept["kv"].shape[0]
    return whole_call(
        functools.partial(attend_body, window),
        [((t, HEADS * HD), F32), ((keys, 2 * HD), BF)],
        (flag, branch_low, w_out, kept["q"], kept["kv"], pos[0][None, :], pos[1][:, None]),
        2 * t * HEADS * HD * (5 * keys + D),
    )


def back_body(
    flag, grad_q, grad_kv, qp, kp, heads, cosine, sine, x, dx, q_own, q_oth, gains,
    grad_x, gq_own, gq_oth, gain_zero, head_grads,
):
    first = flag[0] == 0
    cos, sin = cosine[...], sine[...]
    half = HD // 2

    def turned_back(d, u, gain):
        a, b = d[:, :half], d[:, half:]
        n = jnp.concatenate([a * cos + b * sin, b * cos - a * sin], axis=1)
        return rms_back(u, gain, n)

    parts = []
    query_gain = jnp.zeros((1, HD), F32)
    for head in range(HEADS):
        cols = slice(head * HD, (head + 1) * HD)
        du, dg = turned_back(grad_q[:, cols], qp[:, cols], heads[0:1, :])
        parts.append(du.astype(BF))
        query_gain = query_gain + dg
    dk, key_gain = turned_back(grad_kv[:, :HD], kp[...], heads[1:2, :])
    lo = jnp.concatenate(parts[:2] + [dk.astype(BF)], axis=1)
    hi = jnp.concatenate(parts[2:] + [grad_kv[:, HD:].astype(BF)], axis=1)
    own, oth = chosen(first, lo, hi)
    gq_own[...] = own
    gq_oth[...] = oth
    dz = last_dot(own, q_own[:, :QW]) + last_dot(oth, q_oth[:, :QW])
    part, gain = rms_back(x[...], gains[0:1, :], dz)
    grad_x[...] = dx[...] + part
    gain_zero[...] = gain
    head_grads[...] = jnp.concatenate([query_gain, key_gain], axis=0)


def backward_keys(full, kept, middle, grad_q, grad_kv, cosine, sine_table, flag):
    q_own, q_oth, gains, heads = full
    t = kept["x"].shape[0]
    grad_x, gq_own, gq_oth, gain_zero, head_grads = whole_call(
        back_body,
        [((t, D), F32), ((t, QW), BF), ((t, QW), BF), ((1, D), F32), ((2, HD), F32)],
        (
            flag, grad_q, grad_kv, kept["qp"], kept["kp"], heads, cosine, sine_table, kept["x"],
            middle, q_own, q_oth, gains,
        ),
        4 * t * D * QW,
    )
    wg_q = (t_dot(kept["normed"], gq_own).astype(BF), t_dot(kept["normed"], gq_oth).astype(BF))
    return grad_x, wg_q, gain_zero, head_grads


def halves(grad, count):
    return grad.reshape(count, 2, -1, grad.shape[-1])


def local(
    boundary, positions, w_query, w_key_value, w_out, w_gate_up, w_down, norm_gains, head_gains
):
    section = lax.axis_index("section")
    first = section == 0
    ctx_index = lax.axis_index("ctx")
    tokens = boundary.shape[3]
    seq_length = positions.shape[-1]
    nr = w_query.shape[1]
    hr = head_gains.shape[2]
    ro, rd = w_out.shape[1], w_down.shape[1]
    blocks = lax.axis_size("fsdp") * lax.axis_size("ctx")

    moved = exchange(lax.dynamic_index_in_dim(boundary[0, :, 0], 1 - section, 0, False), "section", 1)
    kept_in = lax.dynamic_index_in_dim(boundary[0, :, 0], section, 0, False)
    x0, cotangent = pick(first, kept_in, moved)
    x0 = x0.astype(F32)
    seq_places = lax.dynamic_index_in_dim(positions[:, 0], section, 0, False)
    near = [
        lax.dynamic_slice_in_dim(seq_places, (ctx_index ^ j) * tokens, tokens)
        for j in range(lax.axis_size("ctx"))
    ]
    pos = (near[0], jnp.concatenate(near))
    flag = section.astype(jnp.int32).reshape(1)

    gain_cols = jnp.concatenate(
        [
            norm_gains[0].T,
            jnp.pad(head_gains[0].T, ((0, nr - hr), (0, 0))),
            jnp.zeros((nr, 128 - 6), BF),
        ],
        axis=1,
    )
    cols = [
        jnp.concatenate(
            [
                w_query[0, :, h * QH : (h + 1) * QH],
                w_key_value[0, :, h * HD : (h + 1) * HD],
                gain_cols,
                w_gate_up[0, :, h * FF : (h + 1) * FF],
            ],
            axis=1,
        )
        for h in range(2)
    ]
    rows = [
        jnp.concatenate(
            [
                w_out[0, h * ro // 2 : (h + 1) * ro // 2],
                w_down[0, h * rd // 2 : (h + 1) * rd // 2],
            ],
            axis=0,
        )
        for h in range(2)
    ]
    col_keep, col_send = pick(first, cols[0], cols[1])
    row_keep, row_send = pick(first, rows[0], rows[1])
    col_recv = exchange(col_send, "section", 1)
    row_recv = exchange(row_send, "section", 1)
    layer_cols = pick(first, col_keep, col_recv)
    layer_rows = pick(first, row_keep, row_recv)

    def query_side(pair):
        q_own, q_oth = [v.reshape(blocks * nr, -1) for v in pair]
        gain_part = q_own[:, QW:].astype(F32)
        gains = gain_part[:, :4].T
        heads = gain_part[:, 4:6].reshape(blocks, nr, 2)[:, :hr].reshape(blocks * hr, 2).T
        return q_own, q_oth, gains, heads

    def feed_side(g_pair, b_pair, gains):
        g_own, g_oth = [v.reshape(blocks * nr, -1) for v in g_pair]
        b_lo, b_hi = pick(first, *b_pair)
        full_out = jnp.concatenate([b_lo[:, : ro // 2], b_hi[:, : ro // 2]], axis=1)
        full_down = jnp.concatenate([b_lo[:, ro // 2 :], b_hi[:, ro // 2 :]], axis=1)
        return g_own, g_oth, full_out.reshape(-1, D), full_down.reshape(-1, D), gains

    def reduce_cols(own, other):
        summed = own.astype(F32) + exchange(other, "section", 1).astype(F32)
        return summed.astype(BF).reshape(blocks, nr, -1)

    def reduce_rows(wg_out, wg_down):
        out_half, down_half = halves(wg_out, blocks), halves(wg_down, blocks)

        def part(index):
            return jnp.concatenate(
                [
                    lax.dynamic_index_in_dim(out_half, index, 1, False),
                    lax.dynamic_index_in_dim(down_half, index, 1, False),
                ],
                axis=1,
            )

        recv = exchange(part(1 - section), "section", 1)
        return (part(section).astype(F32) + recv.astype(F32)).astype(BF)

    def reduce_query(wg_q, norm_grads, head_grads):
        norm_part = jnp.concatenate(norm_grads, axis=0).T
        head_part = head_grads.T.reshape(blocks, hr, 2)
        head_part = jnp.pad(head_part, ((0, 0), (0, nr - hr), (0, 0))).reshape(blocks * nr, 2)
        fill = jnp.zeros((blocks * nr, 128 - 6), F32)
        cols = jnp.concatenate([norm_part, head_part, fill], axis=1).astype(BF)
        own = jnp.concatenate([wg_q[0], cols], axis=1)
        oth = jnp.concatenate([wg_q[1], cols], axis=1)
        return reduce_cols(own, oth)

    tables = [rope_tables(pos[0], base) for base in BASES]
    windows = (WIN, seq_length)

    gather0 = Gather(layer_cols[0], layer_rows[0])
    gather0.begin()
    gather0.rows_z()
    gather0.plane(0)
    gather0.plane(1)
    pairs0 = gather0.pairs()
    query0 = query_side(pairs0[0])
    kept0 = forward_keys(query0, x0, *tables[0], flag)
    cols1, rows1 = tie(layer_cols[1], layer_rows[1], kept0["q"], *gather0.parts)[:2]
    gather1 = Gather(cols1, rows1)
    gather1.begin()
    swapped = [v for pair in pairs0[1:] for v in pair]
    kept0["kv"], *held = tie(kept0["kv"], *swapped, *gather1.parts)
    pairs0[1:] = [held[:2], held[2:4]]
    gather1.parts = held[4:]
    gather1.plane(0)
    mixed = forward_attend(kept0, pos, windows[0], flag)
    mixed, gather1.rows, *gather1.parts = tie(mixed, gather1.rows, *gather1.parts)
    gather1.rows_z()
    gather1.plane(1)
    feed0 = feed_side(*pairs0[1:], query0[2])
    y0 = forward_rest(feed0, kept0, mixed, flag).astype(BF)
    pairs1 = gather1.pairs()
    query1 = query_side(pairs1[0])
    kept1 = forward_keys(query1, y0.astype(F32), *tables[1], flag)
    feed1 = feed_side(*pairs1[1:], query1[2])
    mixed = forward_attend(kept1, pos, windows[1], flag)
    y1 = forward_rest(feed1, kept1, mixed, flag)

    middle1, branch1, wg_g, wg_out, wg_down, norm_grads = backward_feed(
        feed1, kept1, cotangent, flag
    )
    sum_g1 = reduce_cols(*wg_g)
    sum_b1 = reduce_rows(wg_out, wg_down)
    grad_q1, kv_blocks = backward_attend(feed1[2], kept1, branch1, pos, windows[1], flag)
    grad_q1, kv_blocks, sum_g1, sum_b1 = tie(grad_q1, kv_blocks, sum_g1, sum_b1)
    grad_kv = key_return(kv_blocks)
    grad_kv, sum_g1, sum_b1 = tie(grad_kv, sum_g1, sum_b1)
    scat_g1, scat_b1 = Scatter(sum_g1, "both"), Scatter(sum_b1, "yx")
    scat_g1.plane(0)
    grad1, wg_q, gain_zero, head_grads = backward_keys(
        query1, kept1, middle1, grad_q1, grad_kv, *tables[1], flag
    )
    grad1 = grad1.astype(BF)
    sum_q1 = reduce_query(wg_q, [gain_zero, norm_grads], head_grads)

    middle0, branch0, wg_g, wg_out, wg_down, norm_grads = backward_feed(
        feed0, kept0, grad1, flag
    )
    branch0, sum_q1, held0, *held = tie(branch0, sum_q1, *scat_b1.values(), *scat_g1.values())
    scat_g1.put(held)
    scat_b1.put([held0])
    scat_q1 = Scatter(sum_q1, "xy")
    scat_g1.plane(1)
    scat_q1.plane(0)
    scat_b1.plane(0)
    red_g1 = scat_g1.along_z()
    sum_g0 = reduce_cols(*wg_g)
    sum_b0 = reduce_rows(wg_out, wg_down)
    grad_q0, kv_blocks = backward_attend(feed0[2], kept0, branch0, pos, windows[0], flag)
    grad_q0, kv_blocks, sum_g0, sum_b0, red_g1, held0 = tie(
        grad_q0, kv_blocks, sum_g0, sum_b0, red_g1, *scat_q1.values()
    )
    scat_q1.put([held0])
    grad_kv = key_return(kv_blocks)
    scat_b0 = Scatter(sum_b0, "yx")
    scat_b0.plane(0)
    grad_kv, sum_g0, *held = tie(grad_kv, sum_g0, *scat_q1.values(), *scat_b1.values())
    scat_q1.put(held[:1])
    scat_b1.put(held[1:])
    scat_g0 = Scatter(sum_g0, "both")
    scat_g0.plane(0)
    grad0, wg_q, gain_zero, head_grads = backward_keys(
        query0, kept0, middle0, grad_q0, grad_kv, *tables[0], flag
    )
    sum_q0 = reduce_query(wg_q, [gain_zero, norm_grads], head_grads)
    sum_q0, held1, held2, *held = tie(
        sum_q0, *scat_q1.values(), *scat_b1.values(), *scat_g0.values()
    )
    scat_q1.put([held1])
    scat_b1.put([held2])
    scat_g0.put(held)
    scat_q0 = Scatter(sum_q0, "xy")
    scat_q0.plane(0)
    scat_g0.plane(1)
    scat_q0.plane(1)
    scat_q1.plane(1)
    scat_b1.plane(1)
    red_q1, red_b1 = scat_q1.along_z(), scat_b1.along_z()
    red_q0, red_g0 = scat_q0.along_z(), scat_g0.along_z()
    scat_b0.plane(1)
    red_b0 = scat_b0.along_z()
    red_c0 = jnp.concatenate([red_q0, red_g0], axis=1)
    red_c1 = jnp.concatenate([red_q1, red_g1], axis=1)

    out_moved = exchange(jnp.where(first, y1, grad0), "section", 1)
    c_keep, c_send = pick(first, red_c0, red_c1)
    b_keep, b_send = pick(first, red_b0, red_b1)
    c_lo, c_hi = pick(first, c_keep, exchange(c_send, "section", 1))
    b_lo, b_hi = pick(first, b_keep, exchange(b_send, "section", 1))
    boundary_out = jnp.where(
        first, jnp.stack([grad0, out_moved]), jnp.stack([out_moved, y1])
    )[None, :, None]
    return (
        boundary_out,
        jnp.concatenate([c_lo[:, :QH], c_hi[:, :QH]], axis=1)[None],
        jnp.concatenate([c_lo[:, QH:QW], c_hi[:, QH:QW]], axis=1)[None],
        jnp.concatenate([b_lo[: ro // 2], b_hi[: ro // 2]], axis=0)[None],
        jnp.concatenate([c_lo[:, QP:], c_hi[:, QP:]], axis=1)[None],
        jnp.concatenate([b_lo[ro // 2 :], b_hi[ro // 2 :]], axis=0)[None],
        c_lo[:, QW : QW + 4].T[None],
        c_lo[:hr, QW + 4 : QW + 6].T[None],
    )


def solution(mesh):
    in_specs = (
        P("section", None, "fsdp", "ctx", None),
        P(None, "fsdp", None),
        P("section", ("fsdp", "ctx"), None),
        P("section", ("fsdp", "ctx"), None),
        P("section", ("fsdp", "ctx"), None),
        P("section", ("fsdp", "ctx"), None),
        P("section", ("fsdp", "ctx"), None),
        P("section", None, ("fsdp", "ctx")),
        P("section", None, ("fsdp", "ctx")),
    )
    out_specs = (
        P("section", None, "fsdp", "ctx", None),
        P("section", ("fsdp", "ctx"), None),
        P("section", ("fsdp", "ctx"), None),
        P("section", ("fsdp", "ctx"), None),
        P("section", ("fsdp", "ctx"), None),
        P("section", ("fsdp", "ctx"), None),
        P("section", None, ("fsdp", "ctx")),
        P("section", None, ("fsdp", "ctx")),
    )
    return jax.shard_map(local, mesh=mesh, in_specs=in_specs, out_specs=out_specs, check_vma=False)
```

```python
import functools
import math

import jax
import jax.numpy as jnp
from jax import lax
from jax.experimental import pallas as pl
from jax.experimental.pallas import tpu as pltpu
from jax.sharding import PartitionSpec as P

D = 640
FF = 2048
HEADS = 4
HD = 256
WIN = 512
MB = 2
QH = 2 * HD
QW = QH + HD
QP = QW + 128

EPS = 1e-06
BASES = (math.log(10000.0), math.log(1000000.0))
SCALE = 1.0 / math.sqrt(HD)
BF = jnp.bfloat16
GRID = ("fsdp", "ctx")
F32 = jnp.float32


def bits_of(axis):
    return (lax.axis_size(axis) - 1).bit_length()


def exchange(shard, axis, flip):
    pairs = [(i, i ^ flip) for i in range(lax.axis_size(axis))]
    return lax.ppermute(shard, axis, pairs)


def my_bit(axis, bit):
    return (lax.axis_index(axis) >> bit) & 1


def tie(*values):
    return lax.optimization_barrier(values)


def ctx_steps(order):
    count = bits_of("ctx")
    steps = [(bit, count - bit) for bit in range(count)]
    return steps if order == "xy" else steps[::-1]


def z_gather(block):
    count = lax.axis_size("fsdp")
    pieces = [block] + [exchange(block, "fsdp", j) for j in range(1, count)]
    me = lax.axis_index("fsdp")
    return jnp.stack([lax.select_n(me ^ at, *pieces) for at in range(count)])


def ctx_open(buf):
    return buf.reshape((buf.shape[0],) + (1,) * bits_of("ctx") + buf.shape[1:])


def ctx_gather(buf, steps):
    for bit, dim in steps:
        recv = exchange(buf, "ctx", 1 << bit)
        low = my_bit("ctx", bit) == 0
        buf = jnp.concatenate([jnp.where(low, buf, recv), jnp.where(low, recv, buf)], axis=dim)
    return buf


def ctx_close(buf, tail):
    return buf.reshape((-1,) + tail)


def ctx_scatter(buf, steps):
    for bit, dim in steps:
        mine = my_bit("ctx", bit)
        send = lax.dynamic_index_in_dim(buf, 1 - mine, dim, keepdims=True)
        keep = lax.dynamic_index_in_dim(buf, mine, dim, keepdims=True)
        recv = exchange(send, "ctx", 1 << bit)
        buf = (keep.astype(F32) + recv.astype(F32)).astype(BF)
    return buf


def z_scatter(buf):
    me = lax.axis_index("fsdp")
    total = lax.dynamic_index_in_dim(buf, me, 0, False).astype(F32)
    for j in range(1, lax.axis_size("fsdp")):
        part = lax.dynamic_index_in_dim(buf, me ^ j, 0, False)
        total = total + exchange(part, "fsdp", j).astype(F32)
    return total


def pack_rows(rows, height):
    lead, r = rows.shape[:-2], rows.shape[-2]
    if r % 8 or height % 8 or r * D // height % 128 or height // 8 != D // 128:
        return rows.reshape(lead + (height, r * D // height))
    tiles = rows.reshape(lead + (r // 8, 8, D // 128, 128))
    return jnp.swapaxes(tiles, -4, -2).reshape(lead + (height, r * D // height))


def unpack_rows(packed, r):
    lead, height = packed.shape[:-2], packed.shape[-2]
    if r % 8 or height % 8 or r * D // height % 128 or height // 8 != D // 128:
        return packed.reshape(lead + (r, D))
    tiles = packed.reshape(lead + (height // 8, 8, r // 8, 128))
    return jnp.swapaxes(tiles, -4, -2).reshape(lead + (r, D))


class Gather:
    ORDERS = ("yx", "xy", "yx")

    def __init__(self, cols, rows):
        self.q, self.g, self.b = cols[:, :QP], cols[:, QP:], rows

    def begin(self):
        q, g = z_gather(self.q), z_gather(self.g)
        half = g.shape[0] // 2
        self.parts = [ctx_open(v) for v in (q, g[:half], g[half:])]
        self.rows = ctx_gather(ctx_open(self.b[None]), ctx_steps("xy"))

    def plane(self, stage):
        done = []
        for v, order in zip(self.parts, self.ORDERS):
            steps = ctx_steps(order)
            done.append(ctx_gather(v, steps[:1] if stage == 0 else steps[1:]))
        self.parts = done

    def rows_z(self):
        self.rows = z_gather(self.rows[0])

    def pairs(self):
        q, g1, g2 = self.parts
        q = ctx_close(q, self.q.shape)
        b = ctx_close(self.rows, self.b.shape)
        g = jnp.concatenate([ctx_close(g1, self.g.shape), ctx_close(g2, self.g.shape)], axis=0)
        return [(v, exchange(v, "section", 1)) for v in (q, g, b)]


class Scatter:
    def __init__(self, blocks, order):
        fs, cb = lax.axis_size("fsdp"), bits_of("ctx")
        self.tail = blocks.shape[1:]
        buf = blocks.reshape((fs,) + (2,) * cb + self.tail)
        split = order == "both"
        self.parts = [(buf[: fs // 2], "xy"), (buf[fs // 2 :], "yx")] if split else [(buf, order)]

    def values(self):
        return [p[0] for p in self.parts]

    def put(self, values):
        self.parts = [(v, p[1]) for v, p in zip(values, self.parts)]

    def plane(self, stage):
        done = []
        for v, order in self.parts:
            steps = ctx_steps(order)
            done.append(ctx_scatter(v, steps[:1] if stage == 0 else steps[1:]))
        self.put(done)

    def along_z(self):
        buf = jnp.concatenate([v.reshape((-1,) + self.tail) for v in self.values()], axis=0)
        return z_scatter(buf)


def rope_tables(places, log_base):
    half_width = HD // 2
    inverse = jnp.exp(-log_base * (jnp.arange(half_width, dtype=F32) * (2.0 / HD)))
    angles = places.astype(F32)[:, None] * inverse[None, :]
    return (jnp.cos(angles), jnp.sin(angles))


def dot(a, b):
    return jnp.dot(a, b, preferred_element_type=F32)


def dot_t(a, b):
    return jnp.einsum("tc,dc->td", a, b, preferred_element_type=F32)


def t_dot(a, b):
    return jnp.einsum("ta,tb->ab", a, b, preferred_element_type=F32)


def pick(first, own, other):
    return jnp.where(first, own, other), jnp.where(first, other, own)


def key_exchange(keys_values):
    count = lax.axis_size("ctx")
    return [keys_values] + [exchange(keys_values, "ctx", j) for j in range(1, count)]


def key_return(blocks):
    count = lax.axis_size("ctx")
    blocks = jnp.split(blocks, count, axis=0)
    total = blocks[0]
    for j in range(1, count):
        total = total + exchange(blocks[j].astype(BF), "ctx", j).astype(F32)
    return total


def whole_call(body, outs, args, flops, window=None):
    vmem = pl.BlockSpec(memory_space=pltpu.VMEM)
    moved = sum(math.prod(v.shape) * v.dtype.itemsize for v in args)
    moved += sum(math.prod(s) * jnp.dtype(t).itemsize for s, t in outs)
    return pl.pallas_call(
        body,
        out_shape=[jax.ShapeDtypeStruct(s, t) for s, t in outs],
        in_specs=[pl.BlockSpec(memory_space=pltpu.SMEM)] + [vmem] * (len(args) - 1),
        out_specs=[vmem] * len(outs),
        compiler_params=pltpu.CompilerParams(vmem_limit_bytes=52 * 2**20),
        cost_estimate=pl.CostEstimate(
            flops=int(flops) // 64, bytes_accessed=int(moved) // 64, transcendentals=0
        ),
    )(*args)


def inverse_rms(u):
    return lax.rsqrt(jnp.mean(u * u, axis=-1, keepdims=True) + EPS)


def rms_back(u, gain, dz):
    r = inverse_rms(u)
    scaled = dz * gain
    mean = jnp.mean(u * scaled, axis=-1, keepdims=True)
    du = r * (scaled - u * (r * r * mean))
    return du, jnp.sum(dz * u * r, axis=0, keepdims=True)


def last_dot(a, b):
    return lax.dot_general(a, b, (((1,), (1,)), ((), ())), preferred_element_type=F32)


def first_dot(a, b):
    return lax.dot_general(a, b, (((0,), (0,)), ((), ())), preferred_element_type=F32)


def chosen(flag, own, other):
    return jnp.where(flag, own, other), jnp.where(flag, other, own)


def keys_body(flag, x, q_own, q_oth, gains, heads, cosine, sine, normed, qp, kp, q, kv):
    first = flag[0] == 0
    u = x[...]
    h = (u * inverse_rms(u) * gains[0:1, :]).astype(BF)
    normed[...] = h
    lo, hi = chosen(first, dot(h, q_own[:, :QW]), dot(h, q_oth[:, :QW]))
    cos, sin = cosine[...], sine[...]
    half = HD // 2

    def turned(v, gain, out, at):
        n = v * inverse_rms(v) * gain
        a, b = n[:, :half], n[:, half:]
        out[:, at : at + half] = (a * cos - b * sin).astype(BF)
        out[:, at + half : at + HD] = (b * cos + a * sin).astype(BF)

    for head in range(HEADS):
        part = (lo if head < 2 else hi)[:, (head % 2) * HD : (head % 2 + 1) * HD]
        qp[:, head * HD : (head + 1) * HD] = part
        turned(part, heads[0:1, :], q, head * HD)
    k_part = lo[:, QH:]
    kp[...] = k_part
    turned(k_part, heads[1:2, :], kv, 0)
    kv[:, HD:] = hi[:, QH:].astype(BF)


def forward_keys(full, x, cosine, sine_table, flag):
    q_own, q_oth, gains, heads = full
    t = x.shape[0]
    normed, qp, kp, q, kv = whole_call(
        keys_body,
        [((t, D), BF), ((t, HEADS * HD), F32), ((t, HD), F32), ((t, HEADS * HD), BF), ((t, 2 * HD), BF)],
        (flag, x, q_own, q_oth, gains, heads, cosine, sine_table),
        2 * t * D * 2 * QW,
    )
    all_kv = jnp.concatenate(key_exchange(kv), axis=0)
    return dict(x=x, normed=normed, qp=qp, kp=kp, q=q, kv=all_kv)


CHUNK = 512
GELU_A = math.sqrt(2.0 / math.pi)
GELU_B = 0.044715


def mix_body(window, flag, q, kv, pos_q, pos_k, mixed):
    reach = pos_q[...] - pos_k[...]
    allowed = (reach >= 0) & (reach < window)
    k, v = kv[:, :HD], kv[:, HD:]
    for head in range(HEADS):
        cols = slice(head * HD, (head + 1) * HD)
        s = jnp.where(allowed, last_dot(q[:, cols], k) * SCALE, -1e30)
        e = jnp.exp(s - jnp.max(s, axis=-1, keepdims=True))
        total = jnp.sum(e, axis=-1, keepdims=True)
        mixed[:, cols] = (dot(e.astype(BF), v) * (1.0 / total)).astype(BF)


def forward_attend(kept, pos, window, flag):
    t, keys = kept["x"].shape[0], kept["kv"].shape[0]
    return whole_call(
        functools.partial(mix_body, window),
        [((t, HEADS * HD), BF)],
        (flag, kept["q"], kept["kv"], pos[0][:, None], pos[1][None, :]),
        4 * t * HEADS * HD * keys,
    )[0]


def rest_body(
    flag, x, mixed, w_out, g_own, g_oth, w_down, gains,
    branch, middle, normed, gate_out, up_out, hidden, down, result,
):
    first = flag[0] == 0
    b = dot(mixed[...], w_out[...])
    branch[...] = b
    m = x[...] + b * inverse_rms(b) * gains[1:2, :]
    middle[...] = m
    h = (m * inverse_rms(m) * gains[2:3, :]).astype(BF)
    normed[...] = h
    total = jnp.zeros(m.shape, F32)
    for at in range(0, FF, CHUNK):
        cols = slice(at, at + CHUNK)
        gate, up = chosen(first, dot(h, g_own[:, cols]), dot(h, g_oth[:, cols]))
        gate_out[:, cols] = gate
        up_out[:, cols] = up
        th = jnp.tanh(GELU_A * (gate + GELU_B * gate * gate * gate))
        hid = (0.5 * gate * (1.0 + th) * up).astype(BF)
        hidden[:, cols] = hid
        total = total + dot(hid, w_down[cols, :])
    down[...] = total
    result[...] = m + total * inverse_rms(total) * gains[3:4, :]


def forward_rest(full, kept, mixed, flag):
    g_own, g_oth, w_out, w_down, gains = full
    t = kept["x"].shape[0]
    kept["mixed"] = mixed
    names = ("branch", "middle", "normed_two", "gate", "up", "hidden", "down", "result")
    outs = whole_call(
        rest_body,
        [
            ((t, D), F32), ((t, D), F32), ((t, D), BF), ((t, FF), F32),
            ((t, FF), F32), ((t, FF), BF), ((t, D), F32), ((t, D), F32),
        ],
        (flag, kept["x"], mixed, w_out, g_own, g_oth, w_down, gains),
        2 * t * HEADS * HD * D + 6 * t * D * FF,
    )
    kept.update(zip(names, outs))
    return kept["result"]


def feed_body(
    flag, dy, down, gate, up, middle, branch, gains, w_down, g_own, g_oth,
    grad_middle, grad_down, gu_own, gu_oth, grad_branch, gain_grads,
):
    first = flag[0] == 0
    dz = dy[...].astype(F32)
    df, gain_three = rms_back(down[...], gains[3:4, :], dz)
    df = df.astype(BF)
    grad_down[...] = df
    total = jnp.zeros(dz.shape, F32)
    for at in range(0, FF, CHUNK):
        cols = slice(at, at + CHUNK)
        dm = last_dot(df, w_down[cols, :])
        u = gate[:, cols]
        th = jnp.tanh(GELU_A * (u + GELU_B * u * u * u))
        plus = 0.5 * (1.0 + th)
        slope = plus + 0.5 * u * (1.0 - th * th) * (GELU_A * (1.0 + 3.0 * GELU_B * u * u))
        d_gate = (dm * up[:, cols] * slope).astype(BF)
        d_up = (dm * (u * plus)).astype(BF)
        own, oth = chosen(first, d_gate, d_up)
        gu_own[:, cols] = own
        gu_oth[:, cols] = oth
        total = total + last_dot(own, g_own[:, cols]) + last_dot(oth, g_oth[:, cols])
    part, gain_two = rms_back(middle[...], gains[2:3, :], total)
    dx = dz + part
    grad_middle[...] = dx
    da, gain_one = rms_back(branch[...], gains[1:2, :], dx)
    grad_branch[...] = da.astype(BF)
    gain_grads[...] = jnp.concatenate([gain_one, gain_two, gain_three], axis=0)


def backward_feed(full, kept, grad_result, flag):
    g_own, g_oth, w_out, w_down, gains = full
    t = kept["x"].shape[0]
    middle, down_low, gu_own, gu_oth, branch_low, gain_grads = whole_call(
        feed_body,
        [((t, D), F32), ((t, D), BF), ((t, FF), BF), ((t, FF), BF), ((t, D), BF), ((3, D), F32)],
        (
            flag, grad_result, kept["down"], kept["gate"], kept["up"], kept["middle"],
            kept["branch"], gains, w_down, g_own, g_oth,
        ),
        6 * t * D * FF,
    )
    wg_g = (t_dot(kept["normed_two"], gu_own), t_dot(kept["normed_two"], gu_oth).astype(BF))
    wg_out = t_dot(kept["mixed"], branch_low).astype(BF)
    wg_down = t_dot(kept["hidden"], down_low).astype(BF)
    return middle, branch_low, wg_g, wg_out, wg_down, gain_grads


def attend_body(window, flag, da, w_out, q, kv, pos_q, pos_k, grad_q, grad_kv):
    reach = pos_q[...] - pos_k[...]
    allowed = (reach >= 0) & (reach < window)
    k, v = kv[:, :HD], kv[:, HD:]
    for head in range(HEADS):
        cols = slice(head * HD, (head + 1) * HD)
        do = last_dot(da[...], w_out[cols, :]).astype(BF)
        s = jnp.where(allowed, last_dot(k, q[:, cols]) * SCALE, -1e30)
        e = jnp.exp(s - jnp.max(s, axis=0, keepdims=True))
        p = e * (1.0 / jnp.sum(e, axis=0, keepdims=True))
        dp = last_dot(v, do)
        inner = jnp.sum(p * dp, axis=0, keepdims=True)
        ds = (p * (dp - inner)).astype(BF)
        grad_q[:, cols] = first_dot(ds, k) * SCALE
        dk = dot(ds, q[:, cols]) * SCALE
        dv = dot(p.astype(BF), do)
        if head == 0:
            total_k, total_v = dk, dv
        else:
            total_k, total_v = total_k + dk, total_v + dv
    grad_kv[:, :HD] = total_k.astype(BF)
    grad_kv[:, HD:] = total_v.astype(BF)


def backward_attend(w_out, kept, branch_low, pos, window, flag):
    t, keys = kept["x"].shape[0], kept["kv"].shape[0]
    return whole_call(
        functools.partial(attend_body, window),
        [((t, HEADS * HD), F32), ((keys, 2 * HD), BF)],
        (flag, branch_low, w_out, kept["q"], kept["kv"], pos[0][None, :], pos[1][:, None]),
        2 * t * HEADS * HD * (5 * keys + D),
    )


def back_body(
    flag, grad_q, grad_kv, qp, kp, heads, cosine, sine, x, dx, q_own, q_oth, gains,
    grad_x, gq_own, gq_oth, gain_zero, head_grads,
):
    first = flag[0] == 0
    cos, sin = cosine[...], sine[...]
    half = HD // 2

    def turned_back(d, u, gain):
        a, b = d[:, :half], d[:, half:]
        n = jnp.concatenate([a * cos + b * sin, b * cos - a * sin], axis=1)
        return rms_back(u, gain, n)

    parts = []
    query_gain = jnp.zeros((1, HD), F32)
    for head in range(HEADS):
        cols = slice(head * HD, (head + 1) * HD)
        du, dg = turned_back(grad_q[:, cols], qp[:, cols], heads[0:1, :])
        parts.append(du.astype(BF))
        query_gain = query_gain + dg
    dk, key_gain = turned_back(grad_kv[:, :HD], kp[...], heads[1:2, :])
    lo = jnp.concatenate(parts[:2] + [dk.astype(BF)], axis=1)
    hi = jnp.concatenate(parts[2:] + [grad_kv[:, HD:].astype(BF)], axis=1)
    own, oth = chosen(first, lo, hi)
    gq_own[...] = own
    gq_oth[...] = oth
    dz = last_dot(own, q_own[:, :QW]) + last_dot(oth, q_oth[:, :QW])
    part, gain = rms_back(x[...], gains[0:1, :], dz)
    grad_x[...] = dx[...] + part
    gain_zero[...] = gain
    head_grads[...] = jnp.concatenate([query_gain, key_gain], axis=0)


def backward_keys(full, kept, middle, grad_q, grad_kv, cosine, sine_table, flag):
    q_own, q_oth, gains, heads = full
    t = kept["x"].shape[0]
    grad_x, gq_own, gq_oth, gain_zero, head_grads = whole_call(
        back_body,
        [((t, D), F32), ((t, QW), BF), ((t, QW), BF), ((1, D), F32), ((2, HD), F32)],
        (
            flag, grad_q, grad_kv, kept["qp"], kept["kp"], heads, cosine, sine_table, kept["x"],
            middle, q_own, q_oth, gains,
        ),
        4 * t * D * QW,
    )
    wg_q = (t_dot(kept["normed"], gq_own).astype(BF), t_dot(kept["normed"], gq_oth).astype(BF))
    return grad_x, wg_q, gain_zero, head_grads


def halves(grad, count):
    return grad.reshape(count, 2, -1, grad.shape[-1])


def local(
    boundary, positions, w_query, w_key_value, w_out, w_gate_up, w_down, norm_gains, head_gains
):
    section = lax.axis_index("section")
    first = section == 0
    ctx_index = lax.axis_index("ctx")
    tokens = boundary.shape[3]
    seq_length = positions.shape[-1]
    nr = w_query.shape[1]
    hr = head_gains.shape[2]
    ro, rd = w_out.shape[1], w_down.shape[1]
    blocks = lax.axis_size("fsdp") * lax.axis_size("ctx")

    moved = exchange(lax.dynamic_index_in_dim(boundary[0, :, 0], 1 - section, 0, False), "section", 1)
    kept_in = lax.dynamic_index_in_dim(boundary[0, :, 0], section, 0, False)
    x0, cotangent = pick(first, kept_in, moved)
    x0 = x0.astype(F32)
    seq_places = lax.dynamic_index_in_dim(positions[:, 0], section, 0, False)
    near = [
        lax.dynamic_slice_in_dim(seq_places, (ctx_index ^ j) * tokens, tokens)
        for j in range(lax.axis_size("ctx"))
    ]
    pos = (near[0], jnp.concatenate(near))
    flag = section.astype(jnp.int32).reshape(1)

    gain_cols = jnp.concatenate(
        [
            norm_gains[0].T,
            jnp.pad(head_gains[0].T, ((0, nr - hr), (0, 0))),
            jnp.zeros((nr, 128 - 6), BF),
        ],
        axis=1,
    )
    cols = [
        jnp.concatenate(
            [
                w_query[0, :, h * QH : (h + 1) * QH],
                w_key_value[0, :, h * HD : (h + 1) * HD],
                gain_cols,
                w_gate_up[0, :, h * FF : (h + 1) * FF],
            ],
            axis=1,
        )
        for h in range(2)
    ]
    rows = [
        jnp.concatenate(
            [
                w_out[0, h * ro // 2 : (h + 1) * ro // 2],
                w_down[0, h * rd // 2 : (h + 1) * rd // 2],
            ],
            axis=0,
        )
        for h in range(2)
    ]
    col_keep, col_send = pick(first, cols[0], cols[1])
    row_keep, row_send = pick(first, rows[0], rows[1])
    col_recv = exchange(col_send, "section", 1)
    row_recv = exchange(row_send, "section", 1)
    layer_cols = pick(first, col_keep, col_recv)
    layer_rows = pick(first, row_keep, row_recv)

    def query_side(pair):
        q_own, q_oth = [v.reshape(blocks * nr, -1) for v in pair]
        gain_part = q_own[:, QW:].astype(F32)
        gains = gain_part[:, :4].T
        heads = gain_part[:, 4:6].reshape(blocks, nr, 2)[:, :hr].reshape(blocks * hr, 2).T
        return q_own, q_oth, gains, heads

    def feed_side(g_pair, b_pair, gains):
        g_own, g_oth = [v.reshape(blocks * nr, -1) for v in g_pair]
        b_lo, b_hi = pick(first, *b_pair)
        full_out = jnp.concatenate([b_lo[:, : ro // 2], b_hi[:, : ro // 2]], axis=1)
        full_down = jnp.concatenate([b_lo[:, ro // 2 :], b_hi[:, ro // 2 :]], axis=1)
        return g_own, g_oth, full_out.reshape(-1, D), full_down.reshape(-1, D), gains

    def reduce_cols(own, other):
        summed = own.astype(F32) + exchange(other, "section", 1).astype(F32)
        return summed.astype(BF).reshape(blocks, nr, -1)

    def reduce_rows(wg_out, wg_down):
        out_half, down_half = halves(wg_out, blocks), halves(wg_down, blocks)

        def part(index):
            return jnp.concatenate(
                [
                    lax.dynamic_index_in_dim(out_half, index, 1, False),
                    lax.dynamic_index_in_dim(down_half, index, 1, False),
                ],
                axis=1,
            )

        recv = exchange(part(1 - section), "section", 1)
        return (part(section).astype(F32) + recv.astype(F32)).astype(BF)

    def reduce_query(wg_q, norm_grads, head_grads):
        norm_part = jnp.concatenate(norm_grads, axis=0).T
        head_part = head_grads.T.reshape(blocks, hr, 2)
        head_part = jnp.pad(head_part, ((0, 0), (0, nr - hr), (0, 0))).reshape(blocks * nr, 2)
        fill = jnp.zeros((blocks * nr, 128 - 6), F32)
        cols = jnp.concatenate([norm_part, head_part, fill], axis=1).astype(BF)
        own = jnp.concatenate([wg_q[0], cols], axis=1)
        oth = jnp.concatenate([wg_q[1], cols], axis=1)
        return reduce_cols(own, oth)

    tables = [rope_tables(pos[0], base) for base in BASES]
    windows = (WIN, seq_length)

    gather0 = Gather(layer_cols[0], layer_rows[0])
    gather0.begin()
    gather0.rows_z()
    gather0.plane(0)
    gather0.plane(1)
    pairs0 = gather0.pairs()
    query0 = query_side(pairs0[0])
    kept0 = forward_keys(query0, x0, *tables[0], flag)
    whole1 = jnp.concatenate([layer_cols[1], pack_rows(layer_rows[1], nr)], axis=1)
    whole1 = lax.all_gather(whole1, GRID, axis=0)
    swapped = [v for pair in pairs0[1:] for v in pair]
    kept0["kv"], *held = tie(kept0["kv"], *swapped)
    feed0 = feed_side(held[:2], held[2:], query0[2])
    mixed = forward_attend(kept0, pos, windows[0], flag)
    y0 = forward_rest(feed0, kept0, mixed, flag).astype(BF)
    whole1, y0 = tie(whole1, y0)
    cuts = (0, QP, QP + FF, whole1.shape[-1])
    pairs1 = [whole1[..., i:j] for i, j in zip(cuts[:-1], cuts[1:])]
    pairs1 = [(v, exchange(v, "section", 1)) for v in pairs1]
    pairs1[2] = [unpack_rows(v, (ro + rd) // 2) for v in pairs1[2]]
    query1 = query_side(pairs1[0])
    kept1 = forward_keys(query1, y0.astype(F32), *tables[1], flag)
    feed1 = feed_side(*pairs1[1:], query1[2])
    mixed = forward_attend(kept1, pos, windows[1], flag)
    y1 = forward_rest(feed1, kept1, mixed, flag)

    middle1, branch1, wg_g, wg_out, wg_down, norm_grads = backward_feed(
        feed1, kept1, cotangent, flag
    )
    sum_g1 = reduce_cols(*wg_g)
    sum_b1 = reduce_rows(wg_out, wg_down)
    grad_q1, kv_blocks = backward_attend(feed1[2], kept1, branch1, pos, windows[1], flag)
    grad_q1, kv_blocks, sum_g1, sum_b1 = tie(grad_q1, kv_blocks, sum_g1, sum_b1)
    grad_kv = key_return(kv_blocks)
    sums1 = jnp.concatenate([sum_g1, pack_rows(sum_b1, nr)], axis=-1)
    grad_kv, sums1 = tie(grad_kv, sums1)
    sums1 = lax.psum_scatter(sums1, GRID, scatter_dimension=0).astype(F32)
    red_g1, red_b1 = sums1[:, :FF], unpack_rows(sums1[:, FF:], (ro + rd) // 2)
    grad1, wg_q, gain_zero, head_grads = backward_keys(
        query1, kept1, middle1, grad_q1, grad_kv, *tables[1], flag
    )
    grad1 = grad1.astype(BF)
    sum_q1 = reduce_query(wg_q, [gain_zero, norm_grads], head_grads)

    middle0, branch0, wg_g, wg_out, wg_down, norm_grads = backward_feed(
        feed0, kept0, grad1, flag
    )
    branch0, sum_q1 = tie(branch0, sum_q1)
    scat_q1 = Scatter(sum_q1, "xy")
    scat_q1.plane(0)
    sum_g0 = reduce_cols(*wg_g)
    sum_b0 = reduce_rows(wg_out, wg_down)
    grad_q0, kv_blocks = backward_attend(feed0[2], kept0, branch0, pos, windows[0], flag)
    grad_q0, kv_blocks, sum_g0, sum_b0, held0 = tie(
        grad_q0, kv_blocks, sum_g0, sum_b0, *scat_q1.values()
    )
    scat_q1.put([held0])
    grad_kv = key_return(kv_blocks)
    scat_b0 = Scatter(sum_b0, "yx")
    scat_b0.plane(0)
    grad_kv, sum_g0, held0 = tie(grad_kv, sum_g0, *scat_q1.values())
    scat_q1.put([held0])
    scat_g0 = Scatter(sum_g0, "both")
    scat_g0.plane(0)
    grad0, wg_q, gain_zero, head_grads = backward_keys(
        query0, kept0, middle0, grad_q0, grad_kv, *tables[0], flag
    )
    sum_q0 = reduce_query(wg_q, [gain_zero, norm_grads], head_grads)
    sum_q0, held1, *held = tie(sum_q0, *scat_q1.values(), *scat_g0.values())
    scat_q1.put([held1])
    scat_g0.put(held)
    scat_q0 = Scatter(sum_q0, "xy")
    scat_q0.plane(0)
    scat_g0.plane(1)
    scat_q0.plane(1)
    scat_q1.plane(1)
    red_q1 = scat_q1.along_z()
    red_q0, red_g0 = scat_q0.along_z(), scat_g0.along_z()
    scat_b0.plane(1)
    red_b0 = scat_b0.along_z()
    red_c0 = jnp.concatenate([red_q0, red_g0], axis=1)
    red_c1 = jnp.concatenate([red_q1, red_g1], axis=1)

    out_moved = exchange(jnp.where(first, y1, grad0), "section", 1)
    c_keep, c_send = pick(first, red_c0, red_c1)
    b_keep, b_send = pick(first, red_b0, red_b1)
    c_lo, c_hi = pick(first, c_keep, exchange(c_send, "section", 1))
    b_lo, b_hi = pick(first, b_keep, exchange(b_send, "section", 1))
    boundary_out = jnp.where(
        first, jnp.stack([grad0, out_moved]), jnp.stack([out_moved, y1])
    )[None, :, None]
    return (
        boundary_out,
        jnp.concatenate([c_lo[:, :QH], c_hi[:, :QH]], axis=1)[None],
        jnp.concatenate([c_lo[:, QH:QW], c_hi[:, QH:QW]], axis=1)[None],
        jnp.concatenate([b_lo[: ro // 2], b_hi[: ro // 2]], axis=0)[None],
        jnp.concatenate([c_lo[:, QP:], c_hi[:, QP:]], axis=1)[None],
        jnp.concatenate([b_lo[ro // 2 :], b_hi[ro // 2 :]], axis=0)[None],
        c_lo[:, QW : QW + 4].T[None],
        c_lo[:hr, QW + 4 : QW + 6].T[None],
    )


def solution(mesh):
    in_specs = (
        P("section", None, "fsdp", "ctx", None),
        P(None, "fsdp", None),
        P("section", ("fsdp", "ctx"), None),
        P("section", ("fsdp", "ctx"), None),
        P("section", ("fsdp", "ctx"), None),
        P("section", ("fsdp", "ctx"), None),
        P("section", ("fsdp", "ctx"), None),
        P("section", None, ("fsdp", "ctx")),
        P("section", None, ("fsdp", "ctx")),
    )
    out_specs = (
        P("section", None, "fsdp", "ctx", None),
        P("section", ("fsdp", "ctx"), None),
        P("section", ("fsdp", "ctx"), None),
        P("section", ("fsdp", "ctx"), None),
        P("section", ("fsdp", "ctx"), None),
        P("section", ("fsdp", "ctx"), None),
        P("section", None, ("fsdp", "ctx")),
        P("section", None, ("fsdp", "ctx")),
    )
    return jax.shard_map(local, mesh=mesh, in_specs=in_specs, out_specs=out_specs, check_vma=False)
```

```python
import functools
import math

import jax
import jax.numpy as jnp
from jax import lax
from jax.experimental import pallas as pl
from jax.experimental.pallas import tpu as pltpu
from jax.sharding import PartitionSpec as P

D = 640
FF = 2048
HEADS = 4
HD = 256
WIN = 512
MB = 2
QH = 2 * HD
QW = QH + HD
QP = QW + 128

EPS = 1e-06
BASES = (math.log(10000.0), math.log(1000000.0))
SCALE = 1.0 / math.sqrt(HD)
BF = jnp.bfloat16
GRID = ("fsdp", "ctx")
F32 = jnp.float32


def bits_of(axis):
    return (lax.axis_size(axis) - 1).bit_length()


def exchange(shard, axis, flip):
    pairs = [(i, i ^ flip) for i in range(lax.axis_size(axis))]
    return lax.ppermute(shard, axis, pairs)


def my_bit(axis, bit):
    return (lax.axis_index(axis) >> bit) & 1


def tie(*values):
    return lax.optimization_barrier(values)


def ctx_steps(order):
    count = bits_of("ctx")
    steps = [(bit, count - bit) for bit in range(count)]
    return steps if order == "xy" else steps[::-1]


def z_gather(block):
    count = lax.axis_size("fsdp")
    pieces = [block] + [exchange(block, "fsdp", j) for j in range(1, count)]
    me = lax.axis_index("fsdp")
    return jnp.stack([lax.select_n(me ^ at, *pieces) for at in range(count)])


def ctx_open(buf):
    return buf.reshape((buf.shape[0],) + (1,) * bits_of("ctx") + buf.shape[1:])


def ctx_gather(buf, steps):
    for bit, dim in steps:
        recv = exchange(buf, "ctx", 1 << bit)
        low = my_bit("ctx", bit) == 0
        buf = jnp.concatenate([jnp.where(low, buf, recv), jnp.where(low, recv, buf)], axis=dim)
    return buf


def ctx_close(buf, tail):
    return buf.reshape((-1,) + tail)


def ctx_scatter(buf, steps):
    for bit, dim in steps:
        mine = my_bit("ctx", bit)
        send = lax.dynamic_index_in_dim(buf, 1 - mine, dim, keepdims=True)
        keep = lax.dynamic_index_in_dim(buf, mine, dim, keepdims=True)
        recv = exchange(send, "ctx", 1 << bit)
        buf = (keep.astype(F32) + recv.astype(F32)).astype(BF)
    return buf


def z_scatter(buf):
    me = lax.axis_index("fsdp")
    total = lax.dynamic_index_in_dim(buf, me, 0, False).astype(F32)
    for j in range(1, lax.axis_size("fsdp")):
        part = lax.dynamic_index_in_dim(buf, me ^ j, 0, False)
        total = total + exchange(part, "fsdp", j).astype(F32)
    return total


def pack_rows(rows, height):
    lead, r = rows.shape[:-2], rows.shape[-2]
    if r % 8 or height % 8 or r * D // height % 128 or height // 8 != D // 128:
        return rows.reshape(lead + (height, r * D // height))
    tiles = rows.reshape(lead + (r // 8, 8, D // 128, 128))
    return jnp.swapaxes(tiles, -4, -2).reshape(lead + (height, r * D // height))


def unpack_rows(packed, r):
    lead, height = packed.shape[:-2], packed.shape[-2]
    if r % 8 or height % 8 or r * D // height % 128 or height // 8 != D // 128:
        return packed.reshape(lead + (r, D))
    tiles = packed.reshape(lead + (height // 8, 8, r // 8, 128))
    return jnp.swapaxes(tiles, -4, -2).reshape(lead + (r, D))


class Gather:
    ORDERS = ("yx", "xy", "yx")

    def __init__(self, cols, rows):
        self.q, self.g, self.b = cols[:, :QP], cols[:, QP:], rows

    def begin(self):
        q, g = z_gather(self.q), z_gather(self.g)
        half = g.shape[0] // 2
        self.parts = [ctx_open(v) for v in (q, g[:half], g[half:])]
        self.rows = ctx_gather(ctx_open(self.b[None]), ctx_steps("xy"))

    def plane(self, stage):
        done = []
        for v, order in zip(self.parts, self.ORDERS):
            steps = ctx_steps(order)
            done.append(ctx_gather(v, steps[:1] if stage == 0 else steps[1:]))
        self.parts = done

    def rows_z(self):
        self.rows = z_gather(self.rows[0])

    def pairs(self):
        q, g1, g2 = self.parts
        q = ctx_close(q, self.q.shape)
        b = ctx_close(self.rows, self.b.shape)
        g = jnp.concatenate([ctx_close(g1, self.g.shape), ctx_close(g2, self.g.shape)], axis=0)
        return [(v, exchange(v, "section", 1)) for v in (q, g, b)]


class Scatter:
    def __init__(self, blocks, order):
        fs, cb = lax.axis_size("fsdp"), bits_of("ctx")
        self.tail = blocks.shape[1:]
        buf = blocks.reshape((fs,) + (2,) * cb + self.tail)
        split = order == "both"
        self.parts = [(buf[: fs // 2], "xy"), (buf[fs // 2 :], "yx")] if split else [(buf, order)]

    def values(self):
        return [p[0] for p in self.parts]

    def put(self, values):
        self.parts = [(v, p[1]) for v, p in zip(values, self.parts)]

    def plane(self, stage):
        done = []
        for v, order in self.parts:
            steps = ctx_steps(order)
            done.append(ctx_scatter(v, steps[:1] if stage == 0 else steps[1:]))
        self.put(done)

    def ready_for_z(self):
        return jnp.concatenate([v.reshape((-1,) + self.tail) for v in self.values()], axis=0)

    def along_z(self):
        buf = jnp.concatenate([v.reshape((-1,) + self.tail) for v in self.values()], axis=0)
        return z_scatter(buf)


def rows_ring(blocks):
    count = lax.axis_size("fsdp")
    pairs = [(i, (i + 1) % count) for i in range(count)]
    me = lax.axis_index("fsdp")
    buf = blocks.reshape((count,) + (2,) * bits_of("ctx") + blocks.shape[1:])

    def block(back):
        return lax.dynamic_index_in_dim(buf, (me - back) % count, 0, False)

    total = block(1)
    for step in range(count - 1):
        recv = lax.ppermute(total, "fsdp", pairs)
        total = (recv.astype(F32) + block(step + 2).astype(F32)).astype(BF)
    return total


def rows_plane(buf):
    return ctx_scatter(buf[None], ctx_steps("yx")).reshape(buf.shape[-2:]).astype(F32)


def rope_tables(places, log_base):
    half_width = HD // 2
    inverse = jnp.exp(-log_base * (jnp.arange(half_width, dtype=F32) * (2.0 / HD)))
    angles = places.astype(F32)[:, None] * inverse[None, :]
    return (jnp.cos(angles), jnp.sin(angles))


def dot(a, b):
    return jnp.dot(a, b, preferred_element_type=F32)


def dot_t(a, b):
    return jnp.einsum("tc,dc->td", a, b, preferred_element_type=F32)


def t_dot(a, b):
    return jnp.einsum("ta,tb->ab", a, b, preferred_element_type=F32)


def pick(first, own, other):
    return jnp.where(first, own, other), jnp.where(first, other, own)


def key_exchange(keys_values):
    count = lax.axis_size("ctx")
    return [keys_values] + [exchange(keys_values, "ctx", j) for j in range(1, count)]


def key_return(blocks):
    count = lax.axis_size("ctx")
    blocks = jnp.split(blocks, count, axis=0)
    total = blocks[0]
    for j in range(1, count):
        total = total + exchange(blocks[j].astype(BF), "ctx", j).astype(F32)
    return total


def whole_call(body, outs, args, flops, window=None):
    vmem = pl.BlockSpec(memory_space=pltpu.VMEM)
    moved = sum(math.prod(v.shape) * v.dtype.itemsize for v in args)
    moved += sum(math.prod(s) * jnp.dtype(t).itemsize for s, t in outs)
    return pl.pallas_call(
        body,
        out_shape=[jax.ShapeDtypeStruct(s, t) for s, t in outs],
        in_specs=[pl.BlockSpec(memory_space=pltpu.SMEM)] + [vmem] * (len(args) - 1),
        out_specs=[vmem] * len(outs),
        compiler_params=pltpu.CompilerParams(vmem_limit_bytes=52 * 2**20),
        cost_estimate=pl.CostEstimate(
            flops=int(flops) // 64, bytes_accessed=int(moved) // 64, transcendentals=0
        ),
    )(*args)


def inverse_rms(u):
    return lax.rsqrt(jnp.mean(u * u, axis=-1, keepdims=True) + EPS)


def rms_back(u, gain, dz):
    r = inverse_rms(u)
    scaled = dz * gain
    mean = jnp.mean(u * scaled, axis=-1, keepdims=True)
    du = r * (scaled - u * (r * r * mean))
    return du, jnp.sum(dz * u * r, axis=0, keepdims=True)


def last_dot(a, b):
    return lax.dot_general(a, b, (((1,), (1,)), ((), ())), preferred_element_type=F32)


def first_dot(a, b):
    return lax.dot_general(a, b, (((0,), (0,)), ((), ())), preferred_element_type=F32)


def chosen(flag, own, other):
    return jnp.where(flag, own, other), jnp.where(flag, other, own)


def keys_body(flag, x, q_own, q_oth, gains, heads, cosine, sine, normed, qp, kp, q, kv):
    first = flag[0] == 0
    u = x[...]
    h = (u * inverse_rms(u) * gains[0:1, :]).astype(BF)
    normed[...] = h
    lo, hi = chosen(first, dot(h, q_own[:, :QW]), dot(h, q_oth[:, :QW]))
    cos, sin = cosine[...], sine[...]
    half = HD // 2

    def turned(v, gain, out, at):
        n = v * inverse_rms(v) * gain
        a, b = n[:, :half], n[:, half:]
        out[:, at : at + half] = (a * cos - b * sin).astype(BF)
        out[:, at + half : at + HD] = (b * cos + a * sin).astype(BF)

    for head in range(HEADS):
        part = (lo if head < 2 else hi)[:, (head % 2) * HD : (head % 2 + 1) * HD]
        qp[:, head * HD : (head + 1) * HD] = part
        turned(part, heads[0:1, :], q, head * HD)
    k_part = lo[:, QH:]
    kp[...] = k_part
    turned(k_part, heads[1:2, :], kv, 0)
    kv[:, HD:] = hi[:, QH:].astype(BF)


def forward_keys(full, x, cosine, sine_table, flag):
    q_own, q_oth, gains, heads = full
    t = x.shape[0]
    normed, qp, kp, q, kv = whole_call(
        keys_body,
        [((t, D), BF), ((t, HEADS * HD), F32), ((t, HD), F32), ((t, HEADS * HD), BF), ((t, 2 * HD), BF)],
        (flag, x, q_own, q_oth, gains, heads, cosine, sine_table),
        2 * t * D * 2 * QW,
    )
    all_kv = jnp.concatenate(key_exchange(kv), axis=0)
    return dict(x=x, normed=normed, qp=qp, kp=kp, q=q, kv=all_kv)


CHUNK = 512
GELU_A = math.sqrt(2.0 / math.pi)
GELU_B = 0.044715


def mix_body(window, flag, q, kv, pos_q, pos_k, mixed):
    reach = pos_q[...] - pos_k[...]
    allowed = (reach >= 0) & (reach < window)
    k, v = kv[:, :HD], kv[:, HD:]
    for head in range(HEADS):
        cols = slice(head * HD, (head + 1) * HD)
        s = jnp.where(allowed, last_dot(q[:, cols], k) * SCALE, -1e30)
        e = jnp.exp(s - jnp.max(s, axis=-1, keepdims=True))
        total = jnp.sum(e, axis=-1, keepdims=True)
        mixed[:, cols] = (dot(e.astype(BF), v) * (1.0 / total)).astype(BF)


def forward_attend(kept, pos, window, flag):
    t, keys = kept["x"].shape[0], kept["kv"].shape[0]
    return whole_call(
        functools.partial(mix_body, window),
        [((t, HEADS * HD), BF)],
        (flag, kept["q"], kept["kv"], pos[0][:, None], pos[1][None, :]),
        4 * t * HEADS * HD * keys,
    )[0]


def rest_body(
    flag, x, mixed, w_out, g_own, g_oth, w_down, gains,
    branch, middle, normed, gate_out, up_out, hidden, down, result,
):
    first = flag[0] == 0
    b = dot(mixed[...], w_out[...])
    branch[...] = b
    m = x[...] + b * inverse_rms(b) * gains[1:2, :]
    middle[...] = m
    h = (m * inverse_rms(m) * gains[2:3, :]).astype(BF)
    normed[...] = h
    total = jnp.zeros(m.shape, F32)
    for at in range(0, FF, CHUNK):
        cols = slice(at, at + CHUNK)
        gate, up = chosen(first, dot(h, g_own[:, cols]), dot(h, g_oth[:, cols]))
        gate_out[:, cols] = gate
        up_out[:, cols] = up
        th = jnp.tanh(GELU_A * (gate + GELU_B * gate * gate * gate))
        hid = (0.5 * gate * (1.0 + th) * up).astype(BF)
        hidden[:, cols] = hid
        total = total + dot(hid, w_down[cols, :])
    down[...] = total
    result[...] = m + total * inverse_rms(total) * gains[3:4, :]


def forward_rest(full, kept, mixed, flag):
    g_own, g_oth, w_out, w_down, gains = full
    t = kept["x"].shape[0]
    kept["mixed"] = mixed
    names = ("branch", "middle", "normed_two", "gate", "up", "hidden", "down", "result")
    outs = whole_call(
        rest_body,
        [
            ((t, D), F32), ((t, D), F32), ((t, D), BF), ((t, FF), F32),
            ((t, FF), F32), ((t, FF), BF), ((t, D), F32), ((t, D), F32),
        ],
        (flag, kept["x"], mixed, w_out, g_own, g_oth, w_down, gains),
        2 * t * HEADS * HD * D + 6 * t * D * FF,
    )
    kept.update(zip(names, outs))
    return kept["result"]


def feed_body(
    flag, dy, down, gate, up, middle, branch, gains, w_down, g_own, g_oth,
    grad_middle, grad_down, gu_own, gu_oth, grad_branch, gain_grads,
):
    first = flag[0] == 0
    dz = dy[...].astype(F32)
    df, gain_three = rms_back(down[...], gains[3:4, :], dz)
    df = df.astype(BF)
    grad_down[...] = df
    total = jnp.zeros(dz.shape, F32)
    for at in range(0, FF, CHUNK):
        cols = slice(at, at + CHUNK)
        dm = last_dot(df, w_down[cols, :])
        u = gate[:, cols]
        th = jnp.tanh(GELU_A * (u + GELU_B * u * u * u))
        plus = 0.5 * (1.0 + th)
        slope = plus + 0.5 * u * (1.0 - th * th) * (GELU_A * (1.0 + 3.0 * GELU_B * u * u))
        d_gate = (dm * up[:, cols] * slope).astype(BF)
        d_up = (dm * (u * plus)).astype(BF)
        own, oth = chosen(first, d_gate, d_up)
        gu_own[:, cols] = own
        gu_oth[:, cols] = oth
        total = total + last_dot(own, g_own[:, cols]) + last_dot(oth, g_oth[:, cols])
    part, gain_two = rms_back(middle[...], gains[2:3, :], total)
    dx = dz + part
    grad_middle[...] = dx
    da, gain_one = rms_back(branch[...], gains[1:2, :], dx)
    grad_branch[...] = da.astype(BF)
    gain_grads[...] = jnp.concatenate([gain_one, gain_two, gain_three], axis=0)


def backward_feed(full, kept, grad_result, flag):
    g_own, g_oth, w_out, w_down, gains = full
    t = kept["x"].shape[0]
    middle, down_low, gu_own, gu_oth, branch_low, gain_grads = whole_call(
        feed_body,
        [((t, D), F32), ((t, D), BF), ((t, FF), BF), ((t, FF), BF), ((t, D), BF), ((3, D), F32)],
        (
            flag, grad_result, kept["down"], kept["gate"], kept["up"], kept["middle"],
            kept["branch"], gains, w_down, g_own, g_oth,
        ),
        6 * t * D * FF,
    )
    wg_g = (t_dot(kept["normed_two"], gu_own), t_dot(kept["normed_two"], gu_oth).astype(BF))
    wg_out = t_dot(kept["mixed"], branch_low).astype(BF)
    wg_down = t_dot(kept["hidden"], down_low).astype(BF)
    return middle, branch_low, wg_g, wg_out, wg_down, gain_grads


def attend_body(window, flag, da, w_out, q, kv, pos_q, pos_k, grad_q, grad_kv):
    reach = pos_q[...] - pos_k[...]
    allowed = (reach >= 0) & (reach < window)
    k, v = kv[:, :HD], kv[:, HD:]
    for head in range(HEADS):
        cols = slice(head * HD, (head + 1) * HD)
        do = last_dot(da[...], w_out[cols, :]).astype(BF)
        s = jnp.where(allowed, last_dot(k, q[:, cols]) * SCALE, -1e30)
        e = jnp.exp(s - jnp.max(s, axis=0, keepdims=True))
        p = e * (1.0 / jnp.sum(e, axis=0, keepdims=True))
        dp = last_dot(v, do)
        inner = jnp.sum(p * dp, axis=0, keepdims=True)
        ds = (p * (dp - inner)).astype(BF)
        grad_q[:, cols] = first_dot(ds, k) * SCALE
        dk = dot(ds, q[:, cols]) * SCALE
        dv = dot(p.astype(BF), do)
        if head == 0:
            total_k, total_v = dk, dv
        else:
            total_k, total_v = total_k + dk, total_v + dv
    grad_kv[:, :HD] = total_k.astype(BF)
    grad_kv[:, HD:] = total_v.astype(BF)


def backward_attend(w_out, kept, branch_low, pos, window, flag):
    t, keys = kept["x"].shape[0], kept["kv"].shape[0]
    return whole_call(
        functools.partial(attend_body, window),
        [((t, HEADS * HD), F32), ((keys, 2 * HD), BF)],
        (flag, branch_low, w_out, kept["q"], kept["kv"], pos[0][None, :], pos[1][:, None]),
        2 * t * HEADS * HD * (5 * keys + D),
    )


def back_body(
    flag, grad_q, grad_kv, qp, kp, heads, cosine, sine, x, dx, q_own, q_oth, gains,
    grad_x, gq_own, gq_oth, gain_zero, head_grads,
):
    first = flag[0] == 0
    cos, sin = cosine[...], sine[...]
    half = HD // 2

    def turned_back(d, u, gain):
        a, b = d[:, :half], d[:, half:]
        n = jnp.concatenate([a * cos + b * sin, b * cos - a * sin], axis=1)
        return rms_back(u, gain, n)

    parts = []
    query_gain = jnp.zeros((1, HD), F32)
    for head in range(HEADS):
        cols = slice(head * HD, (head + 1) * HD)
        du, dg = turned_back(grad_q[:, cols], qp[:, cols], heads[0:1, :])
        parts.append(du.astype(BF))
        query_gain = query_gain + dg
    dk, key_gain = turned_back(grad_kv[:, :HD], kp[...], heads[1:2, :])
    lo = jnp.concatenate(parts[:2] + [dk.astype(BF)], axis=1)
    hi = jnp.concatenate(parts[2:] + [grad_kv[:, HD:].astype(BF)], axis=1)
    own, oth = chosen(first, lo, hi)
    gq_own[...] = own
    gq_oth[...] = oth
    dz = last_dot(own, q_own[:, :QW]) + last_dot(oth, q_oth[:, :QW])
    part, gain = rms_back(x[...], gains[0:1, :], dz)
    grad_x[...] = dx[...] + part
    gain_zero[...] = gain
    head_grads[...] = jnp.concatenate([query_gain, key_gain], axis=0)


def backward_keys(full, kept, middle, grad_q, grad_kv, cosine, sine_table, flag):
    q_own, q_oth, gains, heads = full
    t = kept["x"].shape[0]
    grad_x, gq_own, gq_oth, gain_zero, head_grads = whole_call(
        back_body,
        [((t, D), F32), ((t, QW), BF), ((t, QW), BF), ((1, D), F32), ((2, HD), F32)],
        (
            flag, grad_q, grad_kv, kept["qp"], kept["kp"], heads, cosine, sine_table, kept["x"],
            middle, q_own, q_oth, gains,
        ),
        4 * t * D * QW,
    )
    wg_q = (t_dot(kept["normed"], gq_own).astype(BF), t_dot(kept["normed"], gq_oth).astype(BF))
    return grad_x, wg_q, gain_zero, head_grads


def halves(grad, count):
    return grad.reshape(count, 2, -1, grad.shape[-1])


def local(
    boundary, positions, w_query, w_key_value, w_out, w_gate_up, w_down, norm_gains, head_gains
):
    section = lax.axis_index("section")
    first = section == 0
    ctx_index = lax.axis_index("ctx")
    tokens = boundary.shape[3]
    seq_length = positions.shape[-1]
    nr = w_query.shape[1]
    hr = head_gains.shape[2]
    ro, rd = w_out.shape[1], w_down.shape[1]
    blocks = lax.axis_size("fsdp") * lax.axis_size("ctx")

    moved = exchange(lax.dynamic_index_in_dim(boundary[0, :, 0], 1 - section, 0, False), "section", 1)
    kept_in = lax.dynamic_index_in_dim(boundary[0, :, 0], section, 0, False)
    x0, cotangent = pick(first, kept_in, moved)
    x0 = x0.astype(F32)
    seq_places = lax.dynamic_index_in_dim(positions[:, 0], section, 0, False)
    near = [
        lax.dynamic_slice_in_dim(seq_places, (ctx_index ^ j) * tokens, tokens)
        for j in range(lax.axis_size("ctx"))
    ]
    pos = (near[0], jnp.concatenate(near))
    flag = section.astype(jnp.int32).reshape(1)

    gain_cols = jnp.concatenate(
        [
            norm_gains[0].T,
            jnp.pad(head_gains[0].T, ((0, nr - hr), (0, 0))),
            jnp.zeros((nr, 128 - 6), BF),
        ],
        axis=1,
    )
    cols = [
        jnp.concatenate(
            [
                w_query[0, :, h * QH : (h + 1) * QH],
                w_key_value[0, :, h * HD : (h + 1) * HD],
                gain_cols,
                w_gate_up[0, :, h * FF : (h + 1) * FF],
            ],
            axis=1,
        )
        for h in range(2)
    ]
    rows = [
        jnp.concatenate(
            [
                w_out[0, h * ro // 2 : (h + 1) * ro // 2],
                w_down[0, h * rd // 2 : (h + 1) * rd // 2],
            ],
            axis=0,
        )
        for h in range(2)
    ]
    col_keep, col_send = pick(first, cols[0], cols[1])
    row_keep, row_send = pick(first, rows[0], rows[1])
    col_recv = exchange(col_send, "section", 1)
    row_recv = exchange(row_send, "section", 1)
    layer_cols = pick(first, col_keep, col_recv)
    layer_rows = pick(first, row_keep, row_recv)

    def query_side(pair):
        q_own, q_oth = [v.reshape(blocks * nr, -1) for v in pair]
        gain_part = q_own[:, QW:].astype(F32)
        gains = gain_part[:, :4].T
        heads = gain_part[:, 4:6].reshape(blocks, nr, 2)[:, :hr].reshape(blocks * hr, 2).T
        return q_own, q_oth, gains, heads

    def feed_side(g_pair, b_pair, gains):
        g_own, g_oth = [v.reshape(blocks * nr, -1) for v in g_pair]
        b_lo, b_hi = pick(first, *b_pair)
        full_out = jnp.concatenate([b_lo[:, : ro // 2], b_hi[:, : ro // 2]], axis=1)
        full_down = jnp.concatenate([b_lo[:, ro // 2 :], b_hi[:, ro // 2 :]], axis=1)
        return g_own, g_oth, full_out.reshape(-1, D), full_down.reshape(-1, D), gains

    def reduce_cols(own, other):
        summed = own.astype(F32) + exchange(other, "section", 1).astype(F32)
        return summed.astype(BF).reshape(blocks, nr, -1)

    def reduce_rows(wg_out, wg_down):
        out_half, down_half = halves(wg_out, blocks), halves(wg_down, blocks)

        def part(index):
            return jnp.concatenate(
                [
                    lax.dynamic_index_in_dim(out_half, index, 1, False),
                    lax.dynamic_index_in_dim(down_half, index, 1, False),
                ],
                axis=1,
            )

        recv = exchange(part(1 - section), "section", 1)
        return (part(section).astype(F32) + recv.astype(F32)).astype(BF)

    def reduce_query(wg_q, norm_grads, head_grads):
        norm_part = jnp.concatenate(norm_grads, axis=0).T
        head_part = head_grads.T.reshape(blocks, hr, 2)
        head_part = jnp.pad(head_part, ((0, 0), (0, nr - hr), (0, 0))).reshape(blocks * nr, 2)
        fill = jnp.zeros((blocks * nr, 128 - 6), F32)
        cols = jnp.concatenate([norm_part, head_part, fill], axis=1).astype(BF)
        own = jnp.concatenate([wg_q[0], cols], axis=1)
        oth = jnp.concatenate([wg_q[1], cols], axis=1)
        return reduce_cols(own, oth)

    tables = [rope_tables(pos[0], base) for base in BASES]
    windows = (WIN, seq_length)

    gather0 = Gather(layer_cols[0], layer_rows[0])
    gather0.begin()
    gather0.rows_z()
    gather0.plane(0)
    gather0.plane(1)
    pairs0 = gather0.pairs()
    query0 = query_side(pairs0[0])
    kept0 = forward_keys(query0, x0, *tables[0], flag)
    whole1 = jnp.concatenate([layer_cols[1], pack_rows(layer_rows[1], nr)], axis=1)
    whole1 = lax.all_gather(whole1, GRID, axis=0)
    swapped = [v for pair in pairs0[1:] for v in pair]
    kept0["kv"], *held = tie(kept0["kv"], *swapped)
    feed0 = feed_side(held[:2], held[2:], query0[2])
    mixed = forward_attend(kept0, pos, windows[0], flag)
    y0 = forward_rest(feed0, kept0, mixed, flag).astype(BF)
    whole1, y0 = tie(whole1, y0)
    cuts = (0, QP, QP + FF, whole1.shape[-1])
    pairs1 = [whole1[..., i:j] for i, j in zip(cuts[:-1], cuts[1:])]
    pairs1 = [(v, exchange(v, "section", 1)) for v in pairs1]
    pairs1[2] = [unpack_rows(v, (ro + rd) // 2) for v in pairs1[2]]
    query1 = query_side(pairs1[0])
    kept1 = forward_keys(query1, y0.astype(F32), *tables[1], flag)
    feed1 = feed_side(*pairs1[1:], query1[2])
    mixed = forward_attend(kept1, pos, windows[1], flag)
    y1 = forward_rest(feed1, kept1, mixed, flag)

    middle1, branch1, wg_g, wg_out, wg_down, norm_grads = backward_feed(
        feed1, kept1, cotangent, flag
    )
    sum_g1 = reduce_cols(*wg_g)
    sum_b1 = reduce_rows(wg_out, wg_down)
    grad_q1, kv_blocks = backward_attend(feed1[2], kept1, branch1, pos, windows[1], flag)
    grad_q1, kv_blocks, sum_g1, sum_b1 = tie(grad_q1, kv_blocks, sum_g1, sum_b1)
    grad_kv = key_return(kv_blocks)
    rows1 = rows_ring(sum_b1)
    grad_kv, sum_g1 = tie(grad_kv, sum_g1)
    scat_g1 = Scatter(sum_g1, "both")
    scat_g1.plane(0)
    grad1, wg_q, gain_zero, head_grads = backward_keys(
        query1, kept1, middle1, grad_q1, grad_kv, *tables[1], flag
    )
    grad1 = grad1.astype(BF)
    sum_q1 = reduce_query(wg_q, [gain_zero, norm_grads], head_grads)

    middle0, branch0, wg_g, wg_out, wg_down, norm_grads = backward_feed(
        feed0, kept0, grad1, flag
    )
    branch0, sum_q1, *held = tie(branch0, sum_q1, *scat_g1.values())
    scat_g1.put(held)
    scat_q1 = Scatter(sum_q1, "xy")
    scat_g1.plane(1)
    scat_q1.plane(0)
    sum_g0 = reduce_cols(*wg_g)
    sum_b0 = reduce_rows(wg_out, wg_down)
    grad_q0, kv_blocks = backward_attend(feed0[2], kept0, branch0, pos, windows[0], flag)
    grad_q0, kv_blocks, sum_g0, sum_b0, rows1, held0, *held = tie(
        grad_q0, kv_blocks, sum_g0, sum_b0, rows1, *scat_q1.values(), *scat_g1.values()
    )
    grad_kv = key_return(kv_blocks)
    rows0 = rows_ring(sum_b0)
    grad_kv, sum_g0, rows1, held0, *held = tie(grad_kv, sum_g0, rows1, held0, *held)
    scat_g0 = Scatter(sum_g0, "both")
    scat_g0.plane(0)
    grad0, wg_q, gain_zero, head_grads = backward_keys(
        query0, kept0, middle0, grad_q0, grad_kv, *tables[0], flag
    )
    sum_q0 = reduce_query(wg_q, [gain_zero, norm_grads], head_grads)
    sum_q0, rows1, held0, first_part, second_part, *held = tie(
        sum_q0, rows1, held0, *scat_g0.values(), *held
    )
    scat_g0.put([first_part, second_part])
    scat_q1.put([held0])
    scat_g1.put(held)
    scat_q0 = Scatter(sum_q0, "xy")
    scat_q0.plane(0)
    scat_g0.plane(1)
    scat_q1.plane(1)
    red_b1 = rows_plane(rows1)
    scat_q0.plane(1)
    red_c1 = z_scatter(
        jnp.concatenate([scat_q1.ready_for_z(), scat_g1.ready_for_z()], axis=-1)
    )
    red_q0, red_g0 = scat_q0.along_z(), scat_g0.along_z()
    red_b0 = rows_plane(rows0)
    red_c0 = jnp.concatenate([red_q0, red_g0], axis=1)

    out_moved = exchange(jnp.where(first, y1, grad0), "section", 1)
    c_keep, c_send = pick(first, red_c0, red_c1)
    b_keep, b_send = pick(first, red_b0, red_b1)
    c_lo, c_hi = pick(first, c_keep, exchange(c_send, "section", 1))
    b_lo, b_hi = pick(first, b_keep, exchange(b_send, "section", 1))
    boundary_out = jnp.where(
        first, jnp.stack([grad0, out_moved]), jnp.stack([out_moved, y1])
    )[None, :, None]
    return (
        boundary_out,
        jnp.concatenate([c_lo[:, :QH], c_hi[:, :QH]], axis=1)[None],
        jnp.concatenate([c_lo[:, QH:QW], c_hi[:, QH:QW]], axis=1)[None],
        jnp.concatenate([b_lo[: ro // 2], b_hi[: ro // 2]], axis=0)[None],
        jnp.concatenate([c_lo[:, QP:], c_hi[:, QP:]], axis=1)[None],
        jnp.concatenate([b_lo[ro // 2 :], b_hi[ro // 2 :]], axis=0)[None],
        c_lo[:, QW : QW + 4].T[None],
        c_lo[:hr, QW + 4 : QW + 6].T[None],
    )


def solution(mesh):
    in_specs = (
        P("section", None, "fsdp", "ctx", None),
        P(None, "fsdp", None),
        P("section", ("fsdp", "ctx"), None),
        P("section", ("fsdp", "ctx"), None),
        P("section", ("fsdp", "ctx"), None),
        P("section", ("fsdp", "ctx"), None),
        P("section", ("fsdp", "ctx"), None),
        P("section", None, ("fsdp", "ctx")),
        P("section", None, ("fsdp", "ctx")),
    )
    out_specs = (
        P("section", None, "fsdp", "ctx", None),
        P("section", ("fsdp", "ctx"), None),
        P("section", ("fsdp", "ctx"), None),
        P("section", ("fsdp", "ctx"), None),
        P("section", ("fsdp", "ctx"), None),
        P("section", ("fsdp", "ctx"), None),
        P("section", None, ("fsdp", "ctx")),
        P("section", None, ("fsdp", "ctx")),
    )
    return jax.shard_map(local, mesh=mesh, in_specs=in_specs, out_specs=out_specs, check_vma=False)
```

```python
import functools
import math

import jax
import jax.numpy as jnp
from jax import lax
from jax.experimental import pallas as pl
from jax.experimental.pallas import tpu as pltpu
from jax.sharding import PartitionSpec as P

D = 640
FF = 2048
HEADS = 4
HD = 256
WIN = 512
MB = 2
QH = 2 * HD
QW = QH + HD
QP = QW + 128

EPS = 1e-06
BASES = (math.log(10000.0), math.log(1000000.0))
SCALE = 1.0 / math.sqrt(HD)
BF = jnp.bfloat16
GRID = ("fsdp", "ctx")
F32 = jnp.float32


def bits_of(axis):
    return (lax.axis_size(axis) - 1).bit_length()


def exchange(shard, axis, flip):
    pairs = [(i, i ^ flip) for i in range(lax.axis_size(axis))]
    return lax.ppermute(shard, axis, pairs)


def my_bit(axis, bit):
    return (lax.axis_index(axis) >> bit) & 1


def tie(*values):
    return lax.optimization_barrier(values)


def ctx_steps(order):
    count = bits_of("ctx")
    steps = [(bit, count - bit) for bit in range(count)]
    return steps if order == "xy" else steps[::-1]


def z_gather(block):
    count = lax.axis_size("fsdp")
    pieces = [block] + [exchange(block, "fsdp", j) for j in range(1, count)]
    me = lax.axis_index("fsdp")
    return jnp.stack([lax.select_n(me ^ at, *pieces) for at in range(count)])


def ctx_open(buf):
    return buf.reshape((buf.shape[0],) + (1,) * bits_of("ctx") + buf.shape[1:])


def ctx_gather(buf, steps):
    for bit, dim in steps:
        recv = exchange(buf, "ctx", 1 << bit)
        low = my_bit("ctx", bit) == 0
        buf = jnp.concatenate([jnp.where(low, buf, recv), jnp.where(low, recv, buf)], axis=dim)
    return buf


def ctx_close(buf, tail):
    return buf.reshape((-1,) + tail)


def ctx_scatter(buf, steps):
    for bit, dim in steps:
        mine = my_bit("ctx", bit)
        send = lax.dynamic_index_in_dim(buf, 1 - mine, dim, keepdims=True)
        keep = lax.dynamic_index_in_dim(buf, mine, dim, keepdims=True)
        recv = exchange(send, "ctx", 1 << bit)
        buf = (keep.astype(F32) + recv.astype(F32)).astype(BF)
    return buf


def z_scatter(buf):
    me = lax.axis_index("fsdp")
    total = lax.dynamic_index_in_dim(buf, me, 0, False).astype(F32)
    for j in range(1, lax.axis_size("fsdp")):
        part = lax.dynamic_index_in_dim(buf, me ^ j, 0, False)
        total = total + exchange(part, "fsdp", j).astype(F32)
    return total


def pack_rows(rows, height):
    lead, r = rows.shape[:-2], rows.shape[-2]
    if r % 8 or height % 8 or r * D // height % 128 or height // 8 != D // 128:
        return rows.reshape(lead + (height, r * D // height))
    tiles = rows.reshape(lead + (r // 8, 8, D // 128, 128))
    return jnp.swapaxes(tiles, -4, -2).reshape(lead + (height, r * D // height))


def unpack_rows(packed, r):
    lead, height = packed.shape[:-2], packed.shape[-2]
    if r % 8 or height % 8 or r * D // height % 128 or height // 8 != D // 128:
        return packed.reshape(lead + (r, D))
    tiles = packed.reshape(lead + (height // 8, 8, r // 8, 128))
    return jnp.swapaxes(tiles, -4, -2).reshape(lead + (r, D))


class Gather:
    ORDERS = ("yx", "xy", "yx")

    def __init__(self, cols, rows):
        self.q, self.g, self.b = cols[:, :QP], cols[:, QP:], rows

    def begin(self):
        q, g = z_gather(self.q), z_gather(self.g)
        half = g.shape[0] // 2
        self.parts = [ctx_open(v) for v in (q, g[:half], g[half:])]
        self.rows = ctx_gather(ctx_open(self.b[None]), ctx_steps("xy"))

    def plane(self, stage):
        done = []
        for v, order in zip(self.parts, self.ORDERS):
            steps = ctx_steps(order)
            done.append(ctx_gather(v, steps[:1] if stage == 0 else steps[1:]))
        self.parts = done

    def rows_z(self):
        self.rows = z_gather(self.rows[0])

    def pairs(self):
        q, g1, g2 = self.parts
        q = ctx_close(q, self.q.shape)
        b = ctx_close(self.rows, self.b.shape)
        g = jnp.concatenate([ctx_close(g1, self.g.shape), ctx_close(g2, self.g.shape)], axis=0)
        return [(v, exchange(v, "section", 1)) for v in (q, g, b)]


class Scatter:
    def __init__(self, blocks, order):
        fs, cb = lax.axis_size("fsdp"), bits_of("ctx")
        self.tail = blocks.shape[1:]
        buf = blocks.reshape((fs,) + (2,) * cb + self.tail)
        split = order == "both"
        self.parts = [(buf[: fs // 2], "xy"), (buf[fs // 2 :], "yx")] if split else [(buf, order)]

    def values(self):
        return [p[0] for p in self.parts]

    def put(self, values):
        self.parts = [(v, p[1]) for v, p in zip(values, self.parts)]

    def plane(self, stage):
        done = []
        for v, order in self.parts:
            steps = ctx_steps(order)
            done.append(ctx_scatter(v, steps[:1] if stage == 0 else steps[1:]))
        self.put(done)

    def ready_for_z(self):
        return jnp.concatenate([v.reshape((-1,) + self.tail) for v in self.values()], axis=0)

    def along_z(self):
        buf = jnp.concatenate([v.reshape((-1,) + self.tail) for v in self.values()], axis=0)
        return z_scatter(buf)


def rows_ring(blocks):
    count = lax.axis_size("fsdp")
    pairs = [(i, (i + 1) % count) for i in range(count)]
    me = lax.axis_index("fsdp")
    buf = blocks.reshape((count,) + (2,) * bits_of("ctx") + blocks.shape[1:])

    def block(back):
        return lax.dynamic_index_in_dim(buf, (me - back) % count, 0, False)

    total = block(1)
    for step in range(count - 1):
        recv = lax.ppermute(total, "fsdp", pairs)
        total = (recv.astype(F32) + block(step + 2).astype(F32)).astype(BF)
    return total


def rows_plane(buf):
    return ctx_scatter(buf[None], ctx_steps("yx")).reshape(buf.shape[-2:]).astype(F32)


def rope_tables(places, log_base):
    half_width = HD // 2
    inverse = jnp.exp(-log_base * (jnp.arange(half_width, dtype=F32) * (2.0 / HD)))
    angles = places.astype(F32)[:, None] * inverse[None, :]
    return (jnp.cos(angles), jnp.sin(angles))


def dot(a, b):
    return jnp.dot(a, b, preferred_element_type=F32)


def dot_t(a, b):
    return jnp.einsum("tc,dc->td", a, b, preferred_element_type=F32)


def t_dot(a, b):
    return jnp.einsum("ta,tb->ab", a, b, preferred_element_type=F32)


def pick(first, own, other):
    return jnp.where(first, own, other), jnp.where(first, other, own)


def key_exchange(keys_values):
    count = lax.axis_size("ctx")
    return [keys_values] + [exchange(keys_values, "ctx", j) for j in range(1, count)]


def key_return(blocks):
    count = lax.axis_size("ctx")
    blocks = jnp.split(blocks, count, axis=0)
    total = blocks[0]
    for j in range(1, count):
        total = total + exchange(blocks[j].astype(BF), "ctx", j).astype(F32)
    return total


def whole_call(body, outs, args, flops, window=None):
    vmem = pl.BlockSpec(memory_space=pltpu.VMEM)
    moved = sum(math.prod(v.shape) * v.dtype.itemsize for v in args)
    moved += sum(math.prod(s) * jnp.dtype(t).itemsize for s, t in outs)
    return pl.pallas_call(
        body,
        out_shape=[jax.ShapeDtypeStruct(s, t) for s, t in outs],
        in_specs=[pl.BlockSpec(memory_space=pltpu.SMEM)] + [vmem] * (len(args) - 1),
        out_specs=[vmem] * len(outs),
        compiler_params=pltpu.CompilerParams(vmem_limit_bytes=52 * 2**20),
        cost_estimate=pl.CostEstimate(
            flops=int(flops) // 64, bytes_accessed=int(moved) // 64, transcendentals=0
        ),
    )(*args)


def inverse_rms(u):
    return lax.rsqrt(jnp.mean(u * u, axis=-1, keepdims=True) + EPS)


def rms_back(u, gain, dz):
    r = inverse_rms(u)
    scaled = dz * gain
    mean = jnp.mean(u * scaled, axis=-1, keepdims=True)
    du = r * (scaled - u * (r * r * mean))
    return du, jnp.sum(dz * u * r, axis=0, keepdims=True)


def last_dot(a, b):
    return lax.dot_general(a, b, (((1,), (1,)), ((), ())), preferred_element_type=F32)


def first_dot(a, b):
    return lax.dot_general(a, b, (((0,), (0,)), ((), ())), preferred_element_type=F32)


def chosen(flag, own, other):
    return jnp.where(flag, own, other), jnp.where(flag, other, own)


def keys_body(flag, x, q_own, q_oth, gains, heads, cosine, sine, normed, qp, kp, q, kv):
    first = flag[0] == 0
    u = x[...]
    h = (u * inverse_rms(u) * gains[0:1, :]).astype(BF)
    normed[...] = h
    lo, hi = chosen(first, dot(h, q_own[:, :QW]), dot(h, q_oth[:, :QW]))
    cos, sin = cosine[...], sine[...]
    half = HD // 2

    def turned(v, gain, out, at):
        n = v * inverse_rms(v) * gain
        a, b = n[:, :half], n[:, half:]
        out[:, at : at + half] = (a * cos - b * sin).astype(BF)
        out[:, at + half : at + HD] = (b * cos + a * sin).astype(BF)

    for head in range(HEADS):
        part = (lo if head < 2 else hi)[:, (head % 2) * HD : (head % 2 + 1) * HD]
        qp[:, head * HD : (head + 1) * HD] = part
        turned(part, heads[0:1, :], q, head * HD)
    k_part = lo[:, QH:]
    kp[...] = k_part
    turned(k_part, heads[1:2, :], kv, 0)
    kv[:, HD:] = hi[:, QH:].astype(BF)


def forward_keys(full, x, cosine, sine_table, flag):
    q_own, q_oth, gains, heads = full
    t = x.shape[0]
    normed, qp, kp, q, kv = whole_call(
        keys_body,
        [((t, D), BF), ((t, HEADS * HD), F32), ((t, HD), F32), ((t, HEADS * HD), BF), ((t, 2 * HD), BF)],
        (flag, x, q_own, q_oth, gains, heads, cosine, sine_table),
        2 * t * D * 2 * QW,
    )
    all_kv = jnp.concatenate(key_exchange(kv), axis=0)
    return dict(x=x, normed=normed, qp=qp, kp=kp, q=q, kv=all_kv)


CHUNK = 512
GELU_A = math.sqrt(2.0 / math.pi)
GELU_B = 0.044715


def mix_body(window, flag, q, kv, pos_q, pos_k, mixed):
    reach = pos_q[...] - pos_k[...]
    allowed = (reach >= 0) & (reach < window)
    k, v = kv[:, :HD], kv[:, HD:]
    for head in range(HEADS):
        cols = slice(head * HD, (head + 1) * HD)
        s = jnp.where(allowed, last_dot(q[:, cols], k) * SCALE, -1e30)
        e = jnp.exp(s - jnp.max(s, axis=-1, keepdims=True))
        total = jnp.sum(e, axis=-1, keepdims=True)
        mixed[:, cols] = (dot(e.astype(BF), v) * (1.0 / total)).astype(BF)


def forward_attend(kept, pos, window, flag):
    t, keys = kept["x"].shape[0], kept["kv"].shape[0]
    return whole_call(
        functools.partial(mix_body, window),
        [((t, HEADS * HD), BF)],
        (flag, kept["q"], kept["kv"], pos[0][:, None], pos[1][None, :]),
        4 * t * HEADS * HD * keys,
    )[0]


def rest_body(
    flag, x, mixed, w_out, g_own, g_oth, w_down, gains,
    branch, middle, normed, gate_out, up_out, hidden, down, result,
):
    first = flag[0] == 0
    b = dot(mixed[...], w_out[...])
    branch[...] = b
    m = x[...] + b * inverse_rms(b) * gains[1:2, :]
    middle[...] = m
    h = (m * inverse_rms(m) * gains[2:3, :]).astype(BF)
    normed[...] = h
    total = jnp.zeros(m.shape, F32)
    for at in range(0, FF, CHUNK):
        cols = slice(at, at + CHUNK)
        gate, up = chosen(first, dot(h, g_own[:, cols]), dot(h, g_oth[:, cols]))
        gate_out[:, cols] = gate
        up_out[:, cols] = up
        th = jnp.tanh(GELU_A * (gate + GELU_B * gate * gate * gate))
        hid = (0.5 * gate * (1.0 + th) * up).astype(BF)
        hidden[:, cols] = hid
        total = total + dot(hid, w_down[cols, :])
    down[...] = total
    result[...] = m + total * inverse_rms(total) * gains[3:4, :]


def forward_rest(full, kept, mixed, flag):
    g_own, g_oth, w_out, w_down, gains = full
    t = kept["x"].shape[0]
    kept["mixed"] = mixed
    names = ("branch", "middle", "normed_two", "gate", "up", "hidden", "down", "result")
    outs = whole_call(
        rest_body,
        [
            ((t, D), F32), ((t, D), F32), ((t, D), BF), ((t, FF), F32),
            ((t, FF), F32), ((t, FF), BF), ((t, D), F32), ((t, D), F32),
        ],
        (flag, kept["x"], mixed, w_out, g_own, g_oth, w_down, gains),
        2 * t * HEADS * HD * D + 6 * t * D * FF,
    )
    kept.update(zip(names, outs))
    return kept["result"]


def feed_body(
    flag, dy, down, gate, up, middle, branch, gains, w_down, g_own, g_oth,
    grad_middle, grad_down, gu_own, gu_oth, grad_branch, gain_grads,
):
    first = flag[0] == 0
    dz = dy[...].astype(F32)
    df, gain_three = rms_back(down[...], gains[3:4, :], dz)
    df = df.astype(BF)
    grad_down[...] = df
    total = jnp.zeros(dz.shape, F32)
    for at in range(0, FF, CHUNK):
        cols = slice(at, at + CHUNK)
        dm = last_dot(df, w_down[cols, :])
        u = gate[:, cols]
        th = jnp.tanh(GELU_A * (u + GELU_B * u * u * u))
        plus = 0.5 * (1.0 + th)
        slope = plus + 0.5 * u * (1.0 - th * th) * (GELU_A * (1.0 + 3.0 * GELU_B * u * u))
        d_gate = (dm * up[:, cols] * slope).astype(BF)
        d_up = (dm * (u * plus)).astype(BF)
        own, oth = chosen(first, d_gate, d_up)
        gu_own[:, cols] = own
        gu_oth[:, cols] = oth
        total = total + last_dot(own, g_own[:, cols]) + last_dot(oth, g_oth[:, cols])
    part, gain_two = rms_back(middle[...], gains[2:3, :], total)
    dx = dz + part
    grad_middle[...] = dx
    da, gain_one = rms_back(branch[...], gains[1:2, :], dx)
    grad_branch[...] = da.astype(BF)
    gain_grads[...] = jnp.concatenate([gain_one, gain_two, gain_three], axis=0)


def backward_feed(full, kept, grad_result, flag):
    g_own, g_oth, w_out, w_down, gains = full
    t = kept["x"].shape[0]
    middle, down_low, gu_own, gu_oth, branch_low, gain_grads = whole_call(
        feed_body,
        [((t, D), F32), ((t, D), BF), ((t, FF), BF), ((t, FF), BF), ((t, D), BF), ((3, D), F32)],
        (
            flag, grad_result, kept["down"], kept["gate"], kept["up"], kept["middle"],
            kept["branch"], gains, w_down, g_own, g_oth,
        ),
        6 * t * D * FF,
    )
    wg_g = (t_dot(kept["normed_two"], gu_own), t_dot(kept["normed_two"], gu_oth).astype(BF))
    wg_out = t_dot(kept["mixed"], branch_low).astype(BF)
    wg_down = t_dot(kept["hidden"], down_low).astype(BF)
    return middle, branch_low, wg_g, wg_out, wg_down, gain_grads


def attend_body(window, flag, da, w_out, q, kv, pos_q, pos_k, grad_q, grad_kv):
    reach = pos_q[...] - pos_k[...]
    allowed = (reach >= 0) & (reach < window)
    k, v = kv[:, :HD], kv[:, HD:]
    for head in range(HEADS):
        cols = slice(head * HD, (head + 1) * HD)
        do = last_dot(da[...], w_out[cols, :]).astype(BF)
        s = jnp.where(allowed, last_dot(k, q[:, cols]) * SCALE, -1e30)
        e = jnp.exp(s - jnp.max(s, axis=0, keepdims=True))
        p = e * (1.0 / jnp.sum(e, axis=0, keepdims=True))
        dp = last_dot(v, do)
        inner = jnp.sum(p * dp, axis=0, keepdims=True)
        ds = (p * (dp - inner)).astype(BF)
        grad_q[:, cols] = first_dot(ds, k) * SCALE
        dk = dot(ds, q[:, cols]) * SCALE
        dv = dot(p.astype(BF), do)
        if head == 0:
            total_k, total_v = dk, dv
        else:
            total_k, total_v = total_k + dk, total_v + dv
    grad_kv[:, :HD] = total_k.astype(BF)
    grad_kv[:, HD:] = total_v.astype(BF)


def backward_attend(w_out, kept, branch_low, pos, window, flag):
    t, keys = kept["x"].shape[0], kept["kv"].shape[0]
    return whole_call(
        functools.partial(attend_body, window),
        [((t, HEADS * HD), F32), ((keys, 2 * HD), BF)],
        (flag, branch_low, w_out, kept["q"], kept["kv"], pos[0][None, :], pos[1][:, None]),
        2 * t * HEADS * HD * (5 * keys + D),
    )


def back_body(
    flag, grad_q, grad_kv, qp, kp, heads, cosine, sine, x, dx, q_own, q_oth, gains,
    grad_x, gq_own, gq_oth, gain_zero, head_grads,
):
    first = flag[0] == 0
    cos, sin = cosine[...], sine[...]
    half = HD // 2

    def turned_back(d, u, gain):
        a, b = d[:, :half], d[:, half:]
        n = jnp.concatenate([a * cos + b * sin, b * cos - a * sin], axis=1)
        return rms_back(u, gain, n)

    parts = []
    query_gain = jnp.zeros((1, HD), F32)
    for head in range(HEADS):
        cols = slice(head * HD, (head + 1) * HD)
        du, dg = turned_back(grad_q[:, cols], qp[:, cols], heads[0:1, :])
        parts.append(du.astype(BF))
        query_gain = query_gain + dg
    dk, key_gain = turned_back(grad_kv[:, :HD], kp[...], heads[1:2, :])
    lo = jnp.concatenate(parts[:2] + [dk.astype(BF)], axis=1)
    hi = jnp.concatenate(parts[2:] + [grad_kv[:, HD:].astype(BF)], axis=1)
    own, oth = chosen(first, lo, hi)
    gq_own[...] = own
    gq_oth[...] = oth
    dz = last_dot(own, q_own[:, :QW]) + last_dot(oth, q_oth[:, :QW])
    part, gain = rms_back(x[...], gains[0:1, :], dz)
    grad_x[...] = dx[...] + part
    gain_zero[...] = gain
    head_grads[...] = jnp.concatenate([query_gain, key_gain], axis=0)


def backward_keys(full, kept, middle, grad_q, grad_kv, cosine, sine_table, flag):
    q_own, q_oth, gains, heads = full
    t = kept["x"].shape[0]
    grad_x, gq_own, gq_oth, gain_zero, head_grads = whole_call(
        back_body,
        [((t, D), F32), ((t, QW), BF), ((t, QW), BF), ((1, D), F32), ((2, HD), F32)],
        (
            flag, grad_q, grad_kv, kept["qp"], kept["kp"], heads, cosine, sine_table, kept["x"],
            middle, q_own, q_oth, gains,
        ),
        4 * t * D * QW,
    )
    wg_q = (t_dot(kept["normed"], gq_own).astype(BF), t_dot(kept["normed"], gq_oth).astype(BF))
    return grad_x, wg_q, gain_zero, head_grads


def halves(grad, count):
    return grad.reshape(count, 2, -1, grad.shape[-1])


def local(
    boundary, positions, w_query, w_key_value, w_out, w_gate_up, w_down, norm_gains, head_gains
):
    section = lax.axis_index("section")
    first = section == 0
    ctx_index = lax.axis_index("ctx")
    tokens = boundary.shape[3]
    seq_length = positions.shape[-1]
    nr = w_query.shape[1]
    hr = head_gains.shape[2]
    ro, rd = w_out.shape[1], w_down.shape[1]
    blocks = lax.axis_size("fsdp") * lax.axis_size("ctx")

    moved = exchange(lax.dynamic_index_in_dim(boundary[0, :, 0], 1 - section, 0, False), "section", 1)
    kept_in = lax.dynamic_index_in_dim(boundary[0, :, 0], section, 0, False)
    x0, cotangent = pick(first, kept_in, moved)
    x0 = x0.astype(F32)
    seq_places = lax.dynamic_index_in_dim(positions[:, 0], section, 0, False)
    near = [
        lax.dynamic_slice_in_dim(seq_places, (ctx_index ^ j) * tokens, tokens)
        for j in range(lax.axis_size("ctx"))
    ]
    pos = (near[0], jnp.concatenate(near))
    flag = section.astype(jnp.int32).reshape(1)

    gain_cols = jnp.concatenate(
        [
            norm_gains[0].T,
            jnp.pad(head_gains[0].T, ((0, nr - hr), (0, 0))),
            jnp.zeros((nr, 128 - 6), BF),
        ],
        axis=1,
    )
    cols = [
        jnp.concatenate(
            [
                w_query[0, :, h * QH : (h + 1) * QH],
                w_key_value[0, :, h * HD : (h + 1) * HD],
                gain_cols,
                w_gate_up[0, :, h * FF : (h + 1) * FF],
            ],
            axis=1,
        )
        for h in range(2)
    ]
    rows = [
        jnp.concatenate(
            [
                w_out[0, h * ro // 2 : (h + 1) * ro // 2],
                w_down[0, h * rd // 2 : (h + 1) * rd // 2],
            ],
            axis=0,
        )
        for h in range(2)
    ]
    col_keep, col_send = pick(first, cols[0], cols[1])
    row_keep, row_send = pick(first, rows[0], rows[1])
    col_recv = exchange(col_send, "section", 1)
    row_recv = exchange(row_send, "section", 1)
    layer_cols = pick(first, col_keep, col_recv)
    layer_rows = pick(first, row_keep, row_recv)

    def query_side(pair):
        q_own, q_oth = [v.reshape(blocks * nr, -1) for v in pair]
        gain_part = q_own[:, QW:].astype(F32)
        gains = gain_part[:, :4].T
        heads = gain_part[:, 4:6].reshape(blocks, nr, 2)[:, :hr].reshape(blocks * hr, 2).T
        return q_own, q_oth, gains, heads

    def feed_side(g_pair, b_pair, gains):
        g_own, g_oth = [v.reshape(blocks * nr, -1) for v in g_pair]
        b_lo, b_hi = pick(first, *b_pair)
        full_out = jnp.concatenate([b_lo[:, : ro // 2], b_hi[:, : ro // 2]], axis=1)
        full_down = jnp.concatenate([b_lo[:, ro // 2 :], b_hi[:, ro // 2 :]], axis=1)
        return g_own, g_oth, full_out.reshape(-1, D), full_down.reshape(-1, D), gains

    def reduce_cols(own, other):
        summed = own.astype(F32) + exchange(other, "section", 1).astype(F32)
        return summed.astype(BF).reshape(blocks, nr, -1)

    def reduce_rows(wg_out, wg_down):
        out_half, down_half = halves(wg_out, blocks), halves(wg_down, blocks)

        def part(index):
            return jnp.concatenate(
                [
                    lax.dynamic_index_in_dim(out_half, index, 1, False),
                    lax.dynamic_index_in_dim(down_half, index, 1, False),
                ],
                axis=1,
            )

        recv = exchange(part(1 - section), "section", 1)
        return (part(section).astype(F32) + recv.astype(F32)).astype(BF)

    def reduce_query(wg_q, norm_grads, head_grads):
        norm_part = jnp.concatenate(norm_grads, axis=0).T
        head_part = head_grads.T.reshape(blocks, hr, 2)
        head_part = jnp.pad(head_part, ((0, 0), (0, nr - hr), (0, 0))).reshape(blocks * nr, 2)
        fill = jnp.zeros((blocks * nr, 128 - 6), F32)
        cols = jnp.concatenate([norm_part, head_part, fill], axis=1).astype(BF)
        own = jnp.concatenate([wg_q[0], cols], axis=1)
        oth = jnp.concatenate([wg_q[1], cols], axis=1)
        return reduce_cols(own, oth)

    tables = [rope_tables(pos[0], base) for base in BASES]
    windows = (WIN, seq_length)

    gather0 = Gather(layer_cols[0], layer_rows[0])
    gather0.begin()
    gather0.rows_z()
    gather0.plane(0)
    gather0.plane(1)
    pairs0 = gather0.pairs()
    query0 = query_side(pairs0[0])
    kept0 = forward_keys(query0, x0, *tables[0], flag)
    whole1 = jnp.concatenate([layer_cols[1], pack_rows(layer_rows[1], nr)], axis=1)
    whole1 = lax.all_gather(whole1, GRID, axis=0)
    swapped = [v for pair in pairs0[1:] for v in pair]
    kept0["kv"], *held = tie(kept0["kv"], *swapped)
    feed0 = feed_side(held[:2], held[2:], query0[2])
    mixed = forward_attend(kept0, pos, windows[0], flag)
    y0 = forward_rest(feed0, kept0, mixed, flag).astype(BF)
    whole1, y0 = tie(whole1, y0)
    query_part = whole1[..., :QP]
    query_pair = tie(query_part, exchange(query_part, "section", 1), whole1)
    whole1 = query_pair[2]
    pairs1 = [whole1[..., QP : QP + FF], whole1[..., QP + FF :]]
    pairs1 = [query_pair[:2]] + [(v, exchange(v, "section", 1)) for v in pairs1]
    pairs1[2] = [unpack_rows(v, (ro + rd) // 2) for v in pairs1[2]]
    query1 = query_side(pairs1[0])
    kept1 = forward_keys(query1, y0.astype(F32), *tables[1], flag)
    feed1 = feed_side(*pairs1[1:], query1[2])
    mixed = forward_attend(kept1, pos, windows[1], flag)
    y1 = forward_rest(feed1, kept1, mixed, flag)

    middle1, branch1, wg_g, wg_out, wg_down, norm_grads = backward_feed(
        feed1, kept1, cotangent, flag
    )
    sum_g1 = reduce_cols(*wg_g)
    sum_b1 = reduce_rows(wg_out, wg_down)
    grad_q1, kv_blocks = backward_attend(feed1[2], kept1, branch1, pos, windows[1], flag)
    grad_q1, kv_blocks, sum_g1, sum_b1 = tie(grad_q1, kv_blocks, sum_g1, sum_b1)
    grad_kv = key_return(kv_blocks)
    red_b1 = lax.psum_scatter(sum_b1, GRID, scatter_dimension=0).astype(F32)
    grad_kv, sum_g1 = tie(grad_kv, sum_g1)
    scat_g1 = Scatter(sum_g1, "both")
    scat_g1.plane(0)
    grad1, wg_q, gain_zero, head_grads = backward_keys(
        query1, kept1, middle1, grad_q1, grad_kv, *tables[1], flag
    )
    grad1 = grad1.astype(BF)
    sum_q1 = reduce_query(wg_q, [gain_zero, norm_grads], head_grads)

    middle0, branch0, wg_g, wg_out, wg_down, norm_grads = backward_feed(
        feed0, kept0, grad1, flag
    )
    branch0, sum_q1, *held = tie(branch0, sum_q1, *scat_g1.values())
    scat_g1.put(held)
    scat_q1 = Scatter(sum_q1, "xy")
    scat_g1.plane(1)
    red_g1 = scat_g1.along_z()
    scat_q1.plane(0)
    sum_g0 = reduce_cols(*wg_g)
    sum_b0 = reduce_rows(wg_out, wg_down)
    grad_q0, kv_blocks = backward_attend(feed0[2], kept0, branch0, pos, windows[0], flag)
    grad_q0, kv_blocks, sum_g0, sum_b0, red_g1 = tie(
        grad_q0, kv_blocks, sum_g0, sum_b0, red_g1
    )
    grad_kv = key_return(kv_blocks)
    rows0 = rows_ring(sum_b0)
    grad_kv, sum_g0, held0 = tie(grad_kv, sum_g0, *scat_q1.values())
    scat_g0 = Scatter(sum_g0, "both")
    scat_g0.plane(0)
    grad0, wg_q, gain_zero, head_grads = backward_keys(
        query0, kept0, middle0, grad_q0, grad_kv, *tables[0], flag
    )
    sum_q0 = reduce_query(wg_q, [gain_zero, norm_grads], head_grads)
    sum_q0, held0, *held = tie(sum_q0, held0, *scat_g0.values())
    scat_g0.put(held)
    scat_q1.put([held0])
    scat_q0 = Scatter(sum_q0, "xy")
    scat_q0.plane(0)
    scat_g0.plane(1)
    scat_q1.plane(1)
    scat_q0.plane(1)
    red_q1 = scat_q1.along_z()
    red_q0, red_g0 = scat_q0.along_z(), scat_g0.along_z()
    red_b0 = rows_plane(rows0)
    red_c0 = jnp.concatenate([red_q0, red_g0], axis=1)
    red_c1 = jnp.concatenate([red_q1, red_g1], axis=1)

    out_moved = exchange(jnp.where(first, y1, grad0), "section", 1)
    c_keep, c_send = pick(first, red_c0, red_c1)
    b_keep, b_send = pick(first, red_b0, red_b1)
    c_lo, c_hi = pick(first, c_keep, exchange(c_send, "section", 1))
    b_lo, b_hi = pick(first, b_keep, exchange(b_send, "section", 1))
    boundary_out = jnp.where(
        first, jnp.stack([grad0, out_moved]), jnp.stack([out_moved, y1])
    )[None, :, None]
    return (
        boundary_out,
        jnp.concatenate([c_lo[:, :QH], c_hi[:, :QH]], axis=1)[None],
        jnp.concatenate([c_lo[:, QH:QW], c_hi[:, QH:QW]], axis=1)[None],
        jnp.concatenate([b_lo[: ro // 2], b_hi[: ro // 2]], axis=0)[None],
        jnp.concatenate([c_lo[:, QP:], c_hi[:, QP:]], axis=1)[None],
        jnp.concatenate([b_lo[ro // 2 :], b_hi[ro // 2 :]], axis=0)[None],
        c_lo[:, QW : QW + 4].T[None],
        c_lo[:hr, QW + 4 : QW + 6].T[None],
    )


def solution(mesh):
    in_specs = (
        P("section", None, "fsdp", "ctx", None),
        P(None, "fsdp", None),
        P("section", ("fsdp", "ctx"), None),
        P("section", ("fsdp", "ctx"), None),
        P("section", ("fsdp", "ctx"), None),
        P("section", ("fsdp", "ctx"), None),
        P("section", ("fsdp", "ctx"), None),
        P("section", None, ("fsdp", "ctx")),
        P("section", None, ("fsdp", "ctx")),
    )
    out_specs = (
        P("section", None, "fsdp", "ctx", None),
        P("section", ("fsdp", "ctx"), None),
        P("section", ("fsdp", "ctx"), None),
        P("section", ("fsdp", "ctx"), None),
        P("section", ("fsdp", "ctx"), None),
        P("section", ("fsdp", "ctx"), None),
        P("section", None, ("fsdp", "ctx")),
        P("section", None, ("fsdp", "ctx")),
    )
    return jax.shard_map(local, mesh=mesh, in_specs=in_specs, out_specs=out_specs, check_vma=False)
```

```python
import functools
import math

import jax
import jax.numpy as jnp
from jax import lax
from jax.experimental import pallas as pl
from jax.experimental.pallas import tpu as pltpu
from jax.sharding import PartitionSpec as P

D = 640
FF = 2048
HEADS = 4
HD = 256
WIN = 512
MB = 2
QH = 2 * HD
QW = QH + HD
QP = QW + 128

EPS = 1e-06
BASES = (math.log(10000.0), math.log(1000000.0))
SCALE = 1.0 / math.sqrt(HD)
BF = jnp.bfloat16
GRID = ("fsdp", "ctx")
F32 = jnp.float32


def bits_of(axis):
    return (lax.axis_size(axis) - 1).bit_length()


def exchange(shard, axis, flip):
    pairs = [(i, i ^ flip) for i in range(lax.axis_size(axis))]
    return lax.ppermute(shard, axis, pairs)


def my_bit(axis, bit):
    return (lax.axis_index(axis) >> bit) & 1


def tie(*values):
    return lax.optimization_barrier(values)


def ctx_steps(order):
    count = bits_of("ctx")
    steps = [(bit, count - bit) for bit in range(count)]
    return steps if order == "xy" else steps[::-1]


def z_gather(block):
    count = lax.axis_size("fsdp")
    pieces = [block] + [exchange(block, "fsdp", j) for j in range(1, count)]
    me = lax.axis_index("fsdp")
    return jnp.stack([lax.select_n(me ^ at, *pieces) for at in range(count)])


def ctx_open(buf):
    return buf.reshape((buf.shape[0],) + (1,) * bits_of("ctx") + buf.shape[1:])


def ctx_gather(buf, steps):
    for bit, dim in steps:
        recv = exchange(buf, "ctx", 1 << bit)
        low = my_bit("ctx", bit) == 0
        buf = jnp.concatenate([jnp.where(low, buf, recv), jnp.where(low, recv, buf)], axis=dim)
    return buf


def ctx_close(buf, tail):
    return buf.reshape((-1,) + tail)


def ctx_scatter(buf, steps):
    for bit, dim in steps:
        mine = my_bit("ctx", bit)
        send = lax.dynamic_index_in_dim(buf, 1 - mine, dim, keepdims=True)
        keep = lax.dynamic_index_in_dim(buf, mine, dim, keepdims=True)
        recv = exchange(send, "ctx", 1 << bit)
        buf = (keep.astype(F32) + recv.astype(F32)).astype(BF)
    return buf


def z_scatter(buf):
    me = lax.axis_index("fsdp")
    total = lax.dynamic_index_in_dim(buf, me, 0, False).astype(F32)
    for j in range(1, lax.axis_size("fsdp")):
        part = lax.dynamic_index_in_dim(buf, me ^ j, 0, False)
        total = total + exchange(part, "fsdp", j).astype(F32)
    return total


def pack_rows(rows, height):
    lead, r = rows.shape[:-2], rows.shape[-2]
    if r % 8 or height % 8 or r * D // height % 128 or height // 8 != D // 128:
        return rows.reshape(lead + (height, r * D // height))
    tiles = rows.reshape(lead + (r // 8, 8, D // 128, 128))
    return jnp.swapaxes(tiles, -4, -2).reshape(lead + (height, r * D // height))


def unpack_rows(packed, r):
    lead, height = packed.shape[:-2], packed.shape[-2]
    if r % 8 or height % 8 or r * D // height % 128 or height // 8 != D // 128:
        return packed.reshape(lead + (r, D))
    tiles = packed.reshape(lead + (height // 8, 8, r // 8, 128))
    return jnp.swapaxes(tiles, -4, -2).reshape(lead + (r, D))


class Gather:
    ORDERS = ("yx", "xy", "yx")

    def __init__(self, cols, rows):
        self.q, self.g, self.b = cols[:, :QP], cols[:, QP:], rows

    def begin(self):
        q, g = z_gather(self.q), z_gather(self.g)
        half = g.shape[0] // 2
        self.parts = [ctx_open(v) for v in (q, g[:half], g[half:])]
        self.rows = ctx_gather(ctx_open(self.b[None]), ctx_steps("xy"))

    def plane(self, stage):
        done = []
        for v, order in zip(self.parts, self.ORDERS):
            steps = ctx_steps(order)
            done.append(ctx_gather(v, steps[:1] if stage == 0 else steps[1:]))
        self.parts = done

    def rows_z(self):
        self.rows = z_gather(self.rows[0])

    def pairs(self):
        q, g1, g2 = self.parts
        q = ctx_close(q, self.q.shape)
        b = ctx_close(self.rows, self.b.shape)
        g = jnp.concatenate([ctx_close(g1, self.g.shape), ctx_close(g2, self.g.shape)], axis=0)
        return [(v, exchange(v, "section", 1)) for v in (q, g, b)]


class Scatter:
    def __init__(self, blocks, order):
        fs, cb = lax.axis_size("fsdp"), bits_of("ctx")
        self.tail = blocks.shape[1:]
        buf = blocks.reshape((fs,) + (2,) * cb + self.tail)
        split = order == "both"
        self.parts = [(buf[: fs // 2], "xy"), (buf[fs // 2 :], "yx")] if split else [(buf, order)]

    def values(self):
        return [p[0] for p in self.parts]

    def put(self, values):
        self.parts = [(v, p[1]) for v, p in zip(values, self.parts)]

    def plane(self, stage):
        done = []
        for v, order in self.parts:
            steps = ctx_steps(order)
            done.append(ctx_scatter(v, steps[:1] if stage == 0 else steps[1:]))
        self.put(done)

    def ready_for_z(self):
        return jnp.concatenate([v.reshape((-1,) + self.tail) for v in self.values()], axis=0)

    def along_z(self):
        buf = jnp.concatenate([v.reshape((-1,) + self.tail) for v in self.values()], axis=0)
        return z_scatter(buf)


def rows_ring(blocks):
    count = lax.axis_size("fsdp")
    pairs = [(i, (i + 1) % count) for i in range(count)]
    me = lax.axis_index("fsdp")
    buf = blocks.reshape((count,) + (2,) * bits_of("ctx") + blocks.shape[1:])

    def block(back):
        return lax.dynamic_index_in_dim(buf, (me - back) % count, 0, False)

    total = block(1)
    for step in range(count - 1):
        recv = lax.ppermute(total, "fsdp", pairs)
        total = (recv.astype(F32) + block(step + 2).astype(F32)).astype(BF)
    return total


def rows_plane(buf):
    return ctx_scatter(buf[None], ctx_steps("yx")).reshape(buf.shape[-2:]).astype(F32)


def rope_tables(places, log_base):
    half_width = HD // 2
    inverse = jnp.exp(-log_base * (jnp.arange(half_width, dtype=F32) * (2.0 / HD)))
    angles = places.astype(F32)[:, None] * inverse[None, :]
    return (jnp.cos(angles), jnp.sin(angles))


def dot(a, b):
    return jnp.dot(a, b, preferred_element_type=F32)


def dot_t(a, b):
    return jnp.einsum("tc,dc->td", a, b, preferred_element_type=F32)


def t_dot(a, b):
    return jnp.einsum("ta,tb->ab", a, b, preferred_element_type=F32)


def pick(first, own, other):
    return jnp.where(first, own, other), jnp.where(first, other, own)


def key_exchange(keys_values):
    count = lax.axis_size("ctx")
    return [keys_values] + [exchange(keys_values, "ctx", j) for j in range(1, count)]


def key_return(blocks):
    count = lax.axis_size("ctx")
    blocks = jnp.split(blocks, count, axis=0)
    total = blocks[0]
    for j in range(1, count):
        total = total + exchange(blocks[j].astype(BF), "ctx", j).astype(F32)
    return total


def whole_call(body, outs, args, flops, window=None):
    vmem = pl.BlockSpec(memory_space=pltpu.VMEM)
    moved = sum(math.prod(v.shape) * v.dtype.itemsize for v in args)
    moved += sum(math.prod(s) * jnp.dtype(t).itemsize for s, t in outs)
    return pl.pallas_call(
        body,
        out_shape=[jax.ShapeDtypeStruct(s, t) for s, t in outs],
        in_specs=[pl.BlockSpec(memory_space=pltpu.SMEM)] + [vmem] * (len(args) - 1),
        out_specs=[vmem] * len(outs),
        compiler_params=pltpu.CompilerParams(vmem_limit_bytes=52 * 2**20),
        cost_estimate=pl.CostEstimate(
            flops=int(flops) // 64, bytes_accessed=int(moved) // 64, transcendentals=0
        ),
    )(*args)


def inverse_rms(u):
    return lax.rsqrt(jnp.mean(u * u, axis=-1, keepdims=True) + EPS)


def rms_back(u, gain, dz):
    r = inverse_rms(u)
    scaled = dz * gain
    mean = jnp.mean(u * scaled, axis=-1, keepdims=True)
    du = r * (scaled - u * (r * r * mean))
    return du, jnp.sum(dz * u * r, axis=0, keepdims=True)


def last_dot(a, b):
    return lax.dot_general(a, b, (((1,), (1,)), ((), ())), preferred_element_type=F32)


def first_dot(a, b):
    return lax.dot_general(a, b, (((0,), (0,)), ((), ())), preferred_element_type=F32)


def chosen(flag, own, other):
    return jnp.where(flag, own, other), jnp.where(flag, other, own)


def keys_body(flag, x, q_own, q_oth, gains, heads, cosine, sine, normed, qp, kp, q, kv):
    first = flag[0] == 0
    u = x[...]
    h = (u * inverse_rms(u) * gains[0:1, :]).astype(BF)
    normed[...] = h
    lo, hi = chosen(first, dot(h, q_own[:, :QW]), dot(h, q_oth[:, :QW]))
    cos, sin = cosine[...], sine[...]
    half = HD // 2

    def turned(v, gain, out, at):
        n = v * inverse_rms(v) * gain
        a, b = n[:, :half], n[:, half:]
        out[:, at : at + half] = (a * cos - b * sin).astype(BF)
        out[:, at + half : at + HD] = (b * cos + a * sin).astype(BF)

    for head in range(HEADS):
        part = (lo if head < 2 else hi)[:, (head % 2) * HD : (head % 2 + 1) * HD]
        qp[:, head * HD : (head + 1) * HD] = part
        turned(part, heads[0:1, :], q, head * HD)
    k_part = lo[:, QH:]
    kp[...] = k_part
    turned(k_part, heads[1:2, :], kv, 0)
    kv[:, HD:] = hi[:, QH:].astype(BF)


def forward_keys(full, x, cosine, sine_table, flag):
    q_own, q_oth, gains, heads = full
    t = x.shape[0]
    normed, qp, kp, q, kv = whole_call(
        keys_body,
        [((t, D), BF), ((t, HEADS * HD), F32), ((t, HD), F32), ((t, HEADS * HD), BF), ((t, 2 * HD), BF)],
        (flag, x, q_own, q_oth, gains, heads, cosine, sine_table),
        2 * t * D * 2 * QW,
    )
    all_kv = jnp.concatenate(key_exchange(kv), axis=0)
    return dict(x=x, normed=normed, qp=qp, kp=kp, q=q, kv=all_kv)


CHUNK = 512
GELU_A = math.sqrt(2.0 / math.pi)
GELU_B = 0.044715


def mix_body(window, flag, q, kv, pos_q, pos_k, mixed):
    reach = pos_q[...] - pos_k[...]
    allowed = (reach >= 0) & (reach < window)
    k, v = kv[:, :HD], kv[:, HD:]
    for head in range(HEADS):
        cols = slice(head * HD, (head + 1) * HD)
        s = jnp.where(allowed, last_dot(q[:, cols], k) * SCALE, -1e30)
        e = jnp.exp(s - jnp.max(s, axis=-1, keepdims=True))
        total = jnp.sum(e, axis=-1, keepdims=True)
        mixed[:, cols] = (dot(e.astype(BF), v) * (1.0 / total)).astype(BF)


def forward_attend(kept, pos, window, flag):
    t, keys = kept["x"].shape[0], kept["kv"].shape[0]
    return whole_call(
        functools.partial(mix_body, window),
        [((t, HEADS * HD), BF)],
        (flag, kept["q"], kept["kv"], pos[0][:, None], pos[1][None, :]),
        4 * t * HEADS * HD * keys,
    )[0]


def rest_body(
    flag, x, mixed, w_out, g_own, g_oth, w_down, gains,
    branch, middle, normed, gate_out, up_out, hidden, down, result,
):
    first = flag[0] == 0
    b = dot(mixed[...], w_out[...])
    branch[...] = b
    m = x[...] + b * inverse_rms(b) * gains[1:2, :]
    middle[...] = m
    h = (m * inverse_rms(m) * gains[2:3, :]).astype(BF)
    normed[...] = h
    total = jnp.zeros(m.shape, F32)
    for at in range(0, FF, CHUNK):
        cols = slice(at, at + CHUNK)
        gate, up = chosen(first, dot(h, g_own[:, cols]), dot(h, g_oth[:, cols]))
        gate_out[:, cols] = gate
        up_out[:, cols] = up
        th = jnp.tanh(GELU_A * (gate + GELU_B * gate * gate * gate))
        hid = (0.5 * gate * (1.0 + th) * up).astype(BF)
        hidden[:, cols] = hid
        total = total + dot(hid, w_down[cols, :])
    down[...] = total
    result[...] = m + total * inverse_rms(total) * gains[3:4, :]


def forward_rest(full, kept, mixed, flag):
    g_own, g_oth, w_out, w_down, gains = full
    t = kept["x"].shape[0]
    kept["mixed"] = mixed
    names = ("branch", "middle", "normed_two", "gate", "up", "hidden", "down", "result")
    outs = whole_call(
        rest_body,
        [
            ((t, D), F32), ((t, D), F32), ((t, D), BF), ((t, FF), F32),
            ((t, FF), F32), ((t, FF), BF), ((t, D), F32), ((t, D), F32),
        ],
        (flag, kept["x"], mixed, w_out, g_own, g_oth, w_down, gains),
        2 * t * HEADS * HD * D + 6 * t * D * FF,
    )
    kept.update(zip(names, outs))
    return kept["result"]


def feed_body(
    flag, dy, down, gate, up, middle, branch, gains, w_down, g_own, g_oth,
    grad_middle, grad_down, gu_own, gu_oth, grad_branch, gain_grads,
):
    first = flag[0] == 0
    dz = dy[...].astype(F32)
    df, gain_three = rms_back(down[...], gains[3:4, :], dz)
    df = df.astype(BF)
    grad_down[...] = df
    total = jnp.zeros(dz.shape, F32)
    for at in range(0, FF, CHUNK):
        cols = slice(at, at + CHUNK)
        dm = last_dot(df, w_down[cols, :])
        u = gate[:, cols]
        th = jnp.tanh(GELU_A * (u + GELU_B * u * u * u))
        plus = 0.5 * (1.0 + th)
        slope = plus + 0.5 * u * (1.0 - th * th) * (GELU_A * (1.0 + 3.0 * GELU_B * u * u))
        d_gate = (dm * up[:, cols] * slope).astype(BF)
        d_up = (dm * (u * plus)).astype(BF)
        own, oth = chosen(first, d_gate, d_up)
        gu_own[:, cols] = own
        gu_oth[:, cols] = oth
        total = total + last_dot(own, g_own[:, cols]) + last_dot(oth, g_oth[:, cols])
    part, gain_two = rms_back(middle[...], gains[2:3, :], total)
    dx = dz + part
    grad_middle[...] = dx
    da, gain_one = rms_back(branch[...], gains[1:2, :], dx)
    grad_branch[...] = da.astype(BF)
    gain_grads[...] = jnp.concatenate([gain_one, gain_two, gain_three], axis=0)


def backward_feed(full, kept, grad_result, flag):
    g_own, g_oth, w_out, w_down, gains = full
    t = kept["x"].shape[0]
    middle, down_low, gu_own, gu_oth, branch_low, gain_grads = whole_call(
        feed_body,
        [((t, D), F32), ((t, D), BF), ((t, FF), BF), ((t, FF), BF), ((t, D), BF), ((3, D), F32)],
        (
            flag, grad_result, kept["down"], kept["gate"], kept["up"], kept["middle"],
            kept["branch"], gains, w_down, g_own, g_oth,
        ),
        6 * t * D * FF,
    )
    wg_g = (t_dot(kept["normed_two"], gu_own), t_dot(kept["normed_two"], gu_oth).astype(BF))
    wg_out = t_dot(kept["mixed"], branch_low).astype(BF)
    wg_down = t_dot(kept["hidden"], down_low).astype(BF)
    return middle, branch_low, wg_g, wg_out, wg_down, gain_grads


def attend_body(window, flag, da, w_out, q, kv, pos_q, pos_k, grad_q, grad_kv):
    reach = pos_q[...] - pos_k[...]
    allowed = (reach >= 0) & (reach < window)
    k, v = kv[:, :HD], kv[:, HD:]
    for head in range(HEADS):
        cols = slice(head * HD, (head + 1) * HD)
        do = last_dot(da[...], w_out[cols, :]).astype(BF)
        s = jnp.where(allowed, last_dot(k, q[:, cols]) * SCALE, -1e30)
        e = jnp.exp(s - jnp.max(s, axis=0, keepdims=True))
        p = e * (1.0 / jnp.sum(e, axis=0, keepdims=True))
        dp = last_dot(v, do)
        inner = jnp.sum(p * dp, axis=0, keepdims=True)
        ds = (p * (dp - inner)).astype(BF)
        grad_q[:, cols] = first_dot(ds, k) * SCALE
        dk = dot(ds, q[:, cols]) * SCALE
        dv = dot(p.astype(BF), do)
        if head == 0:
            total_k, total_v = dk, dv
        else:
            total_k, total_v = total_k + dk, total_v + dv
    grad_kv[:, :HD] = total_k.astype(BF)
    grad_kv[:, HD:] = total_v.astype(BF)


def backward_attend(w_out, kept, branch_low, pos, window, flag):
    t, keys = kept["x"].shape[0], kept["kv"].shape[0]
    return whole_call(
        functools.partial(attend_body, window),
        [((t, HEADS * HD), F32), ((keys, 2 * HD), BF)],
        (flag, branch_low, w_out, kept["q"], kept["kv"], pos[0][None, :], pos[1][:, None]),
        2 * t * HEADS * HD * (5 * keys + D),
    )


def back_body(
    flag, grad_q, grad_kv, qp, kp, heads, cosine, sine, x, dx, q_own, q_oth, gains,
    grad_x, gq_own, gq_oth, gain_zero, head_grads,
):
    first = flag[0] == 0
    cos, sin = cosine[...], sine[...]
    half = HD // 2

    def turned_back(d, u, gain):
        a, b = d[:, :half], d[:, half:]
        n = jnp.concatenate([a * cos + b * sin, b * cos - a * sin], axis=1)
        return rms_back(u, gain, n)

    parts = []
    query_gain = jnp.zeros((1, HD), F32)
    for head in range(HEADS):
        cols = slice(head * HD, (head + 1) * HD)
        du, dg = turned_back(grad_q[:, cols], qp[:, cols], heads[0:1, :])
        parts.append(du.astype(BF))
        query_gain = query_gain + dg
    dk, key_gain = turned_back(grad_kv[:, :HD], kp[...], heads[1:2, :])
    lo = jnp.concatenate(parts[:2] + [dk.astype(BF)], axis=1)
    hi = jnp.concatenate(parts[2:] + [grad_kv[:, HD:].astype(BF)], axis=1)
    own, oth = chosen(first, lo, hi)
    gq_own[...] = own
    gq_oth[...] = oth
    dz = last_dot(own, q_own[:, :QW]) + last_dot(oth, q_oth[:, :QW])
    part, gain = rms_back(x[...], gains[0:1, :], dz)
    grad_x[...] = dx[...] + part
    gain_zero[...] = gain
    head_grads[...] = jnp.concatenate([query_gain, key_gain], axis=0)


def backward_keys(full, kept, middle, grad_q, grad_kv, cosine, sine_table, flag):
    q_own, q_oth, gains, heads = full
    t = kept["x"].shape[0]
    grad_x, gq_own, gq_oth, gain_zero, head_grads = whole_call(
        back_body,
        [((t, D), F32), ((t, QW), BF), ((t, QW), BF), ((1, D), F32), ((2, HD), F32)],
        (
            flag, grad_q, grad_kv, kept["qp"], kept["kp"], heads, cosine, sine_table, kept["x"],
            middle, q_own, q_oth, gains,
        ),
        4 * t * D * QW,
    )
    wg_q = (t_dot(kept["normed"], gq_own).astype(BF), t_dot(kept["normed"], gq_oth).astype(BF))
    return grad_x, wg_q, gain_zero, head_grads


def halves(grad, count):
    return grad.reshape(count, 2, -1, grad.shape[-1])


def local(
    boundary, positions, w_query, w_key_value, w_out, w_gate_up, w_down, norm_gains, head_gains
):
    section = lax.axis_index("section")
    first = section == 0
    ctx_index = lax.axis_index("ctx")
    tokens = boundary.shape[3]
    seq_length = positions.shape[-1]
    nr = w_query.shape[1]
    hr = head_gains.shape[2]
    ro, rd = w_out.shape[1], w_down.shape[1]
    blocks = lax.axis_size("fsdp") * lax.axis_size("ctx")

    moved = exchange(lax.dynamic_index_in_dim(boundary[0, :, 0], 1 - section, 0, False), "section", 1)
    kept_in = lax.dynamic_index_in_dim(boundary[0, :, 0], section, 0, False)
    x0, cotangent = pick(first, kept_in, moved)
    x0 = x0.astype(F32)
    seq_places = lax.dynamic_index_in_dim(positions[:, 0], section, 0, False)
    near = [
        lax.dynamic_slice_in_dim(seq_places, (ctx_index ^ j) * tokens, tokens)
        for j in range(lax.axis_size("ctx"))
    ]
    pos = (near[0], jnp.concatenate(near))
    flag = section.astype(jnp.int32).reshape(1)

    gain_cols = jnp.concatenate(
        [
            norm_gains[0].T,
            jnp.pad(head_gains[0].T, ((0, nr - hr), (0, 0))),
            jnp.zeros((nr, 128 - 6), BF),
        ],
        axis=1,
    )
    cols = [
        jnp.concatenate(
            [
                w_query[0, :, h * QH : (h + 1) * QH],
                w_key_value[0, :, h * HD : (h + 1) * HD],
                gain_cols,
                w_gate_up[0, :, h * FF : (h + 1) * FF],
            ],
            axis=1,
        )
        for h in range(2)
    ]
    rows = [
        jnp.concatenate(
            [
                w_out[0, h * ro // 2 : (h + 1) * ro // 2],
                w_down[0, h * rd // 2 : (h + 1) * rd // 2],
            ],
            axis=0,
        )
        for h in range(2)
    ]
    col_keep, col_send = pick(first, cols[0], cols[1])
    row_keep, row_send = pick(first, rows[0], rows[1])
    col_recv = exchange(col_send, "section", 1)
    row_recv = exchange(row_send, "section", 1)
    layer_cols = pick(first, col_keep, col_recv)
    layer_rows = pick(first, row_keep, row_recv)

    def query_side(pair):
        q_own, q_oth = [v.reshape(blocks * nr, -1) for v in pair]
        gain_part = q_own[:, QW:].astype(F32)
        gains = gain_part[:, :4].T
        heads = gain_part[:, 4:6].reshape(blocks, nr, 2)[:, :hr].reshape(blocks * hr, 2).T
        return q_own, q_oth, gains, heads

    def feed_side(g_pair, b_pair, gains):
        g_own, g_oth = [v.reshape(blocks * nr, -1) for v in g_pair]
        b_lo, b_hi = pick(first, *b_pair)
        full_out = jnp.concatenate([b_lo[:, : ro // 2], b_hi[:, : ro // 2]], axis=1)
        full_down = jnp.concatenate([b_lo[:, ro // 2 :], b_hi[:, ro // 2 :]], axis=1)
        return g_own, g_oth, full_out.reshape(-1, D), full_down.reshape(-1, D), gains

    def reduce_cols(own, other):
        summed = own.astype(F32) + exchange(other, "section", 1).astype(F32)
        return summed.astype(BF).reshape(blocks, nr, -1)

    def reduce_rows(wg_out, wg_down):
        out_half, down_half = halves(wg_out, blocks), halves(wg_down, blocks)

        def part(index):
            return jnp.concatenate(
                [
                    lax.dynamic_index_in_dim(out_half, index, 1, False),
                    lax.dynamic_index_in_dim(down_half, index, 1, False),
                ],
                axis=1,
            )

        recv = exchange(part(1 - section), "section", 1)
        return (part(section).astype(F32) + recv.astype(F32)).astype(BF)

    def reduce_query(wg_q, norm_grads, head_grads):
        norm_part = jnp.concatenate(norm_grads, axis=0).T
        head_part = head_grads.T.reshape(blocks, hr, 2)
        head_part = jnp.pad(head_part, ((0, 0), (0, nr - hr), (0, 0))).reshape(blocks * nr, 2)
        fill = jnp.zeros((blocks * nr, 128 - 6), F32)
        cols = jnp.concatenate([norm_part, head_part, fill], axis=1).astype(BF)
        own = jnp.concatenate([wg_q[0], cols], axis=1)
        oth = jnp.concatenate([wg_q[1], cols], axis=1)
        return reduce_cols(own, oth)

    tables = [rope_tables(pos[0], base) for base in BASES]
    windows = (WIN, seq_length)

    gather0 = Gather(layer_cols[0], layer_rows[0])
    gather0.begin()
    gather0.rows_z()
    gather0.plane(0)
    gather0.plane(1)
    pairs0 = gather0.pairs()
    query0 = query_side(pairs0[0])
    kept0 = forward_keys(query0, x0, *tables[0], flag)
    whole1 = jnp.concatenate([layer_cols[1], pack_rows(layer_rows[1], nr)], axis=1)
    whole1 = lax.all_gather(whole1, GRID, axis=0)
    swapped = [v for pair in pairs0[1:] for v in pair]
    kept0["kv"], *held = tie(kept0["kv"], *swapped)
    feed0 = feed_side(held[:2], held[2:], query0[2])
    mixed = forward_attend(kept0, pos, windows[0], flag)
    y0 = forward_rest(feed0, kept0, mixed, flag).astype(BF)
    whole1, y0 = tie(whole1, y0)
    query_part = whole1[..., :QP]
    query_pair = tie(query_part, exchange(query_part, "section", 1), whole1)
    whole1 = query_pair[2]
    pairs1 = [whole1[..., QP : QP + FF], whole1[..., QP + FF :]]
    pairs1 = [query_pair[:2]] + [(v, exchange(v, "section", 1)) for v in pairs1]
    pairs1[2] = [unpack_rows(v, (ro + rd) // 2) for v in pairs1[2]]
    query1 = query_side(pairs1[0])
    kept1 = forward_keys(query1, y0.astype(F32), *tables[1], flag)
    feed1 = feed_side(*pairs1[1:], query1[2])
    mixed = forward_attend(kept1, pos, windows[1], flag)
    y1 = forward_rest(feed1, kept1, mixed, flag)

    middle1, branch1, wg_g, wg_out, wg_down, norm_grads = backward_feed(
        feed1, kept1, cotangent, flag
    )
    sum_g1 = reduce_cols(*wg_g)
    sum_b1 = reduce_rows(wg_out, wg_down)
    grad_q1, kv_blocks = backward_attend(feed1[2], kept1, branch1, pos, windows[1], flag)
    grad_q1, kv_blocks, sum_g1, sum_b1 = tie(grad_q1, kv_blocks, sum_g1, sum_b1)
    grad_kv = key_return(kv_blocks)
    grad_kv, sum_g1, sum_b1 = tie(grad_kv, sum_g1, sum_b1)
    scat_g1, scat_b1 = Scatter(sum_g1, "both"), Scatter(sum_b1, "yx")
    scat_g1.plane(0)
    scat_b1.plane(0)
    grad1, wg_q, gain_zero, head_grads = backward_keys(
        query1, kept1, middle1, grad_q1, grad_kv, *tables[1], flag
    )
    grad1 = grad1.astype(BF)
    sum_q1 = reduce_query(wg_q, [gain_zero, norm_grads], head_grads)

    middle0, branch0, wg_g, wg_out, wg_down, norm_grads = backward_feed(
        feed0, kept0, grad1, flag
    )
    branch0, sum_q1, held0, *held = tie(branch0, sum_q1, *scat_b1.values(), *scat_g1.values())
    scat_g1.put(held)
    scat_b1.put([held0])
    scat_q1 = Scatter(sum_q1, "xy")
    scat_g1.plane(1)
    red_g1 = scat_g1.along_z()
    scat_b1.plane(1)
    scat_q1.plane(0)
    sum_g0 = reduce_cols(*wg_g)
    sum_b0 = reduce_rows(wg_out, wg_down)
    grad_q0, kv_blocks = backward_attend(feed0[2], kept0, branch0, pos, windows[0], flag)
    grad_q0, kv_blocks, sum_g0, sum_b0, red_g1, held0 = tie(
        grad_q0, kv_blocks, sum_g0, sum_b0, red_g1, *scat_b1.values()
    )
    scat_b1.put([held0])
    grad_kv = key_return(kv_blocks)
    rows0 = rows_ring(sum_b0)
    grad_kv, sum_g0, held0 = tie(grad_kv, sum_g0, *scat_q1.values())
    scat_g0 = Scatter(sum_g0, "both")
    scat_g0.plane(0)
    grad0, wg_q, gain_zero, head_grads = backward_keys(
        query0, kept0, middle0, grad_q0, grad_kv, *tables[0], flag
    )
    sum_q0 = reduce_query(wg_q, [gain_zero, norm_grads], head_grads)
    sum_q0, held0, *held = tie(sum_q0, held0, *scat_g0.values())
    scat_g0.put(held)
    scat_q1.put([held0])
    scat_q0 = Scatter(sum_q0, "xy")
    scat_q0.plane(0)
    scat_g0.plane(1)
    scat_q1.plane(1)
    scat_q0.plane(1)
    rows1 = pack_rows(scat_b1.ready_for_z(), nr)
    red_c1 = z_scatter(jnp.concatenate([scat_q1.ready_for_z(), rows1], axis=-1))
    red_q1, red_b1 = red_c1[:, :QP], unpack_rows(red_c1[:, QP:], (ro + rd) // 2)
    red_q0, red_g0 = scat_q0.along_z(), scat_g0.along_z()
    red_b0 = rows_plane(rows0)
    red_c0 = jnp.concatenate([red_q0, red_g0], axis=1)
    red_c1 = jnp.concatenate([red_q1, red_g1], axis=1)

    out_moved = exchange(jnp.where(first, y1, grad0), "section", 1)
    c_keep, c_send = pick(first, red_c0, red_c1)
    b_keep, b_send = pick(first, red_b0, red_b1)
    c_lo, c_hi = pick(first, c_keep, exchange(c_send, "section", 1))
    b_lo, b_hi = pick(first, b_keep, exchange(b_send, "section", 1))
    boundary_out = jnp.where(
        first, jnp.stack([grad0, out_moved]), jnp.stack([out_moved, y1])
    )[None, :, None]
    return (
        boundary_out,
        jnp.concatenate([c_lo[:, :QH], c_hi[:, :QH]], axis=1)[None],
        jnp.concatenate([c_lo[:, QH:QW], c_hi[:, QH:QW]], axis=1)[None],
        jnp.concatenate([b_lo[: ro // 2], b_hi[: ro // 2]], axis=0)[None],
        jnp.concatenate([c_lo[:, QP:], c_hi[:, QP:]], axis=1)[None],
        jnp.concatenate([b_lo[ro // 2 :], b_hi[ro // 2 :]], axis=0)[None],
        c_lo[:, QW : QW + 4].T[None],
        c_lo[:hr, QW + 4 : QW + 6].T[None],
    )


def solution(mesh):
    in_specs = (
        P("section", None, "fsdp", "ctx", None),
        P(None, "fsdp", None),
        P("section", ("fsdp", "ctx"), None),
        P("section", ("fsdp", "ctx"), None),
        P("section", ("fsdp", "ctx"), None),
        P("section", ("fsdp", "ctx"), None),
        P("section", ("fsdp", "ctx"), None),
        P("section", None, ("fsdp", "ctx")),
        P("section", None, ("fsdp", "ctx")),
    )
    out_specs = (
        P("section", None, "fsdp", "ctx", None),
        P("section", ("fsdp", "ctx"), None),
        P("section", ("fsdp", "ctx"), None),
        P("section", ("fsdp", "ctx"), None),
        P("section", ("fsdp", "ctx"), None),
        P("section", ("fsdp", "ctx"), None),
        P("section", None, ("fsdp", "ctx")),
        P("section", None, ("fsdp", "ctx")),
    )
    return jax.shard_map(local, mesh=mesh, in_specs=in_specs, out_specs=out_specs, check_vma=False)
```
